32 devices in a mesh: gx: 2 (over y), gy: 4 (over x, core), gz: 4 (over z).
Axes of the slice: x: 2, y: 2, z: 4, core: 2. Of those that a mesh axis runs over, the one named last changes fastest.
Arguments:
- right_side: float32 [2, 4, 4, 64, 512], P('gx', 'gy', 'gz'), may hold values from -6 to 6
- diag_blocks: float32 [4, 64, 64], replicated, may hold values from -0.27 to 17.9, as said below
- face_blocks: float32 [6, 4, 64, 64], replicated, may hold values from -2.42 to 0.22
- prolong: float32 [8, 64, 64], replicated, may hold values from -0.75 to 0.75
- mats_fine: int32 [2, 4, 4, 512], P('gx', 'gy', 'gz'), may hold values from 0 to 3
- mats_mid: int32 [2, 4, 4, 64], P('gx', 'gy', 'gz'), may hold values from 0 to 3
- mats_coarse: int32 [2, 4, 4, 8], P('gx', 'gy', 'gz'), may hold values from 0 to 3
Outputs:
- solution: float32 [2, 4, 4, 64, 512], P('gx', 'gy', 'gz')
The draws below stay inside these ranges and needn't reach their ends.
Inputs may be any that keep to these rules, and one draw needn't show every extreme that they name: `diag_blocks`: each block is symmetric positive definite.
All inputs are finite; a program needn't handle non-finite values.
Results may differ from the reference program's by a relative error of at most 0.0003.
Values sent between devices are 32-bit elements; how exact they have to be, the bound alone decides.
No kernel may reach another device: no remote copies, remote signals or barrier semaphores. Data moves between devices by JAX's collectives and lax.ppermute only.
A program may use at most 64 MiB of HBM per device.

```python
import jax
import jax.numpy as jnp
from jax import lax

MODES = 64
MATERIALS = 4
SWEEPS = 2
COARSE_SWEEPS = 4
CYCLES = 2
CX = 8
CY = 8
CZ = 8
N_GX = 2
N_GY = 4
N_GZ = 4


def material_scales(key):
    scale_key = jax.random.fold_in(key, 7)
    first_key, second_key = jax.random.split(scale_key)
    steps = jnp.arange(MATERIALS, dtype=jnp.float32) * (2.0 / (MATERIALS - 1))
    base = jnp.exp2(steps) * jax.random.uniform(first_key, (MATERIALS,), jnp.float32, 0.9, 1.1)
    return jax.random.permutation(second_key, base)


def draw_diag_blocks(key, part):
    scales = material_scales(key)
    noise = jnp.clip(0.03 * jax.random.normal(key, (MATERIALS, MODES, MODES), jnp.float32), -0.06, 0.06)
    symmetric = 0.5 * (noise + jnp.transpose(noise, (0, 2, 1)))
    blocks = 4.0 * jnp.eye(MODES, dtype=jnp.float32)[None] + symmetric
    return blocks * scales[:, None, None]


def draw_face_blocks(key, part):
    scales = material_scales(key)
    face_key = jax.random.fold_in(key, 11)
    noise = jnp.clip(0.025 * jax.random.normal(face_key, (6, MATERIALS, MODES, MODES), jnp.float32), -0.05, 0.05)
    blocks = -0.5 * jnp.eye(MODES, dtype=jnp.float32)[None, None] + noise
    return blocks * scales[None, :, None, None]


def with_ends(drawn, rng, least, top_value):
    place = [jax.random.randint(jax.random.fold_in(rng, axis), (), 0, length) for axis, length in enumerate(drawn.shape)]
    longest = drawn.shape.index(max(drawn.shape))
    next_to = place[:longest] + [(place[longest] + 1) % drawn.shape[longest]] + place[longest + 1:]
    return drawn.at[tuple(place)].set(least).at[tuple(next_to)].set(top_value)


def shard_levels(rng, dims, cuts, low, high):
    loudness, own = 1.0, jax.random.fold_in(rng, 6)
    for dim, shards_of in cuts:
        heights = jnp.exp(jax.random.uniform(jax.random.fold_in(own, dim), (shards_of,), jnp.float32, low / len(cuts), high / len(cuts)))
        loudness = loudness * jnp.repeat(heights, dims[dim] // shards_of).reshape([-1 if axis == dim else 1 for axis in range(len(dims))])
    return loudness


def bell_draw(key, dims, scale, limit, shards=(), kind=jnp.bfloat16):
    values = jax.random.normal(key, dims, jnp.float32) * scale
    if len(shards) > 0:
        values = shard_levels(key, dims, shards, -0.22, 0.18) * values
    return jnp.clip(values, min=-limit, max=limit).astype(kind)


def setup_inputs(seed: int = 0) -> dict:
    seeds = jax.random.split(jax.random.key(seed), 8)
    return {
        "right_side": bell_draw(seeds[0], (N_GX, N_GY, N_GZ, MODES, CX * CY * CZ), 1.0, 6.0, ((0, 2), (1, 4), (2, 4)), jnp.float32),
        "diag_blocks": draw_diag_blocks(jax.random.fold_in(seeds[7], 71), 0),
        "face_blocks": draw_face_blocks(jax.random.fold_in(seeds[7], 71), 0),
        "prolong": bell_draw(seeds[3], (8, MODES, MODES), MODES ** -0.5, 0.75, (), jnp.float32),
        "mats_fine": with_ends(jax.random.randint(seeds[4], (N_GX, N_GY, N_GZ, CX * CY * CZ), 0, MATERIALS), jax.random.fold_in(seeds[4], 1), 0, MATERIALS - 1).astype(jnp.int32),
        "mats_mid": with_ends(jax.random.randint(seeds[5], (N_GX, N_GY, N_GZ, (CX // 2) * (CY // 2) * (CZ // 2)), 0, MATERIALS), jax.random.fold_in(seeds[5], 1), 0, MATERIALS - 1).astype(jnp.int32),
        "mats_coarse": with_ends(jax.random.randint(seeds[6], (N_GX, N_GY, N_GZ, (CX // 4) * (CY // 4) * (CZ // 4)), 0, MATERIALS), jax.random.fold_in(seeds[6], 1), 0, MATERIALS - 1).astype(jnp.int32),
    }


relax_weight = 0.7
restrict_scale = 0.6
highest = lax.Precision.HIGHEST

def inverse_blocks(diag_blocks):
    identity = jnp.eye(MODES, dtype=diag_blocks.dtype)
    result = []
    for material in range(MATERIALS):
        factor = jnp.linalg.cholesky(diag_blocks[material])
        result.append(jax.scipy.linalg.cho_solve((factor, True), identity))
    return jnp.stack(result).reshape(MATERIALS * MODES, MODES)

def coupling_matrix(diag_blocks, face_blocks):
    blocks = jnp.concatenate([diag_blocks[None], face_blocks], axis=0)
    return jnp.transpose(blocks, (1, 2, 0, 3)).reshape(MATERIALS * MODES, 7 * MODES)

def choose_blocks(weights, columns, onehot):
    product = jnp.dot(weights.astype(jnp.float32), columns.astype(jnp.float32), precision=highest, preferred_element_type=jnp.float32)
    product = product.reshape(MATERIALS, MODES, columns.shape[1])
    return jnp.sum(product * onehot.reshape(MATERIALS, 1, columns.shape[1]), axis=0)

def operate(padded, onehot, coupling):
    centre = padded[:, 1:-1, 1:-1, 1:-1]
    stacked = jnp.concatenate([centre, padded[:, 2:, 1:-1, 1:-1], padded[:, :-2, 1:-1, 1:-1], padded[:, 1:-1, 2:, 1:-1], padded[:, 1:-1, :-2, 1:-1], padded[:, 1:-1, 1:-1, 2:], padded[:, 1:-1, 1:-1, :-2]], axis=0)
    columns = stacked.reshape(7 * MODES, -1)
    return choose_blocks(coupling, columns, onehot.reshape(MATERIALS, -1)).reshape(centre.shape)

def apply_inverse(inverse, field, onehot):
    return choose_blocks(inverse, field.reshape(MODES, -1), onehot.reshape(MATERIALS, -1)).reshape(field.shape)

def zero_border(field):
    return jnp.pad(field, ((0, 0), (1, 1), (1, 1), (1, 1)))

def relax(iterate, source, onehot, inverse, coupling):
    residual = source - operate(zero_border(iterate), onehot, coupling)
    return iterate + relax_weight * apply_inverse(inverse, residual, onehot)

def restrict(field, prolong):
    blocked = field.reshape(MODES, field.shape[1] // 2, 2, field.shape[2] // 2, 2, field.shape[3] // 2, 2)
    return restrict_scale * jnp.einsum('abcji,jxaybzc->ixyz', prolong.reshape(2, 2, 2, MODES, MODES), blocked, precision=highest)

def expand(coarse_field, prolong):
    finer = jnp.einsum('abcji,ixyz->jxaybzc', prolong.reshape(2, 2, 2, MODES, MODES), coarse_field, precision=highest)
    return finer.reshape(MODES, 2 * coarse_field.shape[1], 2 * coarse_field.shape[2], 2 * coarse_field.shape[3])

def to_grid(field, size_x, size_y, size_z):
    blocked = field.reshape(N_GX, N_GY, N_GZ, MODES, size_x, size_y, size_z)
    return jnp.transpose(blocked, (3, 0, 4, 1, 5, 2, 6)).reshape(MODES, N_GX * size_x, N_GY * size_y, N_GZ * size_z)

def onehot_grid(materials, size_x, size_y, size_z):
    blocked = materials.reshape(N_GX, N_GY, N_GZ, size_x, size_y, size_z)
    grid = jnp.transpose(blocked, (0, 3, 1, 4, 2, 5)).reshape(N_GX * size_x, N_GY * size_y, N_GZ * size_z)
    return (grid[None] == jnp.arange(MATERIALS, dtype=jnp.int32)[:, None, None, None]).astype(jnp.float32)

def reference(right_side, diag_blocks, face_blocks, prolong, mats_fine, mats_mid, mats_coarse):
    inverse = inverse_blocks(diag_blocks)
    coupling = coupling_matrix(diag_blocks, face_blocks)
    source = to_grid(right_side, CX, CY, CZ)
    onehot_fine = onehot_grid(mats_fine, CX, CY, CZ)
    onehot_mid = onehot_grid(mats_mid, CX // 2, CY // 2, CZ // 2)
    onehot_coarse = onehot_grid(mats_coarse, CX // 4, CY // 4, CZ // 4)

    def coarse_solve(coarse_source):
        iterate = relax_weight * apply_inverse(inverse, coarse_source, onehot_coarse)
        for repeat in range(COARSE_SWEEPS - 1):
            iterate = relax(iterate, coarse_source, onehot_coarse, inverse, coupling)
        return iterate

    def middle(mid_source):
        iterate = relax_weight * apply_inverse(inverse, mid_source, onehot_mid)
        for repeat in range(SWEEPS - 1):
            iterate = relax(iterate, mid_source, onehot_mid, inverse, coupling)
        residual = mid_source - operate(zero_border(iterate), onehot_mid, coupling)
        iterate = iterate + expand(coarse_solve(restrict(residual, prolong)), prolong)
        for repeat in range(SWEEPS):
            iterate = relax(iterate, mid_source, onehot_mid, inverse, coupling)
        return iterate
    iterate = relax_weight * apply_inverse(inverse, source, onehot_fine)
    for repeat in range(SWEEPS - 1):
        iterate = relax(iterate, source, onehot_fine, inverse, coupling)
    for cycle_index in range(CYCLES):
        if cycle_index > 0:
            for repeat in range(SWEEPS):
                iterate = relax(iterate, source, onehot_fine, inverse, coupling)
        residual = source - operate(zero_border(iterate), onehot_fine, coupling)
        iterate = iterate + expand(middle(restrict(residual, prolong)), prolong)
        for repeat in range(SWEEPS):
            iterate = relax(iterate, source, onehot_fine, inverse, coupling)
    blocked = iterate.reshape(MODES, N_GX, CX, N_GY, CY, N_GZ, CZ)
    return jnp.transpose(blocked, (1, 3, 5, 0, 2, 4, 6)).reshape(N_GX, N_GY, N_GZ, MODES, CX * CY * CZ)
```

```python
from functools import partial

import jax
import jax.numpy as jnp
from jax import lax
from jax.experimental import pallas as pl
from jax.experimental.pallas import tpu as pltpu
from jax.sharding import PartitionSpec as P

MODES = 64
MATERIALS = 4
SWEEPS = 2
COARSE_SWEEPS = 4
CYCLES = 2
CX = 8
CY = 8
CZ = 8


relax_weight = 0.7
restrict_scale = 0.6
highest = lax.Precision.HIGHEST


def padded_2(shard, sides, width):
    for axis, dim in sides:
        size, length = (lax.axis_size(axis), shard.shape[dim])
        up = [(i, (i + 1) % size) for i in range(size - 1)]
        down = [(j, i) for i, j in up]
        last = lax.slice_in_dim(shard, length - width, length, axis=dim)
        first = lax.slice_in_dim(shard, 0, width, axis=dim)
        before = lax.ppermute(last, axis, up)
        after = lax.ppermute(first, axis, down)
        shard = jnp.concatenate([before, shard, after], axis=dim)
    return shard


def inverse_blocks(diag_blocks):
    identity = jnp.eye(MODES, dtype=diag_blocks.dtype)
    result = []
    for material in range(MATERIALS):
        factor = jnp.linalg.cholesky(diag_blocks[material])
        result.append(jax.scipy.linalg.cho_solve((factor, True), identity))
    return jnp.stack(result).reshape(MATERIALS * MODES, MODES)


def coupling_matrix(diag_blocks, face_blocks):
    blocks = jnp.concatenate([diag_blocks[None], face_blocks], axis=0)
    return jnp.transpose(blocks, (1, 2, 0, 3)).reshape(MATERIALS * MODES, 7 * MODES)


def choose_blocks(weights, columns, onehot):
    product = jnp.dot(weights, columns, precision=highest, preferred_element_type=jnp.float32)
    product = product.reshape(MATERIALS, MODES, columns.shape[1])
    return jnp.sum(product * onehot.reshape(MATERIALS, 1, columns.shape[1]), axis=0)


def operate(padded, onehot, coupling):
    centre = padded[:, 1:-1, 1:-1, 1:-1]
    stacked = jnp.concatenate(
        [
            centre,
            padded[:, 2:, 1:-1, 1:-1],
            padded[:, :-2, 1:-1, 1:-1],
            padded[:, 1:-1, 2:, 1:-1],
            padded[:, 1:-1, :-2, 1:-1],
            padded[:, 1:-1, 1:-1, 2:],
            padded[:, 1:-1, 1:-1, :-2],
        ],
        axis=0,
    )
    columns = stacked.reshape(7 * MODES, -1)
    return choose_blocks(coupling, columns, onehot.reshape(MATERIALS, -1)).reshape(centre.shape)


def apply_inverse(inverse, field, onehot):
    return choose_blocks(inverse, field.reshape(MODES, -1), onehot.reshape(MATERIALS, -1)).reshape(
        field.shape
    )


def restrict(field, prolong):
    blocked = field.reshape(
        MODES, field.shape[1] // 2, 2, field.shape[2] // 2, 2, field.shape[3] // 2, 2
    )
    return restrict_scale * jnp.einsum(
        "abcji,jxaybzc->ixyz", prolong.reshape(2, 2, 2, MODES, MODES), blocked, precision=highest
    )


def expand(coarse_field, prolong):
    finer = jnp.einsum(
        "abcji,ixyz->jxaybzc",
        prolong.reshape(2, 2, 2, MODES, MODES),
        coarse_field,
        precision=highest,
    )
    return finer.reshape(
        MODES, 2 * coarse_field.shape[1], 2 * coarse_field.shape[2], 2 * coarse_field.shape[3]
    )


def make_onehot(materials):
    return (materials[None] == jnp.arange(MATERIALS, dtype=jnp.int32)[:, None, None, None]).astype(
        jnp.float32
    )


def fine_border(field):
    return padded_2(field, (("gx", 1), ("gy", 2), ("gz", 3)), 1)


def section_border(field):
    padded = padded_2(field, (("gx", 1), ("gy", 2)), 1)
    return jnp.pad(padded, ((0, 0), (0, 0), (0, 0), (1, 1)))


def smooth(iterate, source, onehot, border, inverse, coupling):
    residual = source - operate(border(iterate), onehot, coupling)
    return iterate + relax_weight * apply_inverse(inverse, residual, onehot)


def coarse_solve(source, onehot, border, inverse, coupling):
    iterate = relax_weight * apply_inverse(inverse, source, onehot)
    for repeat in range(COARSE_SWEEPS - 1):
        iterate = smooth(iterate, source, onehot, border, inverse, coupling)
    return iterate


def middle_cycle(source, onehot, border, inverse, coupling, prolong, coarse_solver):
    iterate = relax_weight * apply_inverse(inverse, source, onehot)
    iterate = smooth(iterate, source, onehot, border, inverse, coupling)
    residual = source - operate(border(iterate), onehot, coupling)
    iterate = iterate + expand(coarse_solver(restrict(residual, prolong)), prolong)
    for repeat in range(SWEEPS):
        iterate = smooth(iterate, source, onehot, border, inverse, coupling)
    return iterate


def single_steps(iterate, actions, source, onehot, inverse, coupling):
    residual = None
    for action in actions:
        if action == "sweep":
            iterate = smooth(iterate, source, onehot, fine_border, inverse, coupling)
        else:
            residual = source - operate(fine_border(iterate), onehot, coupling)
    return (iterate, residual)


def per_device(right_side, diag_blocks, face_blocks, prolong, mats_fine, mats_mid, mats_coarse):
    inverse = inverse_blocks(diag_blocks)
    coupling = coupling_matrix(diag_blocks, face_blocks)
    source = right_side[0, 0, 0].reshape(MODES, CX, CY, CZ)
    onehot_fine = make_onehot(mats_fine[0, 0, 0].reshape(CX, CY, CZ))
    onehot_mid = make_onehot(mats_mid[0, 0, 0].reshape(CX // 2, CY // 2, CZ // 2))
    onehot_coarse = make_onehot(mats_coarse[0, 0, 0].reshape(CX // 4, CY // 4, CZ // 4))
    stepper = partial(
        single_steps, source=source, onehot=onehot_fine, inverse=inverse, coupling=coupling
    )
    iterate = relax_weight * apply_inverse(inverse, source, onehot_fine)
    for cycle_index in range(CYCLES):
        if cycle_index == 0:
            actions = ["sweep"] * (SWEEPS - 1) + ["residual"]
        else:
            actions = ["sweep"] * SWEEPS + ["residual"]
        iterate, residual = stepper(iterate, actions)
        gathered_source = lax.all_gather(restrict(residual, prolong), "gz", axis=3, tiled=True)
        gathered_mid = lax.all_gather(onehot_mid, "gz", axis=3, tiled=True)
        gathered_coarse = lax.all_gather(onehot_coarse, "gz", axis=3, tiled=True)
        local_solver = partial(
            coarse_solve,
            onehot=gathered_coarse,
            border=section_border,
            inverse=inverse,
            coupling=coupling,
        )
        section_field = middle_cycle(
            gathered_source, gathered_mid, section_border, inverse, coupling, prolong, local_solver
        )
        iterate = iterate + expand(
            lax.dynamic_slice_in_dim(section_field, lax.axis_index("gz") * (CZ // 2), CZ // 2, 3),
            prolong,
        )
        iterate, unused_residual = stepper(iterate, ["sweep"] * SWEEPS)
    return iterate.reshape(MODES, CX * CY * CZ)[None, None, None]


HALO = 3 * SWEEPS + SWEEPS - 1
PITCH = CY + 2 * HALO
BLOCK = CX * CY * CZ
TILE = 128
LANES = -(-(PITCH * PITCH) // TILE) * TILE
ROWS = MODES + 8
MX, MY, MZ = CX // 2, CY // 2, CZ // 2
VMEM_LIMIT = 48 * 1024 * 1024
f32 = jnp.float32
bf16 = jnp.bfloat16


def split(value):
    high = value.astype(bf16)
    return high, (value - high.astype(f32)).astype(bf16)


def dot(a, b):
    return jnp.dot(a, b, preferred_element_type=f32)


def iota(shape, dim):
    return lax.broadcasted_iota(jnp.int32, shape, dim)


def where_equal(rows, columns):
    return jnp.where(rows == columns, 1.0, 0.0).astype(bf16)


def place(value, selector):
    high, low = split(value)
    return dot(high, selector) + dot(low, selector)


def pick(product, code, first):
    out = jnp.zeros((MODES, product.shape[1]), f32)
    for m in range(MATERIALS):
        out = jnp.where(code == m + first, product[m * MODES:(m + 1) * MODES], out)
    return out


def stack3(value):
    high, low = split(value)
    return jnp.concatenate([high, low, high], axis=0)


def halves(value):
    high, low = split(value)
    return jnp.concatenate([high, low], axis=0)


def thirds(value):
    high, low = split(value)
    return jnp.concatenate([high, high, low], axis=1)


def setup_kernel(diag, face, prolong, w1g, w2g, w1a, w2a, wi, wr, wp):
    a = diag[...]
    row_id = iota((1, MODES, 1), 1)
    lane_id = iota((1, 1, MODES), 2)
    for k in range(MODES):
        pivot = 1.0 / a[:, k:k + 1, k:k + 1]
        on_row, on_lane = row_id == k, lane_id == k
        row = jnp.where(on_lane, pivot, a[:, k:k + 1, :] * pivot)
        column = a[:, :, k:k + 1]
        a = jnp.where(on_row, row, jnp.where(on_lane, 0.0, a) - column * row)
    scaled = relax_weight * a
    near, far, near_g, far_g, inv = [], [], [], [], []
    zero = jnp.zeros((MODES, MODES), f32)
    for m in range(MATERIALS):
        beside = jnp.concatenate([face[1, m], face[0, m]], axis=1)
        across = jnp.concatenate([face[d, m] for d in (2, 3, 4, 5)], axis=1)
        near.append(jnp.concatenate([face[1, m], diag[m], face[0, m]], axis=1))
        far.append(across)
        g = jnp.dot(
            scaled[m], jnp.concatenate([beside, across], axis=1),
            precision=highest, preferred_element_type=f32,
        )
        near_g.append(jnp.concatenate([g[:, :MODES], zero, g[:, MODES:2 * MODES]], axis=1))
        far_g.append(g[:, 2 * MODES:])
        inv.append(scaled[m])
    w1a[...] = halves(jnp.concatenate(near, axis=0))
    w2a[...] = halves(jnp.concatenate(far, axis=0))
    w1g[...] = halves(jnp.concatenate(near_g, axis=0))
    w2g[...] = halves(jnp.concatenate(far_g, axis=0))
    wi[...] = thirds(jnp.concatenate(inv, axis=0))
    for p in range(2):
        wr[p] = thirds(jnp.concatenate([restrict_scale * prolong[p * 4 + c].T for c in range(4)], axis=0))
    wp[...] = thirds(jnp.concatenate([prolong[c] for c in range(8)], axis=0))


def setup(diag_blocks, face_blocks, prolong):
    both = 2 * MATERIALS * MODES
    shapes = [(both, 3 * MODES), (both, 4 * MODES)] * 2
    shapes += [(MATERIALS * MODES, 3 * MODES), (2, 4 * MODES, 3 * MODES), (8 * MODES, 3 * MODES)]
    return pl.pallas_call(
        setup_kernel,
        out_shape=[jax.ShapeDtypeStruct(s, bf16) for s in shapes],
        in_specs=[pl.BlockSpec(memory_space=pltpu.VMEM)] * 3,
        out_specs=[pl.BlockSpec(memory_space=pltpu.VMEM)] * 7,
        compiler_params=pltpu.CompilerParams(vmem_limit_bytes=VMEM_LIMIT),
    )(diag_blocks, face_blocks, prolong)


def layer_start(depth):
    return sum(CY + 2 * (HALO - e) for e in range(1, depth))


def layer_of(index):
    depth, start = jnp.ones_like(index), jnp.zeros_like(index)
    for d in range(2, HALO + 1):
        inside = index >= layer_start(d)
        depth = jnp.where(inside, d, depth)
        start = jnp.where(inside, layer_start(d), start)
    return depth, index - start - (HALO - depth)


def pack_kernel(own, before, after, up, down):
    column = iota((1, 2 * TILE), 1)
    index = column % TILE
    depth, y = layer_of(index)
    z = jnp.where(column < TILE, CZ - depth, depth - 1)
    source = ((y + CY) // CY) * TILE + ((y + CY) % CY) * CZ + z
    source = jnp.where(index < layer_start(HALO + 1), source, -TILE)
    row = iota((3 * TILE, 2 * TILE), 0)
    for odd in range(2):
        selector = where_equal(row, source + odd * CY * CZ)
        parts = []
        for pair in range(CX):
            h, lane = divmod(pair * TILE, BLOCK)
            parts.append(jnp.concatenate([r[h, :, lane:lane + TILE] for r in (before, own, after)], axis=1))
        packed = place(jnp.concatenate(parts, axis=0), selector)
        for pair in range(CX):
            rows = packed[pair * ROWS:(pair + 1) * ROWS]
            up[2 * pair + odd] = rows[:, :TILE]
            down[2 * pair + odd] = rows[:, TILE:]


def pack(own, before, after):
    shape = jax.ShapeDtypeStruct((2 * CX, ROWS, TILE), f32)
    return pl.pallas_call(
        pack_kernel,
        out_shape=[shape, shape],
        in_specs=[pl.BlockSpec(memory_space=pltpu.VMEM)] * 3,
        out_specs=[pl.BlockSpec(memory_space=pltpu.VMEM)] * 2,
        compiler_params=pltpu.CompilerParams(vmem_limit_bytes=VMEM_LIMIT),
    )(own, before, after)


def fine_place(lane):
    y = (lane * 2979) >> 16
    return y - HALO, lane - y * PITCH - HALO


def unpack(own, before, after, low, high, put):
    lane = iota((1, LANES), 1)
    y, z = fine_place(lane)
    valid = lane < PITCH * PITCH
    inner = ((y + CY) // CY) * TILE + ((y + CY) % CY) * CZ + z
    depth = jnp.where(z < 0, -z, z - (CZ - 1))
    start = jnp.zeros_like(lane)
    for d in range(2, HALO + 1):
        start = jnp.where(depth == d, layer_start(d), start)
    inside = (y >= depth - HALO) & (y < CY + HALO - depth)
    outer = jnp.where(z < 0, 3 * TILE, 4 * TILE) + start + y + HALO - depth
    outer = jnp.where(inside, outer, -TILE)
    middle = (z >= 0) & (z < CZ)
    row = iota((5 * TILE, LANES), 0)
    for odd in range(2):
        source = jnp.where(middle, inner + odd * CY * CZ, outer)
        selector = where_equal(row, jnp.where(valid, source, -TILE))
        parts = []
        for pair in range(CX):
            h, at = divmod(pair * TILE, BLOCK)
            x = 2 * pair + odd
            parts.append(
                jnp.concatenate(
                    [r[h, :, at:at + TILE] for r in (before, own, after)] + [low[x], high[x]], axis=1
                )
            )
        placed = place(jnp.concatenate(parts, axis=0), selector)
        for pair in range(CX):
            rows = placed[pair * ROWS:(pair + 1) * ROWS]
            put(2 * pair + odd, rows[:MODES], rows[MODES:MODES + 1])


class Field:
    def __init__(self, full, high, low, shifts, masks):
        self.full, self.high, self.low = full, high, low
        self.shifts, self.masks = shifts, masks

    def put(self, x, value):
        self.full[x + 1] = value
        self.high[x + 1], self.low[x + 1] = split(value)

    def clear_ends(self):
        planes = self.full.shape[0]
        for x in (0, planes - 1):
            self.full[x] = jnp.zeros(self.full.shape[1:], f32)
            self.high[x] = jnp.zeros(self.full.shape[1:], bf16)
            self.low[x] = jnp.zeros(self.full.shape[1:], bf16)

    def get(self, x):
        return self.full[x + 1]


def field_scratch(planes, lanes):
    shape = (planes + 2, MODES, lanes)
    return [pltpu.VMEM(shape, f32), pltpu.VMEM(shape, bf16), pltpu.VMEM(shape, bf16)]


def grid_neighbours(lanes, size_y, size_z, used):
    lane = iota((1, lanes), 1)
    y, z = lane // size_z, lane % size_z
    inside = lane < used
    shifts = (lanes - size_z, size_z, lanes - 1, 1)
    masks = ((y < size_y - 1) & inside, (y > 0) & inside, (z < size_z - 1) & inside, (z > 0) & inside)
    return shifts, masks


def operate_plane(field, x, w1, w2, code):
    centre = field.get(x)
    moved = []
    for shift, mask in zip(field.shifts, field.masks):
        part = pltpu.roll(centre, shift, 1)
        moved.append(part if mask is None else jnp.where(mask, part, 0.0))
    moved_high, moved_low = split(jnp.concatenate(moved, axis=0))
    lanes = centre.shape[1]
    near_high = field.high[pl.ds(x, 3)].reshape(3 * MODES, lanes)
    near_low = field.low[pl.ds(x, 3)].reshape(3 * MODES, lanes)
    half = MATERIALS * MODES
    wide = dot(w1[...], near_high) + dot(w2[...], moved_high)
    total = wide[:half] + wide[half:] + dot(w1[:half], near_low) + dot(w2[:half], moved_low)
    return centre, pick(total, code, 1)


def planes_loop(start, count, body):
    def pair(i, carry):
        body(start + 2 * i)
        body(start + 2 * i + 1)
        return carry

    lax.fori_loop(0, count // 2, pair, 0)
    if count % 2:
        body(start + count - 1)


def sweep(source, target, start, count, w1, w2, gain, code):
    def body(x):
        centre, coupled = operate_plane(source, x, w1, w2, code[x])
        target.put(x, (1.0 - relax_weight) * centre + gain[x] - coupled)

    planes_loop(start, count, body)


def restrict_plane(wr, residuals, parity):
    out = 0.0
    for p in range(2):
        out = out + pick(dot(wr[p], stack3(residuals[p])), parity, 0)
    return out


def expand_planes(wp, raised_high, raised_low, parity):
    product = dot(wp[...], jnp.concatenate([raised_high, raised_low, raised_high], axis=0))
    return [pick(product[p * 4 * MODES:(p + 1) * 4 * MODES], parity, 0) for p in range(2)]


def gather_mid(gathered, sizes, put):
    n_gx, n_gy, n_gz = sizes
    per = MX * MY * MZ
    lines = MY * n_gz * MZ
    column = iota((1, n_gz * 2 * per), 1)
    k, rest = column % MZ, column // MZ
    gz, rest = rest % n_gz, rest // n_gz
    j, rest = rest % MY, rest // MY
    i, h = rest % MX, rest // MX
    source = gz * 2 * per + h * per + (i * MY + j) * MZ + k
    selector = where_equal(iota((n_gz * 2 * per, n_gz * 2 * per), 0), source)
    rows = gathered.shape[1]
    parts = []
    for block in range(n_gx * n_gy):
        parts.append(jnp.concatenate([gathered[block * n_gz + gz] for gz in range(n_gz)], axis=1))
    placed = place(jnp.concatenate(parts, axis=0), selector)
    lower = iota((1, TILE), 1) < lines
    for gx in range(n_gx):
        for i in range(MX):
            quarters = []
            for h in range(2):
                tiles = []
                for pair in range(n_gy // 2):
                    block = [placed[(gx * n_gy + 2 * pair + s) * rows:][:rows] for s in range(2)]
                    at = ((h * MX + i) * lines) // TILE * TILE
                    block = [b[:, at:at + TILE] for b in block]
                    if i % 2 == 0:
                        block[1] = pltpu.roll(block[1], lines, 1)
                    else:
                        block[0] = pltpu.roll(block[0], lines, 1)
                    tiles.append(jnp.where(lower, block[0], block[1]))
                quarters.append(jnp.concatenate(tiles, axis=1))
            put(gx * MX + i, quarters)


def solve_mid(source, gains, codes, fields, coarse, weights, grid):
    w1g, w2g, w1a, w2a, wi, wr, wp = weights
    planes, size_y, size_z = grid
    lanes = size_y * size_z
    gain, coarse_gain = gains
    code, coarse_code = codes
    first, second = fields
    coarse_source, coarse_fields = coarse
    for field in fields + coarse_fields:
        field.clear_ends()

    def start_mid(x):
        value = pick(dot(wi[...], stack3(source[x])), code[x], 1)
        gain[x] = value
        first.put(x, value)

    planes_loop(0, planes, start_mid)
    sweep(first, second, 0, planes, w1g, w2g, gain, code)
    lane = iota((1, lanes), 1)
    y, z = lane // size_z, lane % size_z
    parity = (y % 2) * 2 + z % 2
    tall, wide = iota((lanes, TILE), 0), iota((lanes, TILE), 1)
    squeeze = where_equal((tall // size_z // 2) * (size_z // 2) + tall % size_z // 2, wide)
    target = (y // 2) * (size_z // 2) + z // 2
    raise_lanes = where_equal(iota((TILE, lanes), 0), target)

    def down(x):
        residuals = []
        for p in range(2):
            unused, applied = operate_plane(second, 2 * x + p, w1a, w2a, code[2 * x + p])
            residuals.append(source[2 * x + p] - applied)
        coarse_value = place(restrict_plane(wr, residuals, parity), squeeze)
        value = pick(dot(wi[...], stack3(coarse_value)), coarse_code[x], 1)
        coarse_gain[x] = value
        coarse_fields[0].put(x, value)

    lax.fori_loop(0, planes // 2, lambda i, c: (down(i), c)[1], 0)
    now = 0
    for repeat in range(COARSE_SWEEPS - 1):
        sweep(coarse_fields[now], coarse_fields[1 - now], 0, planes // 2, w1g, w2g, coarse_gain, coarse_code)
        now = 1 - now
    result = coarse_fields[now]

    def up(x):
        high = dot(result.high[x + 1], raise_lanes).astype(bf16)
        low = dot(result.low[x + 1], raise_lanes).astype(bf16)
        for p, value in enumerate(expand_planes(wp, high, low, parity)):
            second.put(2 * x + p, second.get(2 * x + p) + value)

    lax.fori_loop(0, planes // 2, lambda i, c: (up(i), c)[1], 0)
    now = second
    for repeat in range(SWEEPS):
        other = first if now is second else second
        sweep(now, other, 0, planes, w1g, w2g, gain, code)
        now = other
    return now


def add_mid(place_ref, result, field, depth, wp, grid, old):
    planes, size_y, size_z = grid
    gx, gy, gz = place_ref[0], place_ref[1], place_ref[2]
    lane = iota((1, LANES), 1)
    y, z = fine_place(lane)
    parity = (y & 1) * 2 + (z & 1)
    whole_y, whole_z = y + gy * CY, z + gz * CZ
    inside = (lane < PITCH * PITCH) & (whole_y >= 0) & (whole_y < 2 * size_y) & (whole_z >= 0) & (whole_z < 2 * size_z)
    target = jnp.where(inside, (whole_y >> 1) * size_z + (whole_z >> 1), -1)
    raise_lanes = where_equal(iota((size_y * size_z, LANES), 0), target)
    start = gx * ((CX - depth) // 2)

    def up(i, carry):
        x = start + i
        high = dot(result.high[x + 1], raise_lanes).astype(bf16)
        low = dot(result.low[x + 1], raise_lanes).astype(bf16)
        for p, value in enumerate(expand_planes(wp, high, low, parity)):
            field.put(2 * x + p, old[2 * x + p] + value)
        return carry

    lax.fori_loop(0, (CX + depth) // 2, up, 0)


def fine_residual(field, own, source, wr, w1a, w2a, code):
    lane = iota((1, LANES), 1)
    y, z = fine_place(lane)
    parity = (y & 1) * 2 + (z & 1)
    tall, wide = iota((LANES, TILE), 0), iota((LANES, TILE), 1)
    y, z = fine_place(tall)
    inside = (tall < PITCH * PITCH) & (y >= 0) & (y < CY) & (z >= 0) & (z < CZ)
    target = jnp.where(inside, (y >> 1) * MZ + (z >> 1), -BLOCK)
    per = MX * MY * MZ
    index = wide % per
    total = jnp.zeros((MODES, TILE), f32)
    for i in range(MX):
        residuals = []
        for p in range(2):
            x = own + 2 * i + p
            unused, applied = operate_plane(field, x, w1a, w2a, code[x])
            residuals.append(source[2 * i + p] - applied)
        squeeze = where_equal(target + i * MY * MZ, index)
        total = total + place(restrict_plane(wr, residuals, parity), squeeze)
    half = MODES // 2
    return jnp.where(iota((1, TILE), 1) < per, total[:half], total[half:])


def fine_shifts():
    return (LANES - PITCH, PITCH, LANES - 1, 1), (None,) * 4


def first_kernel(grid, place_ref, own, before, after, low, high, w1g, w2g, w1a, w2a, wi, wr, wp,
                 gain, code, solved, source, payload, a0, a1, a2, b0, b1, b2, whole):
    first = Field(a0, a1, a2, *fine_shifts())
    second = Field(b0, b1, b2, *fine_shifts())
    first.clear_ends()
    second.clear_ends()
    gx = place_ref[0]

    def put(x, value, material):
        whole[x] = value
        code[x] = material

    unpack(own, before, after, low, high, put)

    def begin(x):
        value = pick(dot(wi[...], stack3(whole[x])), code[x], 1)
        gain[x] = value
        first.put(x, value)

    planes_loop(0, 2 * CX, begin)
    depth = HALO - 1
    sweep(first, second, gx * (CX - depth), CX + depth, w1g, w2g, gain, code)
    solved[...] = second.full[1:1 + 2 * CX]
    mine = gx * CX
    source[...] = whole[pl.ds(mine, CX)]
    payload[...] = fine_residual(second, mine, source, wr, w1a, w2a, code)


def mid_scratch(grid):
    planes, size_y, size_z = grid
    lanes = size_y * size_z
    return (
        field_scratch(planes, lanes) * 2
        + field_scratch(planes // 2, TILE) * 2
        + [
            pltpu.VMEM((planes, MODES, lanes), f32),
            pltpu.VMEM((planes, MODES, lanes), f32),
            pltpu.VMEM((planes // 2, MODES, TILE), f32),
            pltpu.VMEM((planes // 2, MODES, TILE), f32),
        ]
    )


def run_mid(gathered, sizes, grid, weights, scratch, mid_code, coarse_code, read_codes):
    planes, size_y, size_z = grid
    lanes = size_y * size_z
    near = grid_neighbours(lanes, size_y, size_z, lanes)
    coarse_near = grid_neighbours(TILE, size_y // 2, size_z // 2, lanes // 4)
    fields = [Field(*scratch[0:3], *near), Field(*scratch[3:6], *near)]
    coarse_fields = [Field(*scratch[6:9], *coarse_near), Field(*scratch[9:12], *coarse_near)]
    source, gain, coarse_source, coarse_gain = scratch[12:16]
    half = MODES // 2
    tall, wide = iota((lanes, TILE), 0), iota((lanes, TILE), 1)
    y, z = tall // size_z, tall % size_z
    corner = jnp.where((y % 2 == 0) & (z % 2 == 0), (y // 2) * (size_z // 2) + z // 2, -1)

    def put(x, quarters):
        source[x, :half] = quarters[0][:half]
        source[x, half:] = quarters[1][:half]
        if read_codes:
            mid_code[x] = quarters[0][half:half + 1]
            if x % 2 == 0:
                rows = jnp.broadcast_to(quarters[1][half:half + 1], (8, lanes)).astype(bf16)
                coarse_code[x // 2] = dot(rows, where_equal(corner, wide))[:1]

    gather_mid(gathered, sizes, put)
    return solve_mid(
        source, (gain, coarse_gain), (mid_code, coarse_code), fields, (coarse_source, coarse_fields), weights, grid
    )


def second_kernel(sizes, grid, place_ref, gathered, gain, code, solved, source, w1g, w2g, w1a, w2a, wi, wr, wp,
                  payload, result, mid_code, coarse_code, a0, a1, a2, b0, b1, b2, *scratch):
    weights = (w1g, w2g, w1a, w2a, wi, wr, wp)
    answer = run_mid(gathered, sizes, grid, weights, scratch, mid_code, coarse_code, True)
    now, other = Field(a0, a1, a2, *fine_shifts()), Field(b0, b1, b2, *fine_shifts())
    now.clear_ends()
    other.clear_ends()
    depth = 3 * SWEEPS
    gx = place_ref[0]
    add_mid(place_ref, answer, now, depth, wp, grid, solved)
    for repeat in range(2 * SWEEPS):
        depth -= 1
        sweep(now, other, gx * (CX - depth), CX + depth, w1g, w2g, gain, code)
        now, other = other, now
    payload[...] = fine_residual(now, gx * CX, source, wr, w1a, w2a, code)
    result[...] = now.full[1:1 + 2 * CX]


def third_kernel(sizes, grid, place_ref, gathered, mid_code, coarse_code, gain, code, solved,
                 w1g, w2g, w1a, w2a, wi, wr, wp, result, a0, a1, a2, b0, b1, b2, *scratch):
    weights = (w1g, w2g, w1a, w2a, wi, wr, wp)
    answer = run_mid(gathered, sizes, grid, weights, scratch, mid_code, coarse_code, False)
    now, other = Field(a0, a1, a2, *fine_shifts()), Field(b0, b1, b2, *fine_shifts())
    now.clear_ends()
    other.clear_ends()
    depth = SWEEPS
    gx = place_ref[0]
    add_mid(place_ref, answer, now, depth, wp, grid, solved)
    for repeat in range(SWEEPS):
        depth -= 1
        sweep(now, other, gx * (CX - depth), CX + depth, w1g, w2g, gain, code)
        now, other = other, now
    tall, wide = iota((LANES, TILE), 0), iota((LANES, TILE), 1)
    y, z = fine_place(tall)
    inside = (tall < PITCH * PITCH) & (y >= 0) & (y < CY) & (z >= 0) & (z < CZ)
    target = jnp.where(inside, y * CZ + z, -BLOCK)
    selectors = [where_equal(target + odd * CY * CZ, wide) for odd in range(2)]
    for pair in range(CX // 2):
        total = 0.0
        for odd in range(2):
            value = now.get(gx * CX + 2 * pair + odd)
            high, low = split(value)
            lowest = (value - high.astype(f32) - low.astype(f32)).astype(bf16)
            for part in (high, low, lowest):
                total = total + dot(part, selectors[odd])
        result[:, pair * TILE:(pair + 1) * TILE] = total


def call(kernel, out_shape, scratch, *args):
    vmem = pl.BlockSpec(memory_space=pltpu.VMEM)
    return pl.pallas_call(
        kernel,
        out_shape=out_shape,
        in_specs=[pl.BlockSpec(memory_space=pltpu.SMEM)] + [vmem] * (len(args) - 1),
        out_specs=jax.tree.map(lambda s: vmem, out_shape),
        scratch_shapes=scratch,
        compiler_params=pltpu.CompilerParams(vmem_limit_bytes=VMEM_LIMIT),
    )(*args)


def shape_of(*dims):
    return jax.ShapeDtypeStruct(dims, f32)


def wide_device(sizes, right_side, diag_blocks, face_blocks, prolong, mats_fine, mats_mid, mats_coarse):
    n_gx, n_gy, n_gz = sizes
    axes = ("gx", "gy", "gz")
    grid = (n_gx * MX, n_gy * MY, n_gz * MZ)
    place_ref = jnp.stack([lax.axis_index(a) for a in axes]).astype(jnp.int32)
    codes = (mats_fine.reshape(1, BLOCK) + 1).astype(f32)
    block = jnp.concatenate([right_side.reshape(MODES, BLOCK), jnp.broadcast_to(codes, (8, BLOCK))], axis=0)
    other = lax.ppermute(block, "gx", [(0, 1), (1, 0)])
    own = jnp.where(place_ref[0] == 0, jnp.stack([block, other]), jnp.stack([other, block]))
    up = {a: [(i, i + 1) for i in range(n - 1)] for a, n in zip(axes, sizes)}
    down = {a: [(j, i) for i, j in pairs] for a, pairs in up.items()}
    before, after = lax.ppermute(own, "gy", up["gy"]), lax.ppermute(own, "gy", down["gy"])
    send_up, send_down = pack(own, before, after)
    low, high = lax.ppermute(send_up, "gz", up["gz"]), lax.ppermute(send_down, "gz", down["gz"])
    weights = setup(diag_blocks, face_blocks, prolong)

    fine = field_scratch(2 * CX, LANES) * 2
    half, per = MODES // 2, MX * MY * MZ
    whole = shape_of(2 * CX, MODES, LANES)
    gain, code, solved, source, payload = call(
        partial(first_kernel, grid),
        [whole, shape_of(2 * CX, 1, LANES), whole, shape_of(CX, MODES, LANES), shape_of(half, TILE)],
        fine + [pltpu.VMEM((2 * CX, MODES, LANES), f32)],
        place_ref, own, before, after, low, high, *weights,
    )
    mid = (mats_mid.reshape(per) + 1).astype(f32)
    coarse = (mats_coarse.reshape(MX // 2, 1, MY // 2, 1, MZ // 2, 1) + 1).astype(f32)
    coarse = jnp.broadcast_to(coarse, (MX // 2, 2, MY // 2, 2, MZ // 2, 2)).reshape(per)
    tail = jnp.broadcast_to(jnp.concatenate([mid, coarse])[None], (8, TILE))

    def to_all(value):
        copies = jnp.broadcast_to(value[None], (n_gx * n_gy * n_gz,) + value.shape)
        return lax.all_to_all(copies, axes, 0, 0)

    planes, lanes = grid[0], grid[1] * grid[2]
    payload, solved, mid_code, coarse_code = call(
        partial(second_kernel, sizes, grid),
        [shape_of(half, TILE), whole, shape_of(planes, 1, lanes), shape_of(planes // 2, 1, TILE)],
        fine + mid_scratch(grid),
        place_ref, to_all(jnp.concatenate([payload, tail], axis=0)), gain, code, solved, source, *weights,
    )
    result = call(
        partial(third_kernel, sizes, grid),
        shape_of(MODES, BLOCK),
        fine + mid_scratch(grid),
        place_ref, to_all(payload), mid_code, coarse_code, gain, code, solved, *weights,
    )
    return result[None, None, None]


def solution(mesh):
    placed = (
        P("gx", "gy", "gz", None, None),
        P(),
        P(),
        P(),
        P("gx", "gy", "gz", None),
        P("gx", "gy", "gz", None),
        P("gx", "gy", "gz", None),
    )
    sizes = tuple(mesh.shape[a] for a in ("gx", "gy", "gz"))
    wide = sizes[0] == 2 and sizes[1] % 2 == 0 and sizes[2] * MY * MZ * 2 == TILE and sizes[1] <= 4
    return jax.shard_map(
        partial(wide_device, sizes) if wide else per_device,
        mesh=mesh,
        in_specs=placed,
        out_specs=P("gx", "gy", "gz", None, None),
        check_vma=False,
    )
```

```python
from functools import partial

import jax
import jax.numpy as jnp
from jax import lax
from jax.experimental import pallas as pl
from jax.experimental.pallas import tpu as pltpu
from jax.sharding import PartitionSpec as P

MODES = 64
MATERIALS = 4
SWEEPS = 2
COARSE_SWEEPS = 4
CYCLES = 2
CX = 8
CY = 8
CZ = 8


relax_weight = 0.7
restrict_scale = 0.6
highest = lax.Precision.HIGHEST


def padded_2(shard, sides, width):
    for axis, dim in sides:
        size, length = (lax.axis_size(axis), shard.shape[dim])
        up = [(i, (i + 1) % size) for i in range(size - 1)]
        down = [(j, i) for i, j in up]
        last = lax.slice_in_dim(shard, length - width, length, axis=dim)
        first = lax.slice_in_dim(shard, 0, width, axis=dim)
        before = lax.ppermute(last, axis, up)
        after = lax.ppermute(first, axis, down)
        shard = jnp.concatenate([before, shard, after], axis=dim)
    return shard


def inverse_blocks(diag_blocks):
    identity = jnp.eye(MODES, dtype=diag_blocks.dtype)
    result = []
    for material in range(MATERIALS):
        factor = jnp.linalg.cholesky(diag_blocks[material])
        result.append(jax.scipy.linalg.cho_solve((factor, True), identity))
    return jnp.stack(result).reshape(MATERIALS * MODES, MODES)


def coupling_matrix(diag_blocks, face_blocks):
    blocks = jnp.concatenate([diag_blocks[None], face_blocks], axis=0)
    return jnp.transpose(blocks, (1, 2, 0, 3)).reshape(MATERIALS * MODES, 7 * MODES)


def choose_blocks(weights, columns, onehot):
    product = jnp.dot(weights, columns, precision=highest, preferred_element_type=jnp.float32)
    product = product.reshape(MATERIALS, MODES, columns.shape[1])
    return jnp.sum(product * onehot.reshape(MATERIALS, 1, columns.shape[1]), axis=0)


def operate(padded, onehot, coupling):
    centre = padded[:, 1:-1, 1:-1, 1:-1]
    stacked = jnp.concatenate(
        [
            centre,
            padded[:, 2:, 1:-1, 1:-1],
            padded[:, :-2, 1:-1, 1:-1],
            padded[:, 1:-1, 2:, 1:-1],
            padded[:, 1:-1, :-2, 1:-1],
            padded[:, 1:-1, 1:-1, 2:],
            padded[:, 1:-1, 1:-1, :-2],
        ],
        axis=0,
    )
    columns = stacked.reshape(7 * MODES, -1)
    return choose_blocks(coupling, columns, onehot.reshape(MATERIALS, -1)).reshape(centre.shape)


def apply_inverse(inverse, field, onehot):
    return choose_blocks(inverse, field.reshape(MODES, -1), onehot.reshape(MATERIALS, -1)).reshape(
        field.shape
    )


def restrict(field, prolong):
    blocked = field.reshape(
        MODES, field.shape[1] // 2, 2, field.shape[2] // 2, 2, field.shape[3] // 2, 2
    )
    return restrict_scale * jnp.einsum(
        "abcji,jxaybzc->ixyz", prolong.reshape(2, 2, 2, MODES, MODES), blocked, precision=highest
    )


def expand(coarse_field, prolong):
    finer = jnp.einsum(
        "abcji,ixyz->jxaybzc",
        prolong.reshape(2, 2, 2, MODES, MODES),
        coarse_field,
        precision=highest,
    )
    return finer.reshape(
        MODES, 2 * coarse_field.shape[1], 2 * coarse_field.shape[2], 2 * coarse_field.shape[3]
    )


def make_onehot(materials):
    return (materials[None] == jnp.arange(MATERIALS, dtype=jnp.int32)[:, None, None, None]).astype(
        jnp.float32
    )


def fine_border(field):
    return padded_2(field, (("gx", 1), ("gy", 2), ("gz", 3)), 1)


def section_border(field):
    padded = padded_2(field, (("gx", 1), ("gy", 2)), 1)
    return jnp.pad(padded, ((0, 0), (0, 0), (0, 0), (1, 1)))


def smooth(iterate, source, onehot, border, inverse, coupling):
    residual = source - operate(border(iterate), onehot, coupling)
    return iterate + relax_weight * apply_inverse(inverse, residual, onehot)


def coarse_solve(source, onehot, border, inverse, coupling):
    iterate = relax_weight * apply_inverse(inverse, source, onehot)
    for repeat in range(COARSE_SWEEPS - 1):
        iterate = smooth(iterate, source, onehot, border, inverse, coupling)
    return iterate


def middle_cycle(source, onehot, border, inverse, coupling, prolong, coarse_solver):
    iterate = relax_weight * apply_inverse(inverse, source, onehot)
    iterate = smooth(iterate, source, onehot, border, inverse, coupling)
    residual = source - operate(border(iterate), onehot, coupling)
    iterate = iterate + expand(coarse_solver(restrict(residual, prolong)), prolong)
    for repeat in range(SWEEPS):
        iterate = smooth(iterate, source, onehot, border, inverse, coupling)
    return iterate


def single_steps(iterate, actions, source, onehot, inverse, coupling):
    residual = None
    for action in actions:
        if action == "sweep":
            iterate = smooth(iterate, source, onehot, fine_border, inverse, coupling)
        else:
            residual = source - operate(fine_border(iterate), onehot, coupling)
    return (iterate, residual)


def per_device(right_side, diag_blocks, face_blocks, prolong, mats_fine, mats_mid, mats_coarse):
    inverse = inverse_blocks(diag_blocks)
    coupling = coupling_matrix(diag_blocks, face_blocks)
    source = right_side[0, 0, 0].reshape(MODES, CX, CY, CZ)
    onehot_fine = make_onehot(mats_fine[0, 0, 0].reshape(CX, CY, CZ))
    onehot_mid = make_onehot(mats_mid[0, 0, 0].reshape(CX // 2, CY // 2, CZ // 2))
    onehot_coarse = make_onehot(mats_coarse[0, 0, 0].reshape(CX // 4, CY // 4, CZ // 4))
    stepper = partial(
        single_steps, source=source, onehot=onehot_fine, inverse=inverse, coupling=coupling
    )
    iterate = relax_weight * apply_inverse(inverse, source, onehot_fine)
    for cycle_index in range(CYCLES):
        if cycle_index == 0:
            actions = ["sweep"] * (SWEEPS - 1) + ["residual"]
        else:
            actions = ["sweep"] * SWEEPS + ["residual"]
        iterate, residual = stepper(iterate, actions)
        gathered_source = lax.all_gather(restrict(residual, prolong), "gz", axis=3, tiled=True)
        gathered_mid = lax.all_gather(onehot_mid, "gz", axis=3, tiled=True)
        gathered_coarse = lax.all_gather(onehot_coarse, "gz", axis=3, tiled=True)
        local_solver = partial(
            coarse_solve,
            onehot=gathered_coarse,
            border=section_border,
            inverse=inverse,
            coupling=coupling,
        )
        section_field = middle_cycle(
            gathered_source, gathered_mid, section_border, inverse, coupling, prolong, local_solver
        )
        iterate = iterate + expand(
            lax.dynamic_slice_in_dim(section_field, lax.axis_index("gz") * (CZ // 2), CZ // 2, 3),
            prolong,
        )
        iterate, unused_residual = stepper(iterate, ["sweep"] * SWEEPS)
    return iterate.reshape(MODES, CX * CY * CZ)[None, None, None]


HALO = 3 * SWEEPS + SWEEPS - 1
PITCH = CY + 2 * HALO
BLOCK = CX * CY * CZ
TILE = 128
LANES = -(-(PITCH * PITCH) // TILE) * TILE
ROWS = MODES + 8
MX, MY, MZ = CX // 2, CY // 2, CZ // 2
VMEM_LIMIT = 48 * 1024 * 1024
f32 = jnp.float32
bf16 = jnp.bfloat16


def split(value):
    high = value.astype(bf16)
    return high, (value - high.astype(f32)).astype(bf16)


def dot(a, b):
    return jnp.dot(a, b, preferred_element_type=f32)


def iota(shape, dim):
    return lax.broadcasted_iota(jnp.int32, shape, dim)


def where_equal(rows, columns):
    return jnp.where(rows == columns, 1.0, 0.0).astype(bf16)


def place(value, selector):
    high, low = split(value)
    return dot(high, selector) + dot(low, selector)


def pick(product, code, first):
    out = jnp.zeros((MODES, product.shape[1]), f32)
    for m in range(MATERIALS):
        out = jnp.where(code == m + first, product[m * MODES:(m + 1) * MODES], out)
    return out


def stack3(value):
    high, low = split(value)
    return jnp.concatenate([high, low, high], axis=0)


def thirds(value):
    high, low = split(value)
    return jnp.concatenate([high, high, low], axis=1)


def setup_kernel(diag, face, prolong, wg, wa, wd, wi, wr, wp):
    a = diag[...]
    row_id = iota((1, MODES, 1), 1)
    lane_id = iota((1, 1, MODES), 2)
    for k in range(MODES):
        pivot = 1.0 / a[:, k:k + 1, k:k + 1]
        on_row, on_lane = row_id == k, lane_id == k
        row = jnp.where(on_lane, pivot, a[:, k:k + 1, :] * pivot)
        column = a[:, :, k:k + 1]
        a = jnp.where(on_row, row, jnp.where(on_lane, 0.0, a) - column * row)
    scaled = relax_weight * a
    beside, gains = [], []
    for m in range(MATERIALS):
        faces = jnp.concatenate([face[d, m] for d in (1, 0, 2, 3, 4, 5)], axis=1)
        beside.append(faces)
        gains.append(jnp.dot(scaled[m], faces, precision=highest, preferred_element_type=f32))
    for target, blocks in ((wa, beside), (wg, gains)):
        high, low = split(jnp.concatenate(blocks, axis=0))
        target[...] = jnp.concatenate([high, low, high], axis=1)
    wd[...] = thirds(jnp.concatenate([diag[m] for m in range(MATERIALS)], axis=0))
    wi[...] = thirds(jnp.concatenate([scaled[m] for m in range(MATERIALS)], axis=0))
    for p in range(2):
        wr[p] = thirds(jnp.concatenate([restrict_scale * prolong[p * 4 + c].T for c in range(4)], axis=0))
    wp[...] = thirds(jnp.concatenate([prolong[c] for c in range(8)], axis=0))


def setup(diag_blocks, face_blocks, prolong):
    rows = MATERIALS * MODES
    shapes = [(rows, 18 * MODES)] * 2 + [(rows, 3 * MODES)] * 2
    shapes += [(2, 4 * MODES, 3 * MODES), (8 * MODES, 3 * MODES)]
    return pl.pallas_call(
        setup_kernel,
        out_shape=[jax.ShapeDtypeStruct(s, bf16) for s in shapes],
        in_specs=[pl.BlockSpec(memory_space=pltpu.VMEM)] * 3,
        out_specs=[pl.BlockSpec(memory_space=pltpu.VMEM)] * len(shapes),
        compiler_params=pltpu.CompilerParams(vmem_limit_bytes=VMEM_LIMIT),
    )(diag_blocks, face_blocks, prolong)


def layer_start(depth):
    return sum(CY + 2 * (HALO - e) for e in range(1, depth))


def layer_of(index):
    depth, start = jnp.ones_like(index), jnp.zeros_like(index)
    for d in range(2, HALO + 1):
        inside = index >= layer_start(d)
        depth = jnp.where(inside, d, depth)
        start = jnp.where(inside, layer_start(d), start)
    return depth, index - start - (HALO - depth)


def pack_kernel(own, before, after, up, down):
    column = iota((1, 2 * TILE), 1)
    index = column % TILE
    depth, y = layer_of(index)
    z = jnp.where(column < TILE, CZ - depth, depth - 1)
    source = ((y + CY) // CY) * TILE + ((y + CY) % CY) * CZ + z
    source = jnp.where(index < layer_start(HALO + 1), source, -TILE)
    row = iota((3 * TILE, 2 * TILE), 0)
    for odd in range(2):
        selector = where_equal(row, source + odd * CY * CZ)
        parts = []
        for pair in range(CX):
            h, lane = divmod(pair * TILE, BLOCK)
            parts.append(jnp.concatenate([r[h, :, lane:lane + TILE] for r in (before, own, after)], axis=1))
        packed = place(jnp.concatenate(parts, axis=0), selector)
        for pair in range(CX):
            rows = packed[pair * ROWS:(pair + 1) * ROWS]
            up[2 * pair + odd] = rows[:, :TILE]
            down[2 * pair + odd] = rows[:, TILE:]


def pack(own, before, after):
    shape = jax.ShapeDtypeStruct((2 * CX, ROWS, TILE), f32)
    return pl.pallas_call(
        pack_kernel,
        out_shape=[shape, shape],
        in_specs=[pl.BlockSpec(memory_space=pltpu.VMEM)] * 3,
        out_specs=[pl.BlockSpec(memory_space=pltpu.VMEM)] * 2,
        compiler_params=pltpu.CompilerParams(vmem_limit_bytes=VMEM_LIMIT),
    )(own, before, after)


def fine_place(lane):
    y = (lane * 2979) >> 16
    return y - HALO, lane - y * PITCH - HALO


def unpack(own, before, after, low, high, put):
    lane = iota((1, LANES), 1)
    y, z = fine_place(lane)
    valid = lane < PITCH * PITCH
    inner = ((y + CY) // CY) * TILE + ((y + CY) % CY) * CZ + z
    depth = jnp.where(z < 0, -z, z - (CZ - 1))
    start = jnp.zeros_like(lane)
    for d in range(2, HALO + 1):
        start = jnp.where(depth == d, layer_start(d), start)
    inside = (y >= depth - HALO) & (y < CY + HALO - depth)
    outer = jnp.where(z < 0, 3 * TILE, 4 * TILE) + start + y + HALO - depth
    outer = jnp.where(inside, outer, -TILE)
    middle = (z >= 0) & (z < CZ)
    row = iota((5 * TILE, LANES), 0)
    for odd in range(2):
        source = jnp.where(middle, inner + odd * CY * CZ, outer)
        selector = where_equal(row, jnp.where(valid, source, -TILE))
        parts = []
        for pair in range(CX):
            h, at = divmod(pair * TILE, BLOCK)
            x = 2 * pair + odd
            parts.append(
                jnp.concatenate(
                    [r[h, :, at:at + TILE] for r in (before, own, after)] + [low[x], high[x]], axis=1
                )
            )
        placed = place(jnp.concatenate(parts, axis=0), selector)
        for pair in range(CX):
            rows = placed[pair * ROWS:(pair + 1) * ROWS]
            put(2 * pair + odd, rows[:MODES], rows[MODES:MODES + 1])


class Field:
    def __init__(self, full, high, low, shifts, masks=(None,) * 4):
        self.full, self.high, self.low = full, high, low
        self.shifts, self.masks = shifts, masks

    def put(self, x, value):
        self.full[x + 1] = value
        self.high[x + 1], self.low[x + 1] = split(value)

    def put_parts(self, x, high, low):
        self.full[x + 1] = high + low
        self.high[x + 1], self.low[x + 1] = high.astype(bf16), low.astype(bf16)

    def clear_ends(self):
        planes = self.full.shape[0]
        for x in (0, planes - 1):
            self.full[x] = jnp.zeros(self.full.shape[1:], f32)
            self.high[x] = jnp.zeros(self.full.shape[1:], bf16)
            self.low[x] = jnp.zeros(self.full.shape[1:], bf16)

    def get(self, x):
        return self.full[x + 1]


def field_scratch(planes, lanes):
    shape = (planes + 2, MODES, lanes)
    return [pltpu.VMEM(shape, f32), pltpu.VMEM(shape, bf16), pltpu.VMEM(shape, bf16)]


class Layout:
    def __init__(self, halo, lanes):
        self.halo, self.lanes, self.pitch = halo, lanes, CY + 2 * halo
        self.used = self.pitch * self.pitch
        self.factor = -(-(1 << 16) // self.pitch)

    def place(self, lane):
        y = (lane * self.factor) >> 16
        return y - self.halo, lane - y * self.pitch - self.halo

    def parity(self):
        y, z = self.place(iota((1, self.lanes), 1))
        return (y & 1) * 2 + (z & 1)

    def shifts(self):
        return (self.lanes - self.pitch, self.pitch, self.lanes - 1, 1)

    def field(self, refs):
        return Field(*refs, self.shifts())

    def own_lanes(self, lane):
        y, z = self.place(lane)
        return y, z, (lane < self.used) & (y >= 0) & (y < CY) & (z >= 0) & (z < CZ)


def lanes_for(halo):
    return -(-((CY + 2 * halo) ** 2) // TILE) * TILE


NEAR = 2 * SWEEPS
wide_layout = Layout(HALO, lanes_for(HALO))
near_layout = Layout(NEAR, lanes_for(NEAR))


def near_selector():
    y, z = near_layout.place(iota((1, near_layout.lanes), 1))
    source = (y + HALO) * PITCH + z + HALO
    source = jnp.where(iota((1, near_layout.lanes), 1) < near_layout.used, source, -1)
    return where_equal(iota((LANES, near_layout.lanes), 0), source)


def coupled_rows(centre, field, x):
    moved = []
    for shift, mask in zip(field.shifts, field.masks):
        part = pltpu.roll(centre, shift, 1)
        moved.append(part if mask is None else jnp.where(mask, part, 0.0))
    high, low = split(jnp.concatenate(moved, axis=0))
    high = [field.high[x], field.high[x + 2], high]
    low = [field.low[x], field.low[x + 2], low]
    return jnp.concatenate(high + high + low, axis=0)


def grouped(start, count, size, body):
    groups = -(-count // size)
    least, more = divmod(count, groups)
    at = start
    for length, repeats in ((least + 1, more), (least, groups - more)):
        if repeats == 1:
            body(at, length)
        elif repeats > 1:
            def step(i, carry, at=at, length=length):
                body(at + i * length, length)
                return carry

            lax.fori_loop(0, repeats, step, 0)
        at = at + length * repeats


def group_size(lanes):
    return 5 if lanes > 2 * TILE else 11


def sweep(source, target, start, count, wg, gain, code, store=None):
    def body(first, length):
        values = []
        for x in [first + j for j in range(length)]:
            centre = source.get(x)
            product = dot(wg[...], coupled_rows(centre, source, x))
            values.append((1.0 - relax_weight) * centre + gain[x] - pick(product, code[x], 1))
        for j, value in enumerate(values):
            (store or target.put)(first + j, value)

    grouped(start, count, group_size(source.full.shape[2]), body)


def residual(field, x, source, wa, wd, code):
    centre = field.get(x)
    applied = dot(wa[...], coupled_rows(centre, field, x)) + dot(wd[...], stack3(centre))
    return source - pick(applied, code, 1)


def restrict_plane(wr, residuals, parity):
    out = 0.0
    for p in range(2):
        out = out + pick(dot(wr[p], stack3(residuals[p])), parity, 0)
    return out


def expand_planes(wp, raised_high, raised_low, parity):
    product = dot(wp[...], jnp.concatenate([raised_high, raised_low, raised_high], axis=0))
    return [pick(product[p * 4 * MODES:(p + 1) * 4 * MODES], parity, 0) for p in range(2)]


def gather_mid(place_ref, here, sibling, sizes, put):
    n_gx, n_gy, n_gz = sizes
    per = MX * MY * MZ
    lines = MY * n_gz * MZ
    column = iota((1, n_gz * 2 * per), 1)
    k, rest = column % MZ, column // MZ
    gz, rest = rest % n_gz, rest // n_gz
    j, rest = rest % MY, rest // MY
    i, h = rest % MX, rest // MX
    source = gz * 2 * per + h * per + (i * MY + j) * MZ + k
    selector = where_equal(iota((n_gz * 2 * per, n_gz * 2 * per), 0), source)
    rows = here.shape[2]
    my_x, my_y, my_z = place_ref[0], place_ref[1], place_ref[2]
    parts = []
    for gx in range(n_gx):
        for gy in range(n_gy):
            slot = ((gx ^ my_x) & 1) + 2 * (((gy ^ my_y) >> 1) & 1)
            line = []
            for gz in range(n_gz):
                turn = (my_z + n_gz - gz) % n_gz
                line.append(jnp.where(((gy ^ my_y) & 1) == 0, here[slot, turn], sibling[slot, turn]))
            parts.append(jnp.concatenate(line, axis=1))
    placed = place(jnp.concatenate(parts, axis=0), selector)
    lower = iota((1, TILE), 1) < lines
    for gx in range(n_gx):
        for i in range(MX):
            quarters = []
            for h in range(2):
                tiles = []
                for pair in range(n_gy // 2):
                    block = [placed[(gx * n_gy + 2 * pair + s) * rows:][:rows] for s in range(2)]
                    at = ((h * MX + i) * lines) // TILE * TILE
                    block = [b[:, at:at + TILE] for b in block]
                    if i % 2 == 0:
                        block[1] = pltpu.roll(block[1], lines, 1)
                    else:
                        block[0] = pltpu.roll(block[0], lines, 1)
                    tiles.append(jnp.where(lower, block[0], block[1]))
                quarters.append(jnp.concatenate(tiles, axis=1))
            put(gx * MX + i, quarters)


class Coarse:
    def __init__(self, grid):
        self.x, self.y, self.z = (size // 2 for size in grid)
        self.plane = self.y * self.z
        self.lanes = self.x * self.plane

    def place(self, lane):
        return lane // self.plane, lane // self.z % self.y, lane % self.z

    def solve(self, value, wg, wi, code):
        x, y, z = self.place(iota((1, self.lanes), 1))
        gain = pick(dot(wi[...], stack3(value)), code, 1)
        moves = (
            (self.plane, x > 0), (self.lanes - self.plane, x < self.x - 1),
            (self.lanes - self.z, y < self.y - 1), (self.z, y > 0),
            (self.lanes - 1, z < self.z - 1), (1, z > 0),
        )
        iterate = gain
        for repeat in range(COARSE_SWEEPS - 1):
            moved = [jnp.where(mask, pltpu.roll(iterate, shift, 1), 0.0) for shift, mask in moves]
            high, low = split(jnp.concatenate(moved, axis=0))
            product = dot(wg[...], jnp.concatenate([high, high, low], axis=0))
            iterate = (1.0 - relax_weight) * iterate + gain - pick(product, code, 1)
        return iterate


def solve_mid(source, gain, code, coarse_code, fields, weights, grid):
    wg, wa, wd, wi, wr, wp = weights
    planes, size_y, size_z = grid
    lanes = size_y * size_z
    first, second = fields
    coarse = Coarse(grid)
    for field in fields:
        field.clear_ends()
    for x in range(planes):
        gain[x] = pick(dot(wi[...], stack3(source[x])), code[x], 1)
    for x in range(planes):
        first.put(x, gain[x])
    sweep(first, second, 0, planes, wg, gain, code)
    lane = iota((1, lanes), 1)
    y, z = lane // size_z, lane % size_z
    parity = (y % 2) * 2 + z % 2
    tall, wide = iota((lanes, TILE), 0), iota((lanes, TILE), 1)
    squeeze = (tall // size_z // 2) * coarse.z + tall % size_z // 2
    per_tile = TILE // coarse.plane
    tiles = []
    for tile in range(coarse.lanes // TILE):
        total = 0.0
        for part in range(per_tile):
            pair = tile * per_tile + part
            rests = [residual(second, 2 * pair + p, source[2 * pair + p], wa, wd, code[2 * pair + p]) for p in range(2)]
            total = total + place(restrict_plane(wr, rests, parity), where_equal(squeeze + part * coarse.plane, wide))
        tiles.append(total)
    result = coarse.solve(jnp.concatenate(tiles, axis=1), wg, wi, coarse_code[...])
    target = (y // 2) * coarse.z + z // 2
    row = iota((coarse.lanes, lanes), 0)
    parts = jnp.concatenate(split(result), axis=0)
    for pair in range(coarse.x):
        raised = dot(parts, where_equal(row, target + pair * coarse.plane)).astype(bf16)
        for p, value in enumerate(expand_planes(wp, raised[:MODES], raised[MODES:], parity)):
            second.put(2 * pair + p, second.get(2 * pair + p) + value)
    now, other = second, first
    for repeat in range(SWEEPS):
        sweep(now, other, 0, planes, wg, gain, code)
        now, other = other, now
    return now


def add_mid(place_ref, layout, result, field, depth, wp, grid, old):
    planes, size_y, size_z = grid
    gx, gy, gz = place_ref[0], place_ref[1], place_ref[2]
    lane = iota((1, layout.lanes), 1)
    y, z = layout.place(lane)
    whole_y, whole_z = y + gy * CY, z + gz * CZ
    inside = (lane < layout.used) & (whole_y >= 0) & (whole_y < 2 * size_y) & (whole_z >= 0) & (whole_z < 2 * size_z)
    target = jnp.where(inside, (whole_y >> 1) * size_z + (whole_z >> 1), -1)
    raise_lanes = where_equal(iota((size_y * size_z, layout.lanes), 0), target)
    parity = layout.parity()

    def body(first, length):
        values = []
        for x in [first + j for j in range(length)]:
            parts = jnp.concatenate([result.high[x + 1], result.low[x + 1]], axis=0)
            raised = dot(parts, raise_lanes).astype(bf16)
            for p, value in enumerate(expand_planes(wp, raised[:MODES], raised[MODES:], parity)):
                values.append(old[2 * x + p] + value)
        for j, value in enumerate(values):
            field.put(2 * first + j, value)

    grouped(gx * ((CX - depth) // 2), (CX + depth) // 2, group_size(layout.lanes) // 2, body)


def fine_residual(field, own, source, wr, wa, wd, code):
    layout = near_layout
    tall, wide = iota((layout.lanes, TILE), 0), iota((layout.lanes, TILE), 1)
    y, z, inside = layout.own_lanes(tall)
    target = jnp.where(inside, (y >> 1) * MZ + (z >> 1), -BLOCK)
    per = MX * MY * MZ
    index = wide % per
    parity = layout.parity()
    total = jnp.zeros((MODES, TILE), f32)
    for i in range(MX):
        rests = [residual(field, own + 2 * i + p, source[2 * i + p], wa, wd, code[own + 2 * i + p]) for p in range(2)]
        total = total + place(restrict_plane(wr, rests, parity), where_equal(target + i * MY * MZ, index))
    half = MODES // 2
    return jnp.where(iota((1, TILE), 1) < per, total[:half], total[half:])


def first_kernel(grid, place_ref, own, before, after, low, high, wg, wa, wd, wi, wr, wp,
                 gain, code, solved, near_gain, near_code, source, payload, *scratch):
    first, second = wide_layout.field(scratch[0:3]), wide_layout.field(scratch[3:6])
    near = near_layout.field(scratch[6:9])
    whole = scratch[9]
    for field in (first, second, near):
        field.clear_ends()
    gx = place_ref[0]

    def put(x, value, material):
        whole[x] = value
        code[x] = material

    unpack(own, before, after, low, high, put)
    to_near = near_selector()
    planes = 2 * CX

    def begin(start, length):
        values = [pick(dot(wi[...], stack3(whole[start + j])), code[start + j], 1) for j in range(length)]
        for j, value in enumerate(values):
            gain[start + j] = value
            first.put(start + j, value)
            near_gain[start + j] = place(value, to_near)
        for j in range(length):
            near_code[start + j] = dot(jnp.broadcast_to(code[start + j], (8, LANES)).astype(bf16), to_near)[:1]

    grouped(0, planes, 4, begin)
    depth = HALO - 1
    sweep(first, second, gx * (CX - depth), CX + depth, wg, gain, code)
    solved[...] = second.full[1:1 + planes]
    for j in range(CX + 1):
        x = gx * (CX - 1) + j
        parts = dot(jnp.concatenate([second.high[x + 1], second.low[x + 1]], axis=0), to_near)
        near.put_parts(x, parts[:MODES], parts[MODES:])
    mine = gx * CX
    for j in range(CX):
        source[j] = place(whole[mine + j], to_near)
    payload[...] = fine_residual(near, mine, source, wr, wa, wd, near_code)


def mid_scratch(grid):
    planes, size_y, size_z = grid
    lanes = size_y * size_z
    return field_scratch(planes, lanes) * 2 + [pltpu.VMEM((planes, MODES, lanes), f32)] * 2


def run_mid(place_ref, here, sibling, sizes, grid, weights, scratch, mid_code, coarse_code, read_codes):
    planes, size_y, size_z = grid
    lanes = size_y * size_z
    lane = iota((1, lanes), 1)
    y, z = lane // size_z, lane % size_z
    shifts = (lanes - size_z, size_z, lanes - 1, 1)
    masks = (y < size_y - 1, y > 0, z < size_z - 1, z > 0)
    fields = [Field(*scratch[0:3], shifts, masks), Field(*scratch[3:6], shifts, masks)]
    source, gain = scratch[6:8]
    half = MODES // 2
    coarse = Coarse(grid)
    corners = []

    def put(x, quarters):
        source[x, :half] = quarters[0][:half]
        source[x, half:] = quarters[1][:half]
        if read_codes:
            mid_code[x] = quarters[0][half:half + 1]
            if x % 2 == 0:
                corners.append(jnp.broadcast_to(quarters[1][half:half + 1], (8, lanes)).astype(bf16))

    gather_mid(place_ref, here, sibling, sizes, put)
    if read_codes:
        tall, wide = iota((lanes, coarse.lanes), 0), iota((lanes, coarse.lanes), 1)
        x, cy, cz = coarse.place(wide)
        total = 0.0
        for pair in range(coarse.x):
            selector = where_equal(jnp.where(x == pair, 2 * cy * size_z + 2 * cz, -1), tall)
            total = total + dot(corners[pair], selector)
        coarse_code[...] = total[:1]
    return solve_mid(source, gain, mid_code, coarse_code, fields, weights, grid)


def second_kernel(sizes, grid, place_ref, here, sibling, gain, code, solved, near_gain, near_code, source,
                  wg, wa, wd, wi, wr, wp, payload, result, mid_code, coarse_code, *scratch):
    weights = (wg, wa, wd, wi, wr, wp)
    answer = run_mid(place_ref, here, sibling, sizes, grid, weights, scratch[12:], mid_code, coarse_code, True)
    first, second = wide_layout.field(scratch[0:3]), wide_layout.field(scratch[3:6])
    now, other = near_layout.field(scratch[6:9]), near_layout.field(scratch[9:12])
    for field in (first, second, now, other):
        field.clear_ends()
    depth = 3 * SWEEPS
    gx = place_ref[0]
    add_mid(place_ref, wide_layout, answer, first, depth, wp, grid, solved)
    to_near = near_selector()

    def narrow(x, value):
        parts = dot(jnp.concatenate(split(value), axis=0), to_near)
        now.put_parts(x, parts[:MODES], parts[MODES:])

    for repeat in range(2 * SWEEPS):
        depth -= 1
        start, count = gx * (CX - depth), CX + depth
        if depth > NEAR:
            sweep(first, second, start, count, wg, gain, code)
            first, second = second, first
        elif depth == NEAR:
            sweep(first, None, start, count, wg, gain, code, narrow)
        else:
            sweep(now, other, start, count, wg, near_gain, near_code)
            now, other = other, now
    payload[...] = fine_residual(now, gx * CX, source, wr, wa, wd, near_code)
    result[...] = now.full[1:1 + 2 * CX]


def third_kernel(sizes, grid, place_ref, here, sibling, mid_code, coarse_code, near_gain, near_code, solved,
                 wg, wa, wd, wi, wr, wp, result, *scratch):
    weights = (wg, wa, wd, wi, wr, wp)
    answer = run_mid(place_ref, here, sibling, sizes, grid, weights, scratch[6:], mid_code, coarse_code, False)
    layout = near_layout
    now, other = layout.field(scratch[0:3]), layout.field(scratch[3:6])
    now.clear_ends()
    other.clear_ends()
    depth = SWEEPS
    gx = place_ref[0]
    add_mid(place_ref, layout, answer, now, depth, wp, grid, solved)
    for repeat in range(SWEEPS):
        depth -= 1
        sweep(now, other, gx * (CX - depth), CX + depth, wg, near_gain, near_code)
        now, other = other, now
    tall, wide = iota((layout.lanes, TILE), 0), iota((layout.lanes, TILE), 1)
    y, z, inside = layout.own_lanes(tall)
    target = jnp.where(inside, y * CZ + z, -BLOCK)
    selectors = [where_equal(target + odd * CY * CZ, wide) for odd in range(2)]
    for pair in range(CX // 2):
        total = 0.0
        for odd in range(2):
            value = now.get(gx * CX + 2 * pair + odd)
            high, low = split(value)
            lowest = (value - high.astype(f32) - low.astype(f32)).astype(bf16)
            for part in (high, low, lowest):
                total = total + dot(part, selectors[odd])
        result[:, pair * TILE:(pair + 1) * TILE] = total


def call(kernel, out_shape, scratch, *args):
    vmem = pl.BlockSpec(memory_space=pltpu.VMEM)
    return pl.pallas_call(
        kernel,
        out_shape=out_shape,
        in_specs=[pl.BlockSpec(memory_space=pltpu.SMEM)] + [vmem] * (len(args) - 1),
        out_specs=jax.tree.map(lambda s: vmem, out_shape),
        scratch_shapes=scratch,
        compiler_params=pltpu.CompilerParams(vmem_limit_bytes=VMEM_LIMIT),
    )(*args)


def shape_of(*dims):
    return jax.ShapeDtypeStruct(dims, f32)


def wide_device(sizes, right_side, diag_blocks, face_blocks, prolong, mats_fine, mats_mid, mats_coarse):
    n_gx, n_gy, n_gz = sizes
    axes = ("gx", "gy", "gz")
    grid = (n_gx * MX, n_gy * MY, n_gz * MZ)
    place_ref = jnp.stack([lax.axis_index(a) for a in axes]).astype(jnp.int32)
    codes = (mats_fine.reshape(1, BLOCK) + 1).astype(f32)
    block = jnp.concatenate([right_side.reshape(MODES, BLOCK), jnp.broadcast_to(codes, (8, BLOCK))], axis=0)
    other = lax.ppermute(block, "gx", [(0, 1), (1, 0)])
    own = jnp.where(place_ref[0] == 0, jnp.stack([block, other]), jnp.stack([other, block]))
    up = {a: [(i, i + 1) for i in range(n - 1)] for a, n in zip(axes, sizes)}
    down = {a: [(j, i) for i, j in pairs] for a, pairs in up.items()}
    before, after = lax.ppermute(own, "gy", up["gy"]), lax.ppermute(own, "gy", down["gy"])
    send_up, send_down = pack(own, before, after)
    low, high = lax.ppermute(send_up, "gz", up["gz"]), lax.ppermute(send_down, "gz", down["gz"])
    weights = setup(diag_blocks, face_blocks, prolong)

    wide = field_scratch(2 * CX, LANES)
    near = field_scratch(2 * CX, near_layout.lanes)
    half, per = MODES // 2, MX * MY * MZ
    whole = shape_of(2 * CX, MODES, LANES)
    small = shape_of(2 * CX, MODES, near_layout.lanes)
    gain, code, solved, near_gain, near_code, source, payload = call(
        partial(first_kernel, grid),
        [whole, shape_of(2 * CX, 1, LANES), whole, small, shape_of(2 * CX, 1, near_layout.lanes),
         shape_of(CX, MODES, near_layout.lanes), shape_of(half, TILE)],
        wide * 2 + near + [pltpu.VMEM((2 * CX, MODES, LANES), f32)],
        place_ref, own, before, after, low, high, *weights,
    )
    mid = (mats_mid.reshape(per) + 1).astype(f32)
    coarse = (mats_coarse.reshape(MX // 2, 1, MY // 2, 1, MZ // 2, 1) + 1).astype(f32)
    coarse = jnp.broadcast_to(coarse, (MX // 2, 2, MY // 2, 2, MZ // 2, 2)).reshape(per)
    tail = jnp.broadcast_to(jnp.concatenate([mid, coarse])[None], (8, TILE))

    def to_all(value):
        turns = [[(i, (i + s) % n_gz) for i in range(n_gz)] for s in range(1, n_gz)]
        column = jnp.stack([value] + [lax.ppermute(value, "gz", turn) for turn in turns])
        flips = [
            [(i * n_gy + j, (i ^ dx) * n_gy + (j ^ dy)) for i in range(n_gx) for j in range(n_gy)]
            for dx, dy in ((1, 0), (0, 2), (1, 2))
        ]
        here = jnp.stack([column] + [lax.ppermute(column, ("gx", "gy"), flip) for flip in flips])
        return here, lax.ppermute(here, "gy", [(j, j ^ 1) for j in range(n_gy)])

    planes, lanes = grid[0], grid[1] * grid[2]
    payload, solved, mid_code, coarse_code = call(
        partial(second_kernel, sizes, grid),
        [shape_of(half, TILE), small, shape_of(planes, 1, lanes), shape_of(1, planes * lanes // 8)],
        wide * 2 + near * 2 + mid_scratch(grid),
        place_ref, *to_all(jnp.concatenate([payload, tail], axis=0)), gain, code, solved,
        near_gain, near_code, source, *weights,
    )
    result = call(
        partial(third_kernel, sizes, grid),
        shape_of(MODES, BLOCK),
        near * 2 + mid_scratch(grid),
        place_ref, *to_all(payload), mid_code, coarse_code, near_gain, near_code, solved, *weights,
    )
    return result[None, None, None]


def solution(mesh):
    placed = (
        P("gx", "gy", "gz", None, None),
        P(),
        P(),
        P(),
        P("gx", "gy", "gz", None),
        P("gx", "gy", "gz", None),
        P("gx", "gy", "gz", None),
    )
    sizes = tuple(mesh.shape[a] for a in ("gx", "gy", "gz"))
    wide = sizes[0] == 2 and sizes[1] == 4 and sizes[2] * MY * MZ * 2 == TILE
    return jax.shard_map(
        partial(wide_device, sizes) if wide else per_device,
        mesh=mesh,
        in_specs=placed,
        out_specs=P("gx", "gy", "gz", None, None),
        check_vma=False,
    )
```

```python
from functools import partial

import jax
import jax.numpy as jnp
from jax import lax
from jax.experimental import pallas as pl
from jax.experimental.pallas import tpu as pltpu
from jax.sharding import PartitionSpec as P

MODES = 64
MATERIALS = 4
SWEEPS = 2
COARSE_SWEEPS = 4
CYCLES = 2
CX = 8
CY = 8
CZ = 8


relax_weight = 0.7
restrict_scale = 0.6
highest = lax.Precision.HIGHEST


def padded_2(shard, sides, width):
    for axis, dim in sides:
        size, length = (lax.axis_size(axis), shard.shape[dim])
        up = [(i, (i + 1) % size) for i in range(size - 1)]
        down = [(j, i) for i, j in up]
        last = lax.slice_in_dim(shard, length - width, length, axis=dim)
        first = lax.slice_in_dim(shard, 0, width, axis=dim)
        before = lax.ppermute(last, axis, up)
        after = lax.ppermute(first, axis, down)
        shard = jnp.concatenate([before, shard, after], axis=dim)
    return shard


def inverse_blocks(diag_blocks):
    identity = jnp.eye(MODES, dtype=diag_blocks.dtype)
    result = []
    for material in range(MATERIALS):
        factor = jnp.linalg.cholesky(diag_blocks[material])
        result.append(jax.scipy.linalg.cho_solve((factor, True), identity))
    return jnp.stack(result).reshape(MATERIALS * MODES, MODES)


def coupling_matrix(diag_blocks, face_blocks):
    blocks = jnp.concatenate([diag_blocks[None], face_blocks], axis=0)
    return jnp.transpose(blocks, (1, 2, 0, 3)).reshape(MATERIALS * MODES, 7 * MODES)


def choose_blocks(weights, columns, onehot):
    product = jnp.dot(weights, columns, precision=highest, preferred_element_type=jnp.float32)
    product = product.reshape(MATERIALS, MODES, columns.shape[1])
    return jnp.sum(product * onehot.reshape(MATERIALS, 1, columns.shape[1]), axis=0)


def operate(padded, onehot, coupling):
    centre = padded[:, 1:-1, 1:-1, 1:-1]
    stacked = jnp.concatenate(
        [
            centre,
            padded[:, 2:, 1:-1, 1:-1],
            padded[:, :-2, 1:-1, 1:-1],
            padded[:, 1:-1, 2:, 1:-1],
            padded[:, 1:-1, :-2, 1:-1],
            padded[:, 1:-1, 1:-1, 2:],
            padded[:, 1:-1, 1:-1, :-2],
        ],
        axis=0,
    )
    columns = stacked.reshape(7 * MODES, -1)
    return choose_blocks(coupling, columns, onehot.reshape(MATERIALS, -1)).reshape(centre.shape)


def apply_inverse(inverse, field, onehot):
    return choose_blocks(inverse, field.reshape(MODES, -1), onehot.reshape(MATERIALS, -1)).reshape(
        field.shape
    )


def restrict(field, prolong):
    blocked = field.reshape(
        MODES, field.shape[1] // 2, 2, field.shape[2] // 2, 2, field.shape[3] // 2, 2
    )
    return restrict_scale * jnp.einsum(
        "abcji,jxaybzc->ixyz", prolong.reshape(2, 2, 2, MODES, MODES), blocked, precision=highest
    )


def expand(coarse_field, prolong):
    finer = jnp.einsum(
        "abcji,ixyz->jxaybzc",
        prolong.reshape(2, 2, 2, MODES, MODES),
        coarse_field,
        precision=highest,
    )
    return finer.reshape(
        MODES, 2 * coarse_field.shape[1], 2 * coarse_field.shape[2], 2 * coarse_field.shape[3]
    )


def make_onehot(materials):
    return (materials[None] == jnp.arange(MATERIALS, dtype=jnp.int32)[:, None, None, None]).astype(
        jnp.float32
    )


def fine_border(field):
    return padded_2(field, (("gx", 1), ("gy", 2), ("gz", 3)), 1)


def section_border(field):
    padded = padded_2(field, (("gx", 1), ("gy", 2)), 1)
    return jnp.pad(padded, ((0, 0), (0, 0), (0, 0), (1, 1)))


def smooth(iterate, source, onehot, border, inverse, coupling):
    residual = source - operate(border(iterate), onehot, coupling)
    return iterate + relax_weight * apply_inverse(inverse, residual, onehot)


def coarse_solve(source, onehot, border, inverse, coupling):
    iterate = relax_weight * apply_inverse(inverse, source, onehot)
    for repeat in range(COARSE_SWEEPS - 1):
        iterate = smooth(iterate, source, onehot, border, inverse, coupling)
    return iterate


def middle_cycle(source, onehot, border, inverse, coupling, prolong, coarse_solver):
    iterate = relax_weight * apply_inverse(inverse, source, onehot)
    iterate = smooth(iterate, source, onehot, border, inverse, coupling)
    residual = source - operate(border(iterate), onehot, coupling)
    iterate = iterate + expand(coarse_solver(restrict(residual, prolong)), prolong)
    for repeat in range(SWEEPS):
        iterate = smooth(iterate, source, onehot, border, inverse, coupling)
    return iterate


def single_steps(iterate, actions, source, onehot, inverse, coupling):
    residual = None
    for action in actions:
        if action == "sweep":
            iterate = smooth(iterate, source, onehot, fine_border, inverse, coupling)
        else:
            residual = source - operate(fine_border(iterate), onehot, coupling)
    return (iterate, residual)


def per_device(right_side, diag_blocks, face_blocks, prolong, mats_fine, mats_mid, mats_coarse):
    inverse = inverse_blocks(diag_blocks)
    coupling = coupling_matrix(diag_blocks, face_blocks)
    source = right_side[0, 0, 0].reshape(MODES, CX, CY, CZ)
    onehot_fine = make_onehot(mats_fine[0, 0, 0].reshape(CX, CY, CZ))
    onehot_mid = make_onehot(mats_mid[0, 0, 0].reshape(CX // 2, CY // 2, CZ // 2))
    onehot_coarse = make_onehot(mats_coarse[0, 0, 0].reshape(CX // 4, CY // 4, CZ // 4))
    stepper = partial(
        single_steps, source=source, onehot=onehot_fine, inverse=inverse, coupling=coupling
    )
    iterate = relax_weight * apply_inverse(inverse, source, onehot_fine)
    for cycle_index in range(CYCLES):
        if cycle_index == 0:
            actions = ["sweep"] * (SWEEPS - 1) + ["residual"]
        else:
            actions = ["sweep"] * SWEEPS + ["residual"]
        iterate, residual = stepper(iterate, actions)
        gathered_source = lax.all_gather(restrict(residual, prolong), "gz", axis=3, tiled=True)
        gathered_mid = lax.all_gather(onehot_mid, "gz", axis=3, tiled=True)
        gathered_coarse = lax.all_gather(onehot_coarse, "gz", axis=3, tiled=True)
        local_solver = partial(
            coarse_solve,
            onehot=gathered_coarse,
            border=section_border,
            inverse=inverse,
            coupling=coupling,
        )
        section_field = middle_cycle(
            gathered_source, gathered_mid, section_border, inverse, coupling, prolong, local_solver
        )
        iterate = iterate + expand(
            lax.dynamic_slice_in_dim(section_field, lax.axis_index("gz") * (CZ // 2), CZ // 2, 3),
            prolong,
        )
        iterate, unused_residual = stepper(iterate, ["sweep"] * SWEEPS)
    return iterate.reshape(MODES, CX * CY * CZ)[None, None, None]


HALO = 3 * SWEEPS + SWEEPS - 1
PITCH = CY + 2 * HALO
BLOCK = CX * CY * CZ
TILE = 128
LANES = -(-(PITCH * PITCH) // TILE) * TILE
ROWS = MODES + 8
MX, MY, MZ = CX // 2, CY // 2, CZ // 2
f32 = jnp.float32
bf16 = jnp.bfloat16


def split(value):
    high = value.astype(bf16)
    return high, (value - high.astype(f32)).astype(bf16)


def dot(a, b):
    return jnp.dot(a, b, preferred_element_type=f32)


def iota(shape, dim):
    return lax.broadcasted_iota(jnp.int32, shape, dim)


def where_equal(rows, columns):
    return jnp.where(rows == columns, 1.0, 0.0).astype(bf16)


def place(value, selector):
    high, low = split(value)
    return dot(high, selector) + dot(low, selector)


def pick(product, code, first):
    out = jnp.zeros((MODES, product.shape[1]), f32)
    for m in range(MATERIALS):
        out = jnp.where(code == m + first, product[m * MODES:(m + 1) * MODES], out)
    return out


def stack3(value):
    high, low = split(value)
    return jnp.concatenate([high, low, high], axis=0)


def thirds(value):
    high, low = split(value)
    return jnp.concatenate([high, high, low], axis=1)


def inverse_kernel(diag, scaled):
    a = diag[...]
    row_id = iota((1, MODES, 1), 1)
    lane_id = iota((1, 1, MODES), 2)
    for k in range(MODES):
        pivot = 1.0 / a[:, k:k + 1, k:k + 1]
        on_row, on_lane = row_id == k, lane_id == k
        row = jnp.where(on_lane, pivot, a[:, k:k + 1, :] * pivot)
        column = a[:, :, k:k + 1]
        a = jnp.where(on_row, row, jnp.where(on_lane, 0.0, a) - column * row)
    scaled[...] = relax_weight * a


def weights_kernel(scaled, diag, face, prolong, wg, wa, wd, wi, wr, wp):
    beside, gains = [], []
    for m in range(MATERIALS):
        faces = jnp.concatenate([face[d, m] for d in (1, 0, 2, 3, 4, 5)], axis=1)
        beside.append(faces)
        gains.append(jnp.dot(scaled[m], faces, precision=highest, preferred_element_type=f32))
    for target, blocks in ((wa, beside), (wg, gains)):
        high, low = split(jnp.concatenate(blocks, axis=0))
        target[...] = jnp.concatenate([high, low, high], axis=1)
    wd[...] = thirds(jnp.concatenate([diag[m] for m in range(MATERIALS)], axis=0))
    wi[...] = thirds(jnp.concatenate([scaled[m] for m in range(MATERIALS)], axis=0))
    for p in range(2):
        wr[p] = thirds(jnp.concatenate([restrict_scale * prolong[p * 4 + c].T for c in range(4)], axis=0))
    wp[...] = thirds(jnp.concatenate([prolong[c] for c in range(8)], axis=0))


def invert(diag_blocks):
    return call(inverse_kernel, 6, shape_of(*diag_blocks.shape), [], diag_blocks)


def make_weights(scaled, diag_blocks, face_blocks, prolong):
    rows = MATERIALS * MODES
    shapes = [(rows, 18 * MODES)] * 2 + [(rows, 3 * MODES)] * 2
    shapes += [(2, 4 * MODES, 3 * MODES), (8 * MODES, 3 * MODES)]
    shapes = [jax.ShapeDtypeStruct(shape, bf16) for shape in shapes]
    return call(weights_kernel, 1, shapes, [], scaled, diag_blocks, face_blocks, prolong)


SHALLOW = SWEEPS
PAIRS = CX
SLOT = CY * CZ


def layer_rows(depth, halo):
    return CY + 2 * (halo - depth)


SHALLOW_LANES = sum(layer_rows(d, SHALLOW) for d in range(1, SHALLOW + 1))
DEEP_LANES = sum(layer_rows(d, HALO) for d in range(1, HALO + 1))
PER_TILE = TILE // (2 * SHALLOW_LANES)
SHALLOW_TILES = -(-PAIRS // PER_TILE)


def layer_of(index, first, last, halo):
    depth, start, at = jnp.full_like(index, first), jnp.zeros_like(index), 0
    for d in range(first + 1, last + 1):
        at += layer_rows(d - 1, halo)
        inside = index >= at
        depth, start = jnp.where(inside, d, depth), jnp.where(inside, at, start)
    return depth, index - start - (halo - depth)


def lane_of(depth, y, first, last, halo):
    start, at = jnp.zeros_like(depth), 0
    for d in range(first + 1, last + 1):
        at += layer_rows(d - 1, halo)
        start = jnp.where(depth == d, at, start)
    inside = (depth >= first) & (depth <= last) & (y >= depth - halo) & (y < CY + halo - depth)
    return jnp.where(inside, start + y + halo - depth, -(1 << 20))


def prepare_kernel(place_ref, values, other, materials, other_materials, out):
    mine = place_ref[0]
    for half, (block, kinds) in enumerate(((values, materials), (other, other_materials))):
        first = (mine ^ half) * (BLOCK // TILE)
        codes = jnp.broadcast_to((kinds[...] + 1).astype(f32), (ROWS - MODES, BLOCK))
        for tile in range(BLOCK // TILE):
            lanes = slice(tile * TILE, (tile + 1) * TILE)
            out[first + tile, :MODES] = block[:, lanes]
            out[first + tile, MODES:] = codes[:, lanes]


def pack_kernel(own, before, after, shallow_up, shallow_down, deep_up, deep_down):
    column = iota((1, 4 * TILE), 1)
    lane, kind = column % TILE, column // TILE
    row = iota((3 * TILE, 4 * TILE), 0)
    parts = [jnp.concatenate([r[pair] for r in (before, own, after)], axis=1) for pair in range(PAIRS)]
    parts = split(jnp.concatenate(parts, axis=0))
    shallow = 0.0
    for odd in range(2):
        thin = lane - odd * SHALLOW_LANES
        thin_depth, thin_y = layer_of(thin, 1, SHALLOW, SHALLOW)
        thick_depth, thick_y = layer_of(lane, 1, HALO, HALO)
        depth = jnp.where(kind < 2, thin_depth, thick_depth)
        y = jnp.where(kind < 2, thin_y, thick_y)
        valid = jnp.where(
            kind < 2,
            jnp.where((thin >= 0) & (thin < SHALLOW_LANES), 1, 0),
            jnp.where(lane < DEEP_LANES, 1, 0),
        )
        z = jnp.where(kind % 2 == 0, CZ - depth, depth - 1)
        source = ((y + CY) // CY) * TILE + ((y + CY) % CY) * CZ + z + odd * SLOT
        selector = where_equal(row, jnp.where(valid == 1, source, -1))
        packed = dot(parts[0], selector) + dot(parts[1], selector)
        shallow = shallow + packed[:, :2 * TILE]
        for pair in range(PAIRS):
            rows = packed[pair * ROWS:(pair + 1) * ROWS]
            deep_up[2 * pair + odd], deep_down[2 * pair + odd] = rows[:, 2 * TILE:3 * TILE], rows[:, 3 * TILE:]
    for tile in range(SHALLOW_TILES):
        for kind, out in enumerate((shallow_up, shallow_down)):
            strip = 0.0
            for slot in range(PER_TILE):
                pair = tile * PER_TILE + slot
                if pair < PAIRS:
                    piece = shallow[pair * ROWS:(pair + 1) * ROWS, kind * TILE:(kind + 1) * TILE]
                    strip = strip + (pltpu.roll(piece, slot * 2 * SHALLOW_LANES, 1) if slot else piece)
            out[tile] = strip


def shallow_strip(low, high, pair):
    tile, slot = pair // PER_TILE, pair % PER_TILE
    shift = (TILE - slot * 2 * SHALLOW_LANES) % TILE
    lane = iota((1, TILE), 1)
    return jnp.where(
        lane < TILE // 2,
        pltpu.roll(low[tile], shift, 1),
        pltpu.roll(high[tile], (shift + TILE // 2) % TILE, 1),
    )


def unpack(layout, own, before, after, low, high, first, pairs, put, shallow):
    lane = iota((1, layout.lanes), 1)
    y, z = layout.place(lane)
    inner = ((y + CY) // CY) * TILE + ((y + CY) % CY) * CZ + z
    depth = jnp.where(z < 0, -z, z - (CZ - 1))
    middle = (z >= 0) & (z < CZ)
    if shallow:
        outer = lane_of(depth, y, 1, SHALLOW, SHALLOW) + jnp.where(z < 0, 3 * TILE, 3 * TILE + TILE // 2)
        step = SHALLOW_LANES
    else:
        outer = lane_of(depth, y, 1, HALO, HALO) + jnp.where(z < 0, 3 * TILE, 4 * TILE)
        step = 0
    row = iota(((4 if shallow else 5) * TILE, layout.lanes), 0)
    parts = []
    for odd in range(2):
        if odd == 0 or not shallow:
            parts = []
            for i in range(pairs):
                pair = first + i
                line = [r[pair] for r in (before, own, after)]
                line += [shallow_strip(low, high, pair)] if shallow else [r[2 * pair + odd] for r in (low, high)]
                parts.append(jnp.concatenate(line, axis=1))
            parts = split(jnp.concatenate(parts, axis=0))
        source = jnp.where(middle, inner + odd * SLOT, outer + odd * step)
        selector = where_equal(row, jnp.where(lane < layout.used, source, -1))
        placed = dot(parts[0], selector) + dot(parts[1], selector)
        for i in range(pairs):
            rows = placed[i * ROWS:(i + 1) * ROWS]
            put(2 * (first + i) + odd, rows[:MODES], rows[MODES:MODES + 1])


class Field:
    def __init__(self, full, high, low, shifts, masks=(None,) * 4):
        self.full, self.high, self.low = full, high, low
        self.shifts, self.masks = shifts, masks

    def put(self, x, value):
        self.full[x + 1] = value
        self.high[x + 1], self.low[x + 1] = split(value)

    def put_parts(self, x, high, low):
        self.full[x + 1] = high + low
        self.high[x + 1], self.low[x + 1] = high.astype(bf16), low.astype(bf16)

    def clear_ends(self):
        planes = self.full.shape[0]
        for x in (0, planes - 1):
            self.full[x] = jnp.zeros(self.full.shape[1:], f32)
            self.high[x] = jnp.zeros(self.full.shape[1:], bf16)
            self.low[x] = jnp.zeros(self.full.shape[1:], bf16)

    def get(self, x):
        return self.full[x + 1]


def field_scratch(planes, lanes):
    shape = (planes + 2, MODES, lanes)
    return [pltpu.VMEM(shape, f32), pltpu.VMEM(shape, bf16), pltpu.VMEM(shape, bf16)]


class Layout:
    def __init__(self, halo, lanes):
        self.halo, self.lanes, self.pitch = halo, lanes, CY + 2 * halo
        self.used = self.pitch * self.pitch
        self.factor = -(-(1 << 16) // self.pitch)

    def place(self, lane):
        y = (lane * self.factor) >> 16
        return y - self.halo, lane - y * self.pitch - self.halo

    def parity(self):
        y, z = self.place(iota((1, self.lanes), 1))
        return (y & 1) * 2 + (z & 1)

    def shifts(self):
        return (self.lanes - self.pitch, self.pitch, self.lanes - 1, 1)

    def field(self, refs):
        return Field(*refs, self.shifts())

    def own_lanes(self, lane):
        y, z = self.place(lane)
        return y, z, (lane < self.used) & (y >= 0) & (y < CY) & (z >= 0) & (z < CZ)


def lanes_for(halo):
    return -(-((CY + 2 * halo) ** 2) // TILE) * TILE


NEAR = 2 * SWEEPS
wide_layout = Layout(HALO, lanes_for(HALO))
near_layout = Layout(NEAR, lanes_for(NEAR))


def near_selector():
    y, z = near_layout.place(iota((1, near_layout.lanes), 1))
    source = (y + HALO) * PITCH + z + HALO
    source = jnp.where(iota((1, near_layout.lanes), 1) < near_layout.used, source, -1)
    return where_equal(iota((LANES, near_layout.lanes), 0), source)


def coupled_rows(centre, field, x):
    moved = []
    for shift, mask in zip(field.shifts, field.masks):
        part = pltpu.roll(centre, shift, 1)
        moved.append(part if mask is None else jnp.where(mask, part, 0.0))
    high, low = split(jnp.concatenate(moved, axis=0))
    high = [field.high[x], field.high[x + 2], high]
    low = [field.low[x], field.low[x + 2], low]
    return jnp.concatenate(high + high + low, axis=0)


def grouped(start, count, size, body):
    groups = -(-count // size)
    least, more = divmod(count, groups)
    at = start
    for length, repeats in ((least + 1, more), (least, groups - more)):
        if repeats == 1:
            body(at, length)
        elif repeats > 1:
            def step(i, carry, at=at, length=length):
                body(at + i * length, length)
                return carry

            lax.fori_loop(0, repeats, step, 0)
        at = at + length * repeats


def group_size(lanes):
    return 5 if lanes > 2 * TILE else 11


def sweep(source, target, start, count, wg, gain, code, store=None):
    def body(first, length):
        values = []
        for x in [first + j for j in range(length)]:
            centre = source.get(x)
            product = dot(wg[...], coupled_rows(centre, source, x))
            values.append((1.0 - relax_weight) * centre + gain[x] - pick(product, code[x], 1))
        for j, value in enumerate(values):
            (store or target.put)(first + j, value)

    grouped(start, count, group_size(source.full.shape[2]), body)


def residual(field, x, source, wa, wd, code):
    centre = field.get(x)
    applied = dot(wa[...], coupled_rows(centre, field, x)) + dot(wd[...], stack3(centre))
    return source - pick(applied, code, 1)


def restrict_plane(wr, residuals, parity):
    out = 0.0
    for p in range(2):
        out = out + pick(dot(wr[p], stack3(residuals[p])), parity, 0)
    return out


def expand_planes(wp, raised_high, raised_low, parity):
    product = dot(wp[...], jnp.concatenate([raised_high, raised_low, raised_high], axis=0))
    return [pick(product[p * 4 * MODES:(p + 1) * 4 * MODES], parity, 0) for p in range(2)]


def gather_mid(place_ref, here, sibling, sizes, put):
    n_gx, n_gy, n_gz = sizes
    per = MX * MY * MZ
    lines = MY * n_gz * MZ
    column = iota((1, n_gz * 2 * per), 1)
    k, rest = column % MZ, column // MZ
    gz, rest = rest % n_gz, rest // n_gz
    j, rest = rest % MY, rest // MY
    i, h = rest % MX, rest // MX
    source = gz * 2 * per + h * per + (i * MY + j) * MZ + k
    selector = where_equal(iota((n_gz * 2 * per, n_gz * 2 * per), 0), source)
    rows = here.shape[2]
    my_x, my_y, my_z = place_ref[0], place_ref[1], place_ref[2]
    parts = []
    for gx in range(n_gx):
        for gy in range(n_gy):
            slot = ((gx ^ my_x) & 1) + 2 * (((gy ^ my_y) >> 1) & 1)
            line = []
            for gz in range(n_gz):
                turn = (my_z + n_gz - gz) % n_gz
                line.append(jnp.where(((gy ^ my_y) & 1) == 0, here[slot, turn], sibling[slot, turn]))
            parts.append(jnp.concatenate(line, axis=1))
    placed = place(jnp.concatenate(parts, axis=0), selector)
    lower = iota((1, TILE), 1) < lines
    for gx in range(n_gx):
        for i in range(MX):
            quarters = []
            for h in range(2):
                tiles = []
                for pair in range(n_gy // 2):
                    block = [placed[(gx * n_gy + 2 * pair + s) * rows:][:rows] for s in range(2)]
                    at = ((h * MX + i) * lines) // TILE * TILE
                    block = [b[:, at:at + TILE] for b in block]
                    if i % 2 == 0:
                        block[1] = pltpu.roll(block[1], lines, 1)
                    else:
                        block[0] = pltpu.roll(block[0], lines, 1)
                    tiles.append(jnp.where(lower, block[0], block[1]))
                quarters.append(jnp.concatenate(tiles, axis=1))
            put(gx * MX + i, quarters)


class Coarse:
    def __init__(self, grid):
        self.x, self.y, self.z = (size // 2 for size in grid)
        self.plane = self.y * self.z
        self.lanes = self.x * self.plane

    def place(self, lane):
        return lane // self.plane, lane // self.z % self.y, lane % self.z

    def solve(self, value, wg, wi, code):
        x, y, z = self.place(iota((1, self.lanes), 1))
        gain = pick(dot(wi[...], stack3(value)), code, 1)
        moves = (
            (self.plane, x > 0), (self.lanes - self.plane, x < self.x - 1),
            (self.lanes - self.z, y < self.y - 1), (self.z, y > 0),
            (self.lanes - 1, z < self.z - 1), (1, z > 0),
        )

        def step(repeat, iterate):
            moved = [jnp.where(mask, pltpu.roll(iterate, shift, 1), 0.0) for shift, mask in moves]
            high, low = split(jnp.concatenate(moved, axis=0))
            product = dot(wg[...], jnp.concatenate([high, high, low], axis=0))
            return (1.0 - relax_weight) * iterate + gain - pick(product, code, 1)

        return lax.fori_loop(0, COARSE_SWEEPS - 1, step, gain)


def solve_mid(source, gain, code, coarse_code, fields, weights, grid):
    wg, wa, wd, wi, wr, wp = weights
    planes, size_y, size_z = grid
    lanes = size_y * size_z
    coarse = Coarse(grid)
    for i in range(2):
        fields(i).clear_ends()

    def begin(first, length):
        values = [pick(dot(wi[...], stack3(source[first + j])), code[first + j], 1) for j in range(length)]
        for j, value in enumerate(values):
            gain[first + j] = value
            fields(0).put(first + j, value)

    grouped(0, planes, 4, begin)
    lane = iota((1, lanes), 1)
    y, z = lane // size_z, lane % size_z
    parity = (y % 2) * 2 + z % 2
    tall, wide = iota((lanes, TILE), 0), iota((lanes, TILE), 1)
    squeeze = (tall // size_z // 2) * coarse.z + tall % size_z // 2
    per_tile = TILE // coarse.plane
    target = (y // 2) * coarse.z + z // 2
    row = iota((coarse.lanes, lanes), 0)

    def correct(field):
        tiles = []
        for tile in range(coarse.lanes // TILE):
            total = 0.0
            for part in range(per_tile):
                x = 2 * (tile * per_tile + part)
                rests = [residual(field, x + p, source[x + p], wa, wd, code[x + p]) for p in range(2)]
                selector = where_equal(squeeze + part * coarse.plane, wide)
                total = total + place(restrict_plane(wr, rests, parity), selector)
            tiles.append(total)
        result = coarse.solve(jnp.concatenate(tiles, axis=1), wg, wi, coarse_code[...])
        parts = jnp.concatenate(split(result), axis=0)
        for pair in range(coarse.x):
            raised = dot(parts, where_equal(row, target + pair * coarse.plane)).astype(bf16)
            for p, value in enumerate(expand_planes(wp, raised[:MODES], raised[MODES:], parity)):
                field.put(2 * pair + p, field.get(2 * pair + p) + value)

    def step(i, carry):
        sweep(fields(i % 2), fields(1 - i % 2), 0, planes, wg, gain, code)

        @pl.when(i == SWEEPS - 2)
        def _():
            correct(fields(1 - i % 2))

        return carry

    lax.fori_loop(0, 2 * SWEEPS - 1, step, 0)
    return fields((2 * SWEEPS - 1) % 2)


def add_mid(place_ref, layout, result, field, depth, wp, grid, old):
    planes, size_y, size_z = grid
    gx, gy, gz = place_ref[0], place_ref[1], place_ref[2]
    lane = iota((1, layout.lanes), 1)
    y, z = layout.place(lane)
    whole_y, whole_z = y + gy * CY, z + gz * CZ
    inside = (lane < layout.used) & (whole_y >= 0) & (whole_y < 2 * size_y) & (whole_z >= 0) & (whole_z < 2 * size_z)
    target = jnp.where(inside, (whole_y >> 1) * size_z + (whole_z >> 1), -1)
    raise_lanes = where_equal(iota((size_y * size_z, layout.lanes), 0), target)
    parity = layout.parity()

    def body(first, length):
        values = []
        for x in [first + j for j in range(length)]:
            parts = jnp.concatenate([result.high[x + 1], result.low[x + 1]], axis=0)
            raised = dot(parts, raise_lanes).astype(bf16)
            for p, value in enumerate(expand_planes(wp, raised[:MODES], raised[MODES:], parity)):
                values.append(old[2 * x + p] + value)
        for j, value in enumerate(values):
            field.put(2 * first + j, value)

    grouped(gx * ((CX - depth) // 2), (CX + depth) // 2, group_size(layout.lanes) // 2, body)


def fine_residual(field, own, source, wr, wa, wd, code):
    layout = near_layout
    tall, wide = iota((layout.lanes, TILE), 0), iota((layout.lanes, TILE), 1)
    y, z, inside = layout.own_lanes(tall)
    target = jnp.where(inside, (y >> 1) * MZ + (z >> 1), -BLOCK)
    per = MX * MY * MZ
    index = wide % per
    parity = layout.parity()
    total = jnp.zeros((MODES, TILE), f32)
    for i in range(MX):
        rests = [residual(field, own + 2 * i + p, source[2 * i + p], wa, wd, code[own + 2 * i + p]) for p in range(2)]
        total = total + place(restrict_plane(wr, rests, parity), where_equal(target + i * MY * MZ, index))
    half = MODES // 2
    return jnp.where(iota((1, TILE), 1) < per, total[:half], total[half:])


def near_kernel(place_ref, own, before, after, low, high, wg, wa, wd, wi, wr, wp, source, payload, *scratch):
    layout = near_layout
    first, second = layout.field(scratch[0:3]), layout.field(scratch[3:6])
    whole, gain, code = scratch[6:9]
    first.clear_ends()
    second.clear_ends()
    gx = place_ref[0]

    def put(x, value, material):
        whole[x], code[x] = value, material

    unpack(layout, own, before, after, low, high, gx * ((CX - SHALLOW) // 2), (CX + SHALLOW) // 2, put, True)

    def begin(start, length):
        values = [pick(dot(wi[...], stack3(whole[start + j])), code[start + j], 1) for j in range(length)]
        for j, value in enumerate(values):
            gain[start + j] = value
            first.put(start + j, value)

    grouped(gx * (CX - SHALLOW), CX + SHALLOW, CX + SHALLOW, begin)
    depth = SHALLOW - 1
    sweep(first, second, gx * (CX - depth), CX + depth, wg, gain, code)
    mine = gx * CX
    source[...] = whole[pl.ds(mine, CX)]
    payload[...] = fine_residual(second, mine, source, wr, wa, wd, code)


def gain_kernel(own, before, after, low, high, wi, payload, gain, code, near_gain, near_code, whole):
    def put(x, value, material):
        whole[x], code[x] = value, material

    unpack(wide_layout, own, before, after, low, high, 0, PAIRS, put, False)
    to_near = near_selector()

    def begin(start, length):
        values = [pick(dot(wi[...], stack3(whole[start + j])), code[start + j], 1) for j in range(length)]
        for j, value in enumerate(values):
            gain[start + j] = value
            near_gain[start + j] = place(value, to_near)
        for j in range(length):
            near_code[start + j] = dot(jnp.broadcast_to(code[start + j], (8, LANES)).astype(bf16), to_near)[:1]

    grouped(0, 2 * CX, 4, begin)


def deep_kernel(place_ref, gain, code, wg, after, solved, *scratch):
    first = wide_layout.field(scratch)
    first.clear_ends()
    for x in range(2 * CX):
        first.put(x, gain[x])
    depth = HALO - 1
    gx = place_ref[0]

    def store(x, value):
        solved[x] = value

    sweep(first, None, gx * (CX - depth), CX + depth, wg, gain, code, store)


def mid_scratch(grid):
    planes, size_y, size_z = grid
    lanes = size_y * size_z
    both = [pltpu.VMEM((2,) + ref.shape, ref.dtype) for ref in field_scratch(planes, lanes)]
    return both + [pltpu.VMEM((planes, MODES, lanes), f32)] * 2


def run_mid(place_ref, here, sibling, sizes, grid, weights, scratch, mid_code, coarse_code, read_codes):
    planes, size_y, size_z = grid
    lanes = size_y * size_z
    lane = iota((1, lanes), 1)
    y, z = lane // size_z, lane % size_z
    shifts = (lanes - size_z, size_z, lanes - 1, 1)
    masks = (y < size_y - 1, y > 0, z < size_z - 1, z > 0)
    source, gain = scratch[3:5]

    def fields(i):
        return Field(*(ref.at[i] for ref in scratch[0:3]), shifts, masks)

    half = MODES // 2
    coarse = Coarse(grid)
    corners = []

    def put(x, quarters):
        source[x, :half] = quarters[0][:half]
        source[x, half:] = quarters[1][:half]
        if read_codes:
            mid_code[x] = quarters[0][half:half + 1]
            if x % 2 == 0:
                corners.append(jnp.broadcast_to(quarters[1][half:half + 1], (8, lanes)).astype(bf16))

    gather_mid(place_ref, here, sibling, sizes, put)
    if read_codes:
        tall, wide = iota((lanes, coarse.lanes), 0), iota((lanes, coarse.lanes), 1)
        x, cy, cz = coarse.place(wide)
        total = 0.0
        for pair in range(coarse.x):
            selector = where_equal(jnp.where(x == pair, 2 * cy * size_z + 2 * cz, -1), tall)
            total = total + dot(corners[pair], selector)
        coarse_code[...] = total[:1]
    return solve_mid(source, gain, mid_code, coarse_code, fields, weights, grid)


def second_kernel(sizes, grid, place_ref, here, sibling, gain, code, solved, near_gain, near_code, source,
                  wg, wa, wd, wi, wr, wp, payload, result, mid_code, coarse_code, *scratch):
    weights = (wg, wa, wd, wi, wr, wp)
    answer = run_mid(place_ref, here, sibling, sizes, grid, weights, scratch[12:], mid_code, coarse_code, True)
    first, second = wide_layout.field(scratch[0:3]), wide_layout.field(scratch[3:6])
    now, other = near_layout.field(scratch[6:9]), near_layout.field(scratch[9:12])
    for field in (first, second, now, other):
        field.clear_ends()
    depth = 3 * SWEEPS
    gx = place_ref[0]
    add_mid(place_ref, wide_layout, answer, first, depth, wp, grid, solved)
    to_near = near_selector()

    def narrow(x, value):
        parts = dot(jnp.concatenate(split(value), axis=0), to_near)
        now.put_parts(x, parts[:MODES], parts[MODES:])

    for repeat in range(2 * SWEEPS):
        depth -= 1
        start, count = gx * (CX - depth), CX + depth
        if depth > NEAR:
            sweep(first, second, start, count, wg, gain, code)
            first, second = second, first
        elif depth == NEAR:
            sweep(first, None, start, count, wg, gain, code, narrow)
        else:
            sweep(now, other, start, count, wg, near_gain, near_code)
            now, other = other, now
    payload[...] = fine_residual(now, gx * CX, source, wr, wa, wd, near_code)
    result[...] = now.full[1:1 + 2 * CX]


def third_kernel(sizes, grid, place_ref, here, sibling, mid_code, coarse_code, near_gain, near_code, solved,
                 wg, wa, wd, wi, wr, wp, result, *scratch):
    weights = (wg, wa, wd, wi, wr, wp)
    answer = run_mid(place_ref, here, sibling, sizes, grid, weights, scratch[6:], mid_code, coarse_code, False)
    layout = near_layout
    now, other = layout.field(scratch[0:3]), layout.field(scratch[3:6])
    now.clear_ends()
    other.clear_ends()
    depth = SWEEPS
    gx = place_ref[0]
    add_mid(place_ref, layout, answer, now, depth, wp, grid, solved)
    for repeat in range(SWEEPS):
        depth -= 1
        sweep(now, other, gx * (CX - depth), CX + depth, wg, near_gain, near_code)
        now, other = other, now
    tall, wide = iota((layout.lanes, TILE), 0), iota((layout.lanes, TILE), 1)
    y, z, inside = layout.own_lanes(tall)
    target = jnp.where(inside, y * CZ + z, -BLOCK)
    selectors = [where_equal(target + odd * CY * CZ, wide) for odd in range(2)]
    for pair in range(CX // 2):
        total = 0.0
        for odd in range(2):
            value = now.get(gx * CX + 2 * pair + odd)
            high, low = split(value)
            lowest = (value - high.astype(f32) - low.astype(f32)).astype(bf16)
            for part in (high, low, lowest):
                total = total + dot(part, selectors[odd])
        result[:, pair * TILE:(pair + 1) * TILE] = total


def call(kernel, cost_us, out_shape, scratch, *args, limit=16):
    vmem, smem = pl.BlockSpec(memory_space=pltpu.VMEM), pl.BlockSpec(memory_space=pltpu.SMEM)
    unused = pl.BlockSpec(memory_space=pl.ANY)
    specs = [unused if isinstance(a, After) else smem if a.dtype == jnp.int32 and a.ndim == 1 else vmem for a in args]
    args = [a.value if isinstance(a, After) else a for a in args]
    cost = pl.CostEstimate(flops=int(cost_us * 1e9), bytes_accessed=int(cost_us * 3e6), transcendentals=0)
    return pl.pallas_call(
        kernel,
        out_shape=out_shape,
        in_specs=specs,
        out_specs=jax.tree.map(lambda s: vmem, out_shape),
        scratch_shapes=scratch,
        cost_estimate=cost,
        compiler_params=pltpu.CompilerParams(vmem_limit_bytes=limit * 1024 * 1024),
    )(*args)


class After:
    def __init__(self, value):
        self.value = value


def shape_of(*dims):
    return jax.ShapeDtypeStruct(dims, f32)


def wide_device(sizes, right_side, diag_blocks, face_blocks, prolong, mats_fine, mats_mid, mats_coarse):
    n_gx, n_gy, n_gz = sizes
    axes = ("gx", "gy", "gz")
    grid = (n_gx * MX, n_gy * MY, n_gz * MZ)
    place_ref = jnp.stack([lax.axis_index(a) for a in axes]).astype(jnp.int32)
    tiles = BLOCK // TILE
    values, kinds = right_side.reshape(MODES, BLOCK), mats_fine.reshape(1, BLOCK)
    swap = [(0, 1), (1, 0)]
    others = lax.ppermute(values, "gx", swap), lax.ppermute(kinds, "gx", swap)
    scaled = invert(diag_blocks)
    own = call(
        prepare_kernel, 0.5, shape_of(2 * tiles, ROWS, TILE), [], place_ref, values, others[0], kinds, others[1]
    )
    up = {a: [(i, i + 1) for i in range(n - 1)] for a, n in zip(axes, sizes)}
    down = {a: [(j, i) for i, j in pairs] for a, pairs in up.items()}
    before, after = lax.ppermute(own, "gy", up["gy"]), lax.ppermute(own, "gy", down["gy"])
    weights = make_weights(scaled, diag_blocks, face_blocks, prolong)
    thin, thick = shape_of(SHALLOW_TILES, ROWS, TILE), shape_of(2 * PAIRS, ROWS, TILE)
    send = call(pack_kernel, 1.5, [thin, thin, thick, thick], [], own, before, after)
    low, high, deep_low, deep_high = (
        lax.ppermute(value, "gz", to["gz"]) for value, to in zip(send, (up, down, up, down))
    )

    wide = field_scratch(2 * CX, LANES)
    near = field_scratch(2 * CX, near_layout.lanes)
    half, per = MODES // 2, MX * MY * MZ
    whole = shape_of(2 * CX, MODES, LANES)
    small = shape_of(2 * CX, MODES, near_layout.lanes)
    small_code = shape_of(2 * CX, 1, near_layout.lanes)
    source, payload = call(
        near_kernel, 7,
        [shape_of(CX, MODES, near_layout.lanes), shape_of(half, TILE)],
        near * 2 + [pltpu.VMEM(s.shape, f32) for s in (small, small, small_code)],
        place_ref, own, before, after, low, high, *weights,
    )
    mid = (mats_mid.reshape(per) + 1).astype(f32)
    coarse = (mats_coarse.reshape(MX // 2, 1, MY // 2, 1, MZ // 2, 1) + 1).astype(f32)
    coarse = jnp.broadcast_to(coarse, (MX // 2, 2, MY // 2, 2, MZ // 2, 2)).reshape(per)
    tail = jnp.broadcast_to(jnp.concatenate([mid, coarse])[None], (8, TILE))

    def along_z(value):
        turns = [[(i, (i + s) % n_gz) for i in range(n_gz)] for s in range(1, n_gz)]
        return jnp.stack([value] + [lax.ppermute(value, "gz", turn) for turn in turns])

    def to_all(column):
        flips = [
            [(i * n_gy + j, (i ^ dx) * n_gy + (j ^ dy)) for i in range(n_gx) for j in range(n_gy)]
            for dx, dy in ((1, 0), (0, 2), (1, 2))
        ]
        here = jnp.stack([column] + [lax.ppermute(column, ("gx", "gy"), flip) for flip in flips])
        return here, lax.ppermute(here, "gy", [(j, j ^ 1) for j in range(n_gy)])

    column = along_z(jnp.concatenate([payload, tail], axis=0))
    gain, code, near_gain, near_code = call(
        gain_kernel, 6,
        [whole, shape_of(2 * CX, 1, LANES), small, small_code],
        [pltpu.VMEM(whole.shape, f32)],
        own, before, after, deep_low, deep_high, weights[3], After(payload),
    )
    solved = call(deep_kernel, 7, whole, wide, place_ref, gain, code, weights[0], After(column))
    planes, lanes = grid[0], grid[1] * grid[2]
    payload, solved, mid_code, coarse_code = call(
        partial(second_kernel, sizes, grid), 37,
        [shape_of(half, TILE), small, shape_of(planes, 1, lanes), shape_of(1, planes * lanes // 8)],
        wide * 2 + near * 2 + mid_scratch(grid),
        place_ref, *to_all(column), gain, code, solved,
        near_gain, near_code, source, *weights, limit=32,
    )
    result = call(
        partial(third_kernel, sizes, grid), 18,
        shape_of(MODES, BLOCK),
        near * 2 + mid_scratch(grid),
        place_ref, *to_all(along_z(payload)), mid_code, coarse_code, near_gain, near_code, solved, *weights,
    )
    return result[None, None, None]


def solution(mesh):
    placed = (
        P("gx", "gy", "gz", None, None),
        P(),
        P(),
        P(),
        P("gx", "gy", "gz", None),
        P("gx", "gy", "gz", None),
        P("gx", "gy", "gz", None),
    )
    sizes = tuple(mesh.shape[a] for a in ("gx", "gy", "gz"))
    wide = sizes[0] == 2 and sizes[1] == 4 and sizes[2] * MY * MZ * 2 == TILE
    return jax.shard_map(
        partial(wide_device, sizes) if wide else per_device,
        mesh=mesh,
        in_specs=placed,
        out_specs=P("gx", "gy", "gz", None, None),
        check_vma=False,
    )
```

```python
from functools import partial

import jax
import jax.numpy as jnp
from jax import lax
from jax.experimental import pallas as pl
from jax.experimental.pallas import tpu as pltpu
from jax.sharding import PartitionSpec as P

MODES = 64
MATERIALS = 4
SWEEPS = 2
COARSE_SWEEPS = 4
CYCLES = 2
CX = 8
CY = 8
CZ = 8


relax_weight = 0.7
restrict_scale = 0.6
highest = lax.Precision.HIGHEST


def padded_2(shard, sides, width):
    for axis, dim in sides:
        size, length = (lax.axis_size(axis), shard.shape[dim])
        up = [(i, (i + 1) % size) for i in range(size - 1)]
        down = [(j, i) for i, j in up]
        last = lax.slice_in_dim(shard, length - width, length, axis=dim)
        first = lax.slice_in_dim(shard, 0, width, axis=dim)
        before = lax.ppermute(last, axis, up)
        after = lax.ppermute(first, axis, down)
        shard = jnp.concatenate([before, shard, after], axis=dim)
    return shard


def inverse_blocks(diag_blocks):
    identity = jnp.eye(MODES, dtype=diag_blocks.dtype)
    result = []
    for material in range(MATERIALS):
        factor = jnp.linalg.cholesky(diag_blocks[material])
        result.append(jax.scipy.linalg.cho_solve((factor, True), identity))
    return jnp.stack(result).reshape(MATERIALS * MODES, MODES)


def coupling_matrix(diag_blocks, face_blocks):
    blocks = jnp.concatenate([diag_blocks[None], face_blocks], axis=0)
    return jnp.transpose(blocks, (1, 2, 0, 3)).reshape(MATERIALS * MODES, 7 * MODES)


def choose_blocks(weights, columns, onehot):
    product = jnp.dot(weights, columns, precision=highest, preferred_element_type=jnp.float32)
    product = product.reshape(MATERIALS, MODES, columns.shape[1])
    return jnp.sum(product * onehot.reshape(MATERIALS, 1, columns.shape[1]), axis=0)


def operate(padded, onehot, coupling):
    centre = padded[:, 1:-1, 1:-1, 1:-1]
    stacked = jnp.concatenate(
        [
            centre,
            padded[:, 2:, 1:-1, 1:-1],
            padded[:, :-2, 1:-1, 1:-1],
            padded[:, 1:-1, 2:, 1:-1],
            padded[:, 1:-1, :-2, 1:-1],
            padded[:, 1:-1, 1:-1, 2:],
            padded[:, 1:-1, 1:-1, :-2],
        ],
        axis=0,
    )
    columns = stacked.reshape(7 * MODES, -1)
    return choose_blocks(coupling, columns, onehot.reshape(MATERIALS, -1)).reshape(centre.shape)


def apply_inverse(inverse, field, onehot):
    return choose_blocks(inverse, field.reshape(MODES, -1), onehot.reshape(MATERIALS, -1)).reshape(
        field.shape
    )


def restrict(field, prolong):
    blocked = field.reshape(
        MODES, field.shape[1] // 2, 2, field.shape[2] // 2, 2, field.shape[3] // 2, 2
    )
    return restrict_scale * jnp.einsum(
        "abcji,jxaybzc->ixyz", prolong.reshape(2, 2, 2, MODES, MODES), blocked, precision=highest
    )


def expand(coarse_field, prolong):
    finer = jnp.einsum(
        "abcji,ixyz->jxaybzc",
        prolong.reshape(2, 2, 2, MODES, MODES),
        coarse_field,
        precision=highest,
    )
    return finer.reshape(
        MODES, 2 * coarse_field.shape[1], 2 * coarse_field.shape[2], 2 * coarse_field.shape[3]
    )


def make_onehot(materials):
    return (materials[None] == jnp.arange(MATERIALS, dtype=jnp.int32)[:, None, None, None]).astype(
        jnp.float32
    )


def fine_border(field):
    return padded_2(field, (("gx", 1), ("gy", 2), ("gz", 3)), 1)


def section_border(field):
    padded = padded_2(field, (("gx", 1), ("gy", 2)), 1)
    return jnp.pad(padded, ((0, 0), (0, 0), (0, 0), (1, 1)))


def smooth(iterate, source, onehot, border, inverse, coupling):
    residual = source - operate(border(iterate), onehot, coupling)
    return iterate + relax_weight * apply_inverse(inverse, residual, onehot)


def coarse_solve(source, onehot, border, inverse, coupling):
    iterate = relax_weight * apply_inverse(inverse, source, onehot)
    for repeat in range(COARSE_SWEEPS - 1):
        iterate = smooth(iterate, source, onehot, border, inverse, coupling)
    return iterate


def middle_cycle(source, onehot, border, inverse, coupling, prolong, coarse_solver):
    iterate = relax_weight * apply_inverse(inverse, source, onehot)
    iterate = smooth(iterate, source, onehot, border, inverse, coupling)
    residual = source - operate(border(iterate), onehot, coupling)
    iterate = iterate + expand(coarse_solver(restrict(residual, prolong)), prolong)
    for repeat in range(SWEEPS):
        iterate = smooth(iterate, source, onehot, border, inverse, coupling)
    return iterate


def single_steps(iterate, actions, source, onehot, inverse, coupling):
    residual = None
    for action in actions:
        if action == "sweep":
            iterate = smooth(iterate, source, onehot, fine_border, inverse, coupling)
        else:
            residual = source - operate(fine_border(iterate), onehot, coupling)
    return (iterate, residual)


def per_device(right_side, diag_blocks, face_blocks, prolong, mats_fine, mats_mid, mats_coarse):
    inverse = inverse_blocks(diag_blocks)
    coupling = coupling_matrix(diag_blocks, face_blocks)
    source = right_side[0, 0, 0].reshape(MODES, CX, CY, CZ)
    onehot_fine = make_onehot(mats_fine[0, 0, 0].reshape(CX, CY, CZ))
    onehot_mid = make_onehot(mats_mid[0, 0, 0].reshape(CX // 2, CY // 2, CZ // 2))
    onehot_coarse = make_onehot(mats_coarse[0, 0, 0].reshape(CX // 4, CY // 4, CZ // 4))
    stepper = partial(
        single_steps, source=source, onehot=onehot_fine, inverse=inverse, coupling=coupling
    )
    iterate = relax_weight * apply_inverse(inverse, source, onehot_fine)
    for cycle_index in range(CYCLES):
        if cycle_index == 0:
            actions = ["sweep"] * (SWEEPS - 1) + ["residual"]
        else:
            actions = ["sweep"] * SWEEPS + ["residual"]
        iterate, residual = stepper(iterate, actions)
        gathered_source = lax.all_gather(restrict(residual, prolong), "gz", axis=3, tiled=True)
        gathered_mid = lax.all_gather(onehot_mid, "gz", axis=3, tiled=True)
        gathered_coarse = lax.all_gather(onehot_coarse, "gz", axis=3, tiled=True)
        local_solver = partial(
            coarse_solve,
            onehot=gathered_coarse,
            border=section_border,
            inverse=inverse,
            coupling=coupling,
        )
        section_field = middle_cycle(
            gathered_source, gathered_mid, section_border, inverse, coupling, prolong, local_solver
        )
        iterate = iterate + expand(
            lax.dynamic_slice_in_dim(section_field, lax.axis_index("gz") * (CZ // 2), CZ // 2, 3),
            prolong,
        )
        iterate, unused_residual = stepper(iterate, ["sweep"] * SWEEPS)
    return iterate.reshape(MODES, CX * CY * CZ)[None, None, None]


HALO = 3 * SWEEPS + SWEEPS - 1
PITCH = CY + 2 * HALO
BLOCK = CX * CY * CZ
TILE = 128
LANES = -(-(PITCH * PITCH) // TILE) * TILE
ROWS = MODES + 8
MX, MY, MZ = CX // 2, CY // 2, CZ // 2
f32 = jnp.float32
bf16 = jnp.bfloat16


def split(value):
    high = value.astype(bf16)
    return high, (value - high.astype(f32)).astype(bf16)


def dot(a, b):
    return jnp.dot(a, b, preferred_element_type=f32)


def iota(shape, dim):
    return lax.broadcasted_iota(jnp.int32, shape, dim)


def where_equal(rows, columns):
    return jnp.where(rows == columns, 1.0, 0.0).astype(bf16)


def place(value, selector):
    high, low = split(value)
    return dot(high, selector) + dot(low, selector)


def pick(product, code, first):
    out = jnp.zeros((MODES, product.shape[1]), f32)
    for m in range(MATERIALS):
        out = jnp.where(code == m + first, product[m * MODES:(m + 1) * MODES], out)
    return out


def stack3(value):
    high, low = split(value)
    return jnp.concatenate([high, low, high], axis=0)


def thirds(value):
    high, low = split(value)
    return jnp.concatenate([high, high, low], axis=1)


def inverse_kernel(diag, scaled):
    a = diag[...]
    row_id = iota((1, MODES, 1), 1)
    lane_id = iota((1, 1, MODES), 2)
    for k in range(MODES):
        pivot = 1.0 / a[:, k:k + 1, k:k + 1]
        on_row, on_lane = row_id == k, lane_id == k
        row = jnp.where(on_lane, pivot, a[:, k:k + 1, :] * pivot)
        column = a[:, :, k:k + 1]
        a = jnp.where(on_row, row, jnp.where(on_lane, 0.0, a) - column * row)
    scaled[...] = relax_weight * a


def weights_kernel(scaled, diag, face, prolong, wg, wa, wd, wi, wr, wp):
    beside, gains = [], []
    for m in range(MATERIALS):
        faces = jnp.concatenate([face[d, m] for d in (1, 0, 2, 3, 4, 5)], axis=1)
        beside.append(faces)
        gains.append(jnp.dot(scaled[m], faces, precision=highest, preferred_element_type=f32))
    for target, blocks in ((wa, beside), (wg, gains)):
        high, low = split(jnp.concatenate(blocks, axis=0))
        target[...] = jnp.concatenate([high, low, high], axis=1)
    wd[...] = thirds(jnp.concatenate([diag[m] for m in range(MATERIALS)], axis=0))
    wi[...] = thirds(jnp.concatenate([scaled[m] for m in range(MATERIALS)], axis=0))
    for p in range(2):
        wr[p] = thirds(jnp.concatenate([restrict_scale * prolong[p * 4 + c].T for c in range(4)], axis=0))
    wp[...] = thirds(jnp.concatenate([prolong[c] for c in range(8)], axis=0))


def invert(diag_blocks):
    return call(inverse_kernel, 6, shape_of(*diag_blocks.shape), [], diag_blocks)


def make_weights(scaled, diag_blocks, face_blocks, prolong):
    rows = MATERIALS * MODES
    shapes = [(rows, 18 * MODES)] * 2 + [(rows, 3 * MODES)] * 2
    shapes += [(2, 4 * MODES, 3 * MODES), (8 * MODES, 3 * MODES)]
    shapes = [jax.ShapeDtypeStruct(shape, bf16) for shape in shapes]
    return call(weights_kernel, 1, shapes, [], scaled, diag_blocks, face_blocks, prolong)


SHALLOW = SWEEPS
PAIRS = CX
SLOT = CY * CZ


def layer_rows(depth, halo):
    return CY + 2 * (halo - depth)


SHALLOW_LANES = sum(layer_rows(d, SHALLOW) for d in range(1, SHALLOW + 1))
DEEP_LANES = sum(layer_rows(d, HALO) for d in range(1, HALO + 1))
PER_TILE = TILE // (2 * SHALLOW_LANES)
SHALLOW_TILES = -(-PAIRS // PER_TILE)


def layer_of(index, first, last, halo):
    depth, start, at = jnp.full_like(index, first), jnp.zeros_like(index), 0
    for d in range(first + 1, last + 1):
        at += layer_rows(d - 1, halo)
        inside = index >= at
        depth, start = jnp.where(inside, d, depth), jnp.where(inside, at, start)
    return depth, index - start - (halo - depth)


def lane_of(depth, y, first, last, halo):
    start, at = jnp.zeros_like(depth), 0
    for d in range(first + 1, last + 1):
        at += layer_rows(d - 1, halo)
        start = jnp.where(depth == d, at, start)
    inside = (depth >= first) & (depth <= last) & (y >= depth - halo) & (y < CY + halo - depth)
    return jnp.where(inside, start + y + halo - depth, -(1 << 20))


def prepare_kernel(place_ref, values, other, materials, other_materials, out):
    mine = place_ref[0]
    for half, (block, kinds) in enumerate(((values, materials), (other, other_materials))):
        first = (mine ^ half) * (BLOCK // TILE)
        codes = jnp.broadcast_to((kinds[...] + 1).astype(f32), (ROWS - MODES, BLOCK))
        for tile in range(BLOCK // TILE):
            lanes = slice(tile * TILE, (tile + 1) * TILE)
            out[first + tile, :MODES] = block[:, lanes]
            out[first + tile, MODES:] = codes[:, lanes]


def swap_tile(y, odd):
    place = (y + CY) // CY
    return jnp.where(place == 1, 1, jnp.where(place // 2 == odd, 2, 0))


def pack_kernel(place_ref, own, first, second, thin_first, thin_second, thick_first, thick_second):
    column = iota((1, 4 * TILE), 1)
    lane, kind = column % TILE, column // TILE
    row = iota((3 * TILE, 4 * TILE), 0)
    odd_y, odd_z = place_ref[1] & 1, place_ref[2] & 1
    parts = [jnp.concatenate([r[pair] for r in (first, own, second)], axis=1) for pair in range(PAIRS)]
    parts = split(jnp.concatenate(parts, axis=0))
    shallow = 0.0
    for odd in range(2):
        thin = lane - odd * SHALLOW_LANES
        thin_depth, thin_y = layer_of(thin, 1, SHALLOW, SHALLOW)
        thick_depth, thick_y = layer_of(lane, 1, HALO, HALO)
        depth = jnp.where(kind < 2, thin_depth, thick_depth)
        y = jnp.where(kind < 2, thin_y, thick_y)
        valid = jnp.where(
            kind < 2,
            jnp.where((thin >= 0) & (thin < SHALLOW_LANES), 1, 0),
            jnp.where(lane < DEEP_LANES, 1, 0),
        )
        z = jnp.where(kind % 2 == odd_z, CZ - depth, depth - 1)
        source = swap_tile(y, odd_y) * TILE + ((y + CY) % CY) * CZ + z + odd * SLOT
        selector = where_equal(row, jnp.where(valid == 1, source, -1))
        packed = dot(parts[0], selector) + dot(parts[1], selector)
        shallow = shallow + packed[:, :2 * TILE]
        for pair in range(PAIRS):
            rows = packed[pair * ROWS:(pair + 1) * ROWS]
            thick_first[2 * pair + odd], thick_second[2 * pair + odd] = rows[:, 2 * TILE:3 * TILE], rows[:, 3 * TILE:]
    for tile in range(SHALLOW_TILES):
        for kind, out in enumerate((thin_first, thin_second)):
            strip = 0.0
            for slot in range(PER_TILE):
                pair = tile * PER_TILE + slot
                if pair < PAIRS:
                    piece = shallow[pair * ROWS:(pair + 1) * ROWS, kind * TILE:(kind + 1) * TILE]
                    strip = strip + (pltpu.roll(piece, slot * 2 * SHALLOW_LANES, 1) if slot else piece)
            out[tile] = strip


def shallow_strip(first, second, pair):
    tile, slot = pair // PER_TILE, pair % PER_TILE
    shift = (TILE - slot * 2 * SHALLOW_LANES) % TILE
    lane = iota((1, TILE), 1)
    return jnp.where(
        lane < TILE // 2,
        pltpu.roll(first[tile], shift, 1),
        pltpu.roll(second[tile], (shift + TILE // 2) % TILE, 1),
    )


def in_grid(place_ref, sizes, y, z):
    whole_y, whole_z = y + place_ref[1] * CY, z + place_ref[2] * CZ
    return (whole_y >= 0) & (whole_y < sizes[1] * CY) & (whole_z >= 0) & (whole_z < sizes[2] * CZ)


def unpack(layout, sizes, place_ref, own, along_y, along_z, start, pairs, put, shallow):
    lane = iota((1, layout.lanes), 1)
    y, z = layout.place(lane)
    odd_y, odd_z = place_ref[1] & 1, place_ref[2] & 1
    inner = swap_tile(y, odd_y) * TILE + ((y + CY) % CY) * CZ + z
    depth = jnp.where(z < 0, -z, z - (CZ - 1))
    middle = (z >= 0) & (z < CZ)
    strip = jnp.where(jnp.where(z < 0, 0, 1) == odd_z, 1, 0)
    if shallow:
        outer = lane_of(depth, y, 1, SHALLOW, SHALLOW) + 3 * TILE + strip * (TILE // 2)
        step = SHALLOW_LANES
    else:
        outer = lane_of(depth, y, 1, HALO, HALO) + (3 + strip) * TILE
        step = 0
    row = iota(((4 if shallow else 5) * TILE, layout.lanes), 0)
    valid = (lane < layout.used) & in_grid(place_ref, sizes, y, z)
    parts = []
    for odd in range(2):
        if odd == 0 or not shallow:
            parts = []
            for i in range(pairs):
                pair = start + i
                line = [r[pair] for r in (along_y[0], own, along_y[1])]
                line += [shallow_strip(*along_z, pair)] if shallow else [r[2 * pair + odd] for r in along_z]
                parts.append(jnp.concatenate(line, axis=1))
            parts = split(jnp.concatenate(parts, axis=0))
        source = jnp.where(middle, inner + odd * SLOT, outer + odd * step)
        selector = where_equal(row, jnp.where(valid, source, -1))
        placed = dot(parts[0], selector) + dot(parts[1], selector)
        for i in range(pairs):
            rows = placed[i * ROWS:(i + 1) * ROWS]
            put(2 * (start + i) + odd, rows[:MODES], rows[MODES:MODES + 1])


class Field:
    def __init__(self, full, high, low, shifts, masks=(None,) * 4):
        self.full, self.high, self.low = full, high, low
        self.shifts, self.masks = shifts, masks

    def put(self, x, value):
        self.full[x + 1] = value
        self.high[x + 1], self.low[x + 1] = split(value)

    def put_parts(self, x, high, low):
        self.full[x + 1] = high + low
        self.high[x + 1], self.low[x + 1] = high.astype(bf16), low.astype(bf16)

    def clear_ends(self):
        planes = self.full.shape[0]
        for x in (0, planes - 1):
            self.full[x] = jnp.zeros(self.full.shape[1:], f32)
            self.high[x] = jnp.zeros(self.full.shape[1:], bf16)
            self.low[x] = jnp.zeros(self.full.shape[1:], bf16)

    def get(self, x):
        return self.full[x + 1]


def field_scratch(planes, lanes):
    shape = (planes + 2, MODES, lanes)
    return [pltpu.VMEM(shape, f32), pltpu.VMEM(shape, bf16), pltpu.VMEM(shape, bf16)]


class Layout:
    def __init__(self, halo, lanes):
        self.halo, self.lanes, self.pitch = halo, lanes, CY + 2 * halo
        self.used = self.pitch * self.pitch
        self.factor = -(-(1 << 16) // self.pitch)

    def place(self, lane):
        y = (lane * self.factor) >> 16
        return y - self.halo, lane - y * self.pitch - self.halo

    def parity(self):
        y, z = self.place(iota((1, self.lanes), 1))
        return (y & 1) * 2 + (z & 1)

    def shifts(self):
        return (self.lanes - self.pitch, self.pitch, self.lanes - 1, 1)

    def field(self, refs):
        return Field(*refs, self.shifts())

    def own_lanes(self, lane):
        y, z = self.place(lane)
        return y, z, (lane < self.used) & (y >= 0) & (y < CY) & (z >= 0) & (z < CZ)


def lanes_for(halo):
    return -(-((CY + 2 * halo) ** 2) // TILE) * TILE


NEAR = 2 * SWEEPS
wide_layout = Layout(HALO, lanes_for(HALO))
near_layout = Layout(NEAR, lanes_for(NEAR))


def near_selector():
    y, z = near_layout.place(iota((1, near_layout.lanes), 1))
    source = (y + HALO) * PITCH + z + HALO
    source = jnp.where(iota((1, near_layout.lanes), 1) < near_layout.used, source, -1)
    return where_equal(iota((LANES, near_layout.lanes), 0), source)


def coupled_rows(centre, field, x):
    moved = []
    for shift, mask in zip(field.shifts, field.masks):
        part = pltpu.roll(centre, shift, 1)
        moved.append(part if mask is None else jnp.where(mask, part, 0.0))
    high, low = split(jnp.concatenate(moved, axis=0))
    high = [field.high[x], field.high[x + 2], high]
    low = [field.low[x], field.low[x + 2], low]
    return jnp.concatenate(high + high + low, axis=0)


def grouped(start, count, size, body):
    groups = -(-count // size)
    length = -(-count // groups)
    if groups == 1:
        body(start, count)
        return

    def step(i, carry):
        body(start + jnp.minimum(i * length, count - length), length)
        return carry

    lax.fori_loop(0, groups, step, 0)


def group_size(lanes):
    return 7 if lanes > 2 * TILE else 6


def sweep(source, target, start, count, wg, gain, code, store=None, size=None):
    def body(first, length):
        values = []
        for x in [first + j for j in range(length)]:
            centre = source.get(x)
            product = dot(wg[...], coupled_rows(centre, source, x))
            values.append((1.0 - relax_weight) * centre + gain[x] - pick(product, code[x], 1))
        for j, value in enumerate(values):
            (store or target.put)(first + j, value)

    grouped(start, count, size or group_size(source.full.shape[2]), body)


def residual(field, x, source, wa, wd, code):
    centre = field.get(x)
    applied = dot(wa[...], coupled_rows(centre, field, x)) + dot(wd[...], stack3(centre))
    return source - pick(applied, code, 1)


def restrict_plane(wr, residuals, parity):
    out = 0.0
    for p in range(2):
        out = out + pick(dot(wr[p], stack3(residuals[p])), parity, 0)
    return out


def expand_planes(wp, raised_high, raised_low, parity):
    product = dot(wp[...], jnp.concatenate([raised_high, raised_low, raised_high], axis=0))
    return [pick(product[p * 4 * MODES:(p + 1) * 4 * MODES], parity, 0) for p in range(2)]


def gather_mid(place_ref, here, sibling, sizes, put):
    n_gx, n_gy, n_gz = sizes
    per = MX * MY * MZ
    lines = MY * n_gz * MZ
    column = iota((1, n_gz * 2 * per), 1)
    k, rest = column % MZ, column // MZ
    gz, rest = rest % n_gz, rest // n_gz
    j, rest = rest % MY, rest // MY
    i, h = rest % MX, rest // MX
    source = gz * 2 * per + h * per + (i * MY + j) * MZ + k
    selector = where_equal(iota((n_gz * 2 * per, n_gz * 2 * per), 0), source)
    rows = here.shape[2]
    my_x, my_y, my_z = place_ref[0], place_ref[1], place_ref[2]
    parts = []
    for gx in range(n_gx):
        for gy in range(n_gy):
            slot = ((gx ^ my_x) & 1) + 2 * (((gy ^ my_y) >> 1) & 1)
            line = []
            for gz in range(n_gz):
                turn = my_z ^ gz
                line.append(jnp.where(((gy ^ my_y) & 1) == 0, here[slot, turn], sibling[slot, turn]))
            parts.append(jnp.concatenate(line, axis=1))
    placed = place(jnp.concatenate(parts, axis=0), selector)
    lower = iota((1, TILE), 1) < lines
    for gx in range(n_gx):
        for i in range(MX):
            quarters = []
            for h in range(2):
                tiles = []
                for pair in range(n_gy // 2):
                    block = [placed[(gx * n_gy + 2 * pair + s) * rows:][:rows] for s in range(2)]
                    at = ((h * MX + i) * lines) // TILE * TILE
                    block = [b[:, at:at + TILE] for b in block]
                    if i % 2 == 0:
                        block[1] = pltpu.roll(block[1], lines, 1)
                    else:
                        block[0] = pltpu.roll(block[0], lines, 1)
                    tiles.append(jnp.where(lower, block[0], block[1]))
                quarters.append(jnp.concatenate(tiles, axis=1))
            put(gx * MX + i, quarters)


class Coarse:
    def __init__(self, grid):
        self.x, self.y, self.z = (size // 2 for size in grid)
        self.plane = self.y * self.z
        self.lanes = self.x * self.plane

    def place(self, lane):
        return lane // self.plane, lane // self.z % self.y, lane % self.z

    def solve(self, value, wg, wi, code):
        x, y, z = self.place(iota((1, self.lanes), 1))
        gain = pick(dot(wi[...], stack3(value)), code, 1)
        moves = (
            (self.plane, x > 0), (self.lanes - self.plane, x < self.x - 1),
            (self.lanes - self.z, y < self.y - 1), (self.z, y > 0),
            (self.lanes - 1, z < self.z - 1), (1, z > 0),
        )

        def step(repeat, iterate):
            moved = [jnp.where(mask, pltpu.roll(iterate, shift, 1), 0.0) for shift, mask in moves]
            high, low = split(jnp.concatenate(moved, axis=0))
            product = dot(wg[...], jnp.concatenate([high, high, low], axis=0))
            return (1.0 - relax_weight) * iterate + gain - pick(product, code, 1)

        return lax.fori_loop(0, COARSE_SWEEPS - 1, step, gain)


def solve_mid(source, gain, code, coarse_source, coarse_code, fields, weights, grid):
    wg, wa, wd, wi, wr, wp = weights
    planes, size_y, size_z = grid
    lanes = size_y * size_z
    coarse = Coarse(grid)
    for i in range(2):
        fields(i).clear_ends()

    def begin(first, length):
        values = [pick(dot(wi[...], stack3(source[first + j])), code[first + j], 1) for j in range(length)]
        for j, value in enumerate(values):
            gain[first + j] = value
            fields(0).put(first + j, value)

    grouped(0, planes, 4, begin)
    lane = iota((1, lanes), 1)
    y, z = lane // size_z, lane % size_z
    parity = (y % 2) * 2 + z % 2
    tall, wide = iota((lanes, TILE), 0), iota((lanes, TILE), 1)
    squeeze = (tall // size_z // 2) * coarse.z + tall % size_z // 2
    per_tile = TILE // coarse.plane
    target = (y // 2) * coarse.z + z // 2
    row = iota((coarse.lanes, lanes), 0)

    def correct(field):
        def down(tile, carry):
            total = 0.0
            for part in range(per_tile):
                x = 2 * (tile * per_tile + part)
                rests = [residual(field, x + p, source[x + p], wa, wd, code[x + p]) for p in range(2)]
                selector = where_equal(squeeze + part * coarse.plane, wide)
                total = total + place(restrict_plane(wr, rests, parity), selector)
            coarse_source[:, pl.ds(pl.multiple_of(tile * TILE, TILE), TILE)] = total
            return carry

        lax.fori_loop(0, coarse.lanes // TILE, down, 0)
        result = coarse.solve(coarse_source[...], wg, wi, coarse_code[...])
        parts = jnp.concatenate(split(result), axis=0)

        def up(step, carry):
            for pair in (2 * step, 2 * step + 1):
                raised = dot(parts, where_equal(row, target + pair * coarse.plane)).astype(bf16)
                for p, value in enumerate(expand_planes(wp, raised[:MODES], raised[MODES:], parity)):
                    field.put(2 * pair + p, field.get(2 * pair + p) + value)
            return carry

        lax.fori_loop(0, coarse.x // 2, up, 0)

    def step(i, carry):
        sweep(fields(i % 2), fields(1 - i % 2), 0, planes, wg, gain, code, size=planes)

        @pl.when(i == SWEEPS - 2)
        def _():
            correct(fields(1 - i % 2))

        return carry

    lax.fori_loop(0, 2 * SWEEPS - 1, step, 0)
    return fields((2 * SWEEPS - 1) % 2)


def add_mid(place_ref, layout, result, field, depth, wp, grid, old):
    planes, size_y, size_z = grid
    gx, gy, gz = place_ref[0], place_ref[1], place_ref[2]
    lane = iota((1, layout.lanes), 1)
    y, z = layout.place(lane)
    whole_y, whole_z = y + gy * CY, z + gz * CZ
    inside = (lane < layout.used) & (whole_y >= 0) & (whole_y < 2 * size_y) & (whole_z >= 0) & (whole_z < 2 * size_z)
    target = jnp.where(inside, (whole_y >> 1) * size_z + (whole_z >> 1), -1)
    raise_lanes = where_equal(iota((size_y * size_z, layout.lanes), 0), target)
    parity = layout.parity()

    def body(first, length):
        values = []
        for x in [first + j for j in range(length)]:
            parts = jnp.concatenate([result.high[x + 1], result.low[x + 1]], axis=0)
            raised = dot(parts, raise_lanes).astype(bf16)
            for p, value in enumerate(expand_planes(wp, raised[:MODES], raised[MODES:], parity)):
                values.append(old[2 * x + p] + value)
        for j, value in enumerate(values):
            field.put(2 * first + j, value)

    grouped(gx * ((CX - depth) // 2), (CX + depth) // 2, max(group_size(layout.lanes) // 3, 1), body)


def fine_residual(field, own, source, wr, wa, wd, code):
    layout = near_layout
    tall, wide = iota((layout.lanes, TILE), 0), iota((layout.lanes, TILE), 1)
    y, z, inside = layout.own_lanes(tall)
    target = jnp.where(inside, (y >> 1) * MZ + (z >> 1), -BLOCK)
    per = MX * MY * MZ
    index = wide % per
    parity = layout.parity()
    def add(step, total):
        for i in (2 * step, 2 * step + 1):
            x = own + 2 * i
            rests = [residual(field, x + p, source[2 * i + p], wa, wd, code[x + p]) for p in range(2)]
            total = total + place(restrict_plane(wr, rests, parity), where_equal(target + i * MY * MZ, index))
        return total

    total = lax.fori_loop(0, MX // 2, add, jnp.zeros((MODES, TILE), f32))
    half = MODES // 2
    return jnp.where(iota((1, TILE), 1) < per, total[:half], total[half:])


def near_kernel(sizes, place_ref, own, y0, y1, z0, z1, wg, wa, wd, wi, wr, wp, source, payload, *scratch):
    layout = near_layout
    first, second = layout.field(scratch[0:3]), layout.field(scratch[3:6])
    whole, gain, code = scratch[6:9]
    first.clear_ends()
    second.clear_ends()
    gx = place_ref[0]

    def put(x, value, material):
        whole[x], code[x] = value, material

    start, pairs = gx * ((CX - SHALLOW) // 2), (CX + SHALLOW) // 2
    unpack(layout, sizes, place_ref, own, (y0, y1), (z0, z1), start, pairs, put, True)

    def begin(start, length):
        values = [pick(dot(wi[...], stack3(whole[start + j])), code[start + j], 1) for j in range(length)]
        for j, value in enumerate(values):
            gain[start + j] = value
            first.put(start + j, value)

    grouped(gx * (CX - SHALLOW), CX + SHALLOW, group_size(layout.lanes), begin)
    depth = SHALLOW - 1
    sweep(first, second, gx * (CX - depth), CX + depth, wg, gain, code)
    mine = gx * CX
    source[...] = whole[pl.ds(mine, CX)]
    payload[...] = fine_residual(second, mine, source, wr, wa, wd, code)


def gain_kernel(sizes, place_ref, own, y0, y1, z0, z1, wi, payload, gain, code, near_gain, near_code, whole):
    def put(x, value, material):
        whole[x], code[x] = value, material

    unpack(wide_layout, sizes, place_ref, own, (y0, y1), (z0, z1), 0, PAIRS, put, False)
    to_near = near_selector()

    def begin(start, length):
        values = [pick(dot(wi[...], stack3(whole[start + j])), code[start + j], 1) for j in range(length)]
        for j, value in enumerate(values):
            gain[start + j] = value
            near_gain[start + j] = place(value, to_near)
        for j in range(length):
            near_code[start + j] = dot(jnp.broadcast_to(code[start + j], (8, LANES)).astype(bf16), to_near)[:1]

    grouped(0, 2 * CX, 4, begin)


def deep_kernel(place_ref, gain, code, wg, after, solved, *scratch):
    first = wide_layout.field(scratch)
    first.clear_ends()
    for x in range(2 * CX):
        first.put(x, gain[x])
    depth = HALO - 1
    gx = place_ref[0]

    def store(x, value):
        solved[x] = value

    sweep(first, None, gx * (CX - depth), CX + depth, wg, gain, code, store)


def mid_scratch(grid):
    planes, size_y, size_z = grid
    lanes = size_y * size_z
    both = [pltpu.VMEM((2,) + ref.shape, ref.dtype) for ref in field_scratch(planes, lanes)]
    return both + [pltpu.VMEM((planes, MODES, lanes), f32)] * 2 + [pltpu.VMEM((MODES, planes * lanes // 8), f32)]


def run_mid(place_ref, here, sibling, sizes, grid, weights, scratch, mid_code, coarse_code, read_codes):
    planes, size_y, size_z = grid
    lanes = size_y * size_z
    lane = iota((1, lanes), 1)
    y, z = lane // size_z, lane % size_z
    shifts = (lanes - size_z, size_z, lanes - 1, 1)
    masks = (y < size_y - 1, y > 0, z < size_z - 1, z > 0)
    source, gain, coarse_source = scratch[3:6]

    def fields(i):
        return Field(*(ref.at[i] for ref in scratch[0:3]), shifts, masks)

    half = MODES // 2
    coarse = Coarse(grid)
    corners = []

    def put(x, quarters):
        source[x, :half] = quarters[0][:half]
        source[x, half:] = quarters[1][:half]
        if read_codes:
            mid_code[x] = quarters[0][half:half + 1]
            if x % 2 == 0:
                corners.append(jnp.broadcast_to(quarters[1][half:half + 1], (8, lanes)).astype(bf16))

    gather_mid(place_ref, here, sibling, sizes, put)
    if read_codes:
        tall, wide = iota((lanes, coarse.lanes), 0), iota((lanes, coarse.lanes), 1)
        x, cy, cz = coarse.place(wide)
        total = 0.0
        for pair in range(coarse.x):
            selector = where_equal(jnp.where(x == pair, 2 * cy * size_z + 2 * cz, -1), tall)
            total = total + dot(corners[pair], selector)
        coarse_code[...] = total[:1]
    return solve_mid(source, gain, mid_code, coarse_source, coarse_code, fields, weights, grid)


def second_kernel(sizes, grid, place_ref, here, sibling, gain, code, solved, near_gain, near_code, source,
                  wg, wa, wd, wi, wr, wp, payload, result, mid_code, coarse_code, *scratch):
    weights = (wg, wa, wd, wi, wr, wp)
    answer = run_mid(place_ref, here, sibling, sizes, grid, weights, scratch[12:], mid_code, coarse_code, True)
    first, second = wide_layout.field(scratch[0:3]), wide_layout.field(scratch[3:6])
    now, other = near_layout.field(scratch[6:9]), near_layout.field(scratch[9:12])
    for field in (first, second, now, other):
        field.clear_ends()
    depth = 3 * SWEEPS
    gx = place_ref[0]
    add_mid(place_ref, wide_layout, answer, first, depth, wp, grid, solved)
    to_near = near_selector()

    def narrow(x, value):
        parts = dot(jnp.concatenate(split(value), axis=0), to_near)
        now.put_parts(x, parts[:MODES], parts[MODES:])

    for repeat in range(2 * SWEEPS):
        depth -= 1
        start, count = gx * (CX - depth), CX + depth
        if depth > NEAR:
            sweep(first, second, start, count, wg, gain, code)
            first, second = second, first
        elif depth == NEAR:
            sweep(first, None, start, count, wg, gain, code, narrow)
        else:
            sweep(now, other, start, count, wg, near_gain, near_code)
            now, other = other, now
    payload[...] = fine_residual(now, gx * CX, source, wr, wa, wd, near_code)
    result[...] = now.full[1:1 + 2 * CX]


def third_kernel(sizes, grid, place_ref, here, sibling, mid_code, coarse_code, near_gain, near_code, solved,
                 wg, wa, wd, wi, wr, wp, result, *scratch):
    weights = (wg, wa, wd, wi, wr, wp)
    answer = run_mid(place_ref, here, sibling, sizes, grid, weights, scratch[6:], mid_code, coarse_code, False)
    layout = near_layout
    now, other = layout.field(scratch[0:3]), layout.field(scratch[3:6])
    now.clear_ends()
    other.clear_ends()
    depth = SWEEPS
    gx = place_ref[0]
    add_mid(place_ref, layout, answer, now, depth, wp, grid, solved)
    for repeat in range(SWEEPS):
        depth -= 1
        sweep(now, other, gx * (CX - depth), CX + depth, wg, near_gain, near_code)
        now, other = other, now
    tall, wide = iota((layout.lanes, TILE), 0), iota((layout.lanes, TILE), 1)
    y, z, inside = layout.own_lanes(tall)
    target = jnp.where(inside, y * CZ + z, -BLOCK)
    selectors = [where_equal(target + odd * CY * CZ, wide) for odd in range(2)]
    for pair in range(CX // 2):
        total = 0.0
        for odd in range(2):
            value = now.get(gx * CX + 2 * pair + odd)
            high, low = split(value)
            lowest = (value - high.astype(f32) - low.astype(f32)).astype(bf16)
            for part in (high, low, lowest):
                total = total + dot(part, selectors[odd])
        result[:, pair * TILE:(pair + 1) * TILE] = total


def call(kernel, cost_us, out_shape, scratch, *args, limit=16):
    vmem, smem = pl.BlockSpec(memory_space=pltpu.VMEM), pl.BlockSpec(memory_space=pltpu.SMEM)
    unused = pl.BlockSpec(memory_space=pl.ANY)
    specs = [unused if isinstance(a, After) else smem if a.dtype == jnp.int32 and a.ndim == 1 else vmem for a in args]
    args = [a.value if isinstance(a, After) else a for a in args]
    cost = pl.CostEstimate(flops=int(cost_us * 1e9), bytes_accessed=int(cost_us * 3e6), transcendentals=0)
    return pl.pallas_call(
        kernel,
        out_shape=out_shape,
        in_specs=specs,
        out_specs=jax.tree.map(lambda s: vmem, out_shape),
        scratch_shapes=scratch,
        cost_estimate=cost,
        compiler_params=pltpu.CompilerParams(vmem_limit_bytes=limit * 1024 * 1024),
    )(*args)


class After:
    def __init__(self, value):
        self.value = value


def shape_of(*dims):
    return jax.ShapeDtypeStruct(dims, f32)


def wide_device(sizes, right_side, diag_blocks, face_blocks, prolong, mats_fine, mats_mid, mats_coarse):
    n_gx, n_gy, n_gz = sizes
    axes = ("gx", "gy", "gz")
    grid = (n_gx * MX, n_gy * MY, n_gz * MZ)
    place_ref = jnp.stack([lax.axis_index(a) for a in axes]).astype(jnp.int32)
    tiles = BLOCK // TILE
    values, kinds = right_side.reshape(MODES, BLOCK), mats_fine.reshape(1, BLOCK)
    swap = [(0, 1), (1, 0)]
    others = lax.ppermute(values, "gx", swap), lax.ppermute(kinds, "gx", swap)
    scaled = invert(diag_blocks)
    own = call(
        prepare_kernel, 0.5, shape_of(2 * tiles, ROWS, TILE), [], place_ref, values, others[0], kinds, others[1]
    )
    swaps = {}
    for axis, n in zip(axes, sizes):
        inner = [pair for i in range(1, n - 1, 2) for pair in ((i, i + 1), (i + 1, i))]
        swaps[axis] = [(i, i ^ 1) for i in range(n)], [(0, 0)] + inner + [(n - 1, n - 1)]
    along_y = [lax.ppermute(own, "gy", swap) for swap in swaps["gy"]]
    weights = make_weights(scaled, diag_blocks, face_blocks, prolong)
    thin, thick = shape_of(SHALLOW_TILES, ROWS, TILE), shape_of(2 * PAIRS, ROWS, TILE)
    send = call(pack_kernel, 1.5, [thin, thin, thick, thick], [], place_ref, own, *along_y)
    shallow = [lax.ppermute(value, "gz", swap) for value, swap in zip(send[:2], swaps["gz"])]
    deep = [lax.ppermute(value, "gz", swap) for value, swap in zip(send[2:], swaps["gz"])]

    wide = field_scratch(2 * CX, LANES)
    near = field_scratch(2 * CX, near_layout.lanes)
    half, per = MODES // 2, MX * MY * MZ
    whole = shape_of(2 * CX, MODES, LANES)
    small = shape_of(2 * CX, MODES, near_layout.lanes)
    small_code = shape_of(2 * CX, 1, near_layout.lanes)
    source, payload = call(
        partial(near_kernel, sizes), 7,
        [shape_of(CX, MODES, near_layout.lanes), shape_of(half, TILE)],
        near * 2 + [pltpu.VMEM(s.shape, f32) for s in (small, small, small_code)],
        place_ref, own, *along_y, *shallow, *weights,
    )
    mid = (mats_mid.reshape(per) + 1).astype(f32)
    coarse = (mats_coarse.reshape(MX // 2, 1, MY // 2, 1, MZ // 2, 1) + 1).astype(f32)
    coarse = jnp.broadcast_to(coarse, (MX // 2, 2, MY // 2, 2, MZ // 2, 2)).reshape(per)
    tail = jnp.broadcast_to(jnp.concatenate([mid, coarse])[None], (8, TILE))

    def along_z(value):
        turns = [[(i, i ^ s) for i in range(n_gz)] for s in range(1, n_gz)]
        return jnp.stack([value] + [lax.ppermute(value, "gz", turn) for turn in turns])

    def to_all(column):
        flips = [
            [(i * n_gy + j, (i ^ dx) * n_gy + (j ^ dy)) for i in range(n_gx) for j in range(n_gy)]
            for dx, dy in ((1, 0), (0, 2), (1, 2))
        ]
        here = jnp.stack([column] + [lax.ppermute(column, ("gx", "gy"), flip) for flip in flips])
        return here, lax.ppermute(here, "gy", [(j, j ^ 1) for j in range(n_gy)])

    column = along_z(jnp.concatenate([payload, tail], axis=0))
    gain, code, near_gain, near_code = call(
        partial(gain_kernel, sizes), 6,
        [whole, shape_of(2 * CX, 1, LANES), small, small_code],
        [pltpu.VMEM(whole.shape, f32)],
        place_ref, own, *along_y, *deep, weights[3], After(payload),
    )
    solved = call(deep_kernel, 7, whole, wide, place_ref, gain, code, weights[0], After(column))
    planes, lanes = grid[0], grid[1] * grid[2]
    payload, solved, mid_code, coarse_code = call(
        partial(second_kernel, sizes, grid), 37,
        [shape_of(half, TILE), small, shape_of(planes, 1, lanes), shape_of(1, planes * lanes // 8)],
        wide * 2 + near * 2 + mid_scratch(grid),
        place_ref, *to_all(column), gain, code, solved,
        near_gain, near_code, source, *weights, limit=32,
    )
    result = call(
        partial(third_kernel, sizes, grid), 18,
        shape_of(MODES, BLOCK),
        near * 2 + mid_scratch(grid),
        place_ref, *to_all(along_z(payload)), mid_code, coarse_code, near_gain, near_code, solved, *weights,
    )
    return result[None, None, None]


def solution(mesh):
    placed = (
        P("gx", "gy", "gz", None, None),
        P(),
        P(),
        P(),
        P("gx", "gy", "gz", None),
        P("gx", "gy", "gz", None),
        P("gx", "gy", "gz", None),
    )
    sizes = tuple(mesh.shape[a] for a in ("gx", "gy", "gz"))
    wide = sizes[0] == 2 and sizes[1] == 4 and sizes[2] * MY * MZ * 2 == TILE
    return jax.shard_map(
        partial(wide_device, sizes) if wide else per_device,
        mesh=mesh,
        in_specs=placed,
        out_specs=P("gx", "gy", "gz", None, None),
        check_vma=False,
    )
```

```python
from functools import partial

import jax
import jax.numpy as jnp
from jax import lax
from jax.experimental import pallas as pl
from jax.experimental.pallas import tpu as pltpu
from jax.sharding import PartitionSpec as P

MODES = 64
MATERIALS = 4
SWEEPS = 2
COARSE_SWEEPS = 4
CYCLES = 2
CX = 8
CY = 8
CZ = 8


relax_weight = 0.7
restrict_scale = 0.6
highest = lax.Precision.HIGHEST


def padded_2(shard, sides, width):
    for axis, dim in sides:
        size, length = (lax.axis_size(axis), shard.shape[dim])
        up = [(i, (i + 1) % size) for i in range(size - 1)]
        down = [(j, i) for i, j in up]
        last = lax.slice_in_dim(shard, length - width, length, axis=dim)
        first = lax.slice_in_dim(shard, 0, width, axis=dim)
        before = lax.ppermute(last, axis, up)
        after = lax.ppermute(first, axis, down)
        shard = jnp.concatenate([before, shard, after], axis=dim)
    return shard


def inverse_blocks(diag_blocks):
    identity = jnp.eye(MODES, dtype=diag_blocks.dtype)
    result = []
    for material in range(MATERIALS):
        factor = jnp.linalg.cholesky(diag_blocks[material])
        result.append(jax.scipy.linalg.cho_solve((factor, True), identity))
    return jnp.stack(result).reshape(MATERIALS * MODES, MODES)


def coupling_matrix(diag_blocks, face_blocks):
    blocks = jnp.concatenate([diag_blocks[None], face_blocks], axis=0)
    return jnp.transpose(blocks, (1, 2, 0, 3)).reshape(MATERIALS * MODES, 7 * MODES)


def choose_blocks(weights, columns, onehot):
    product = jnp.dot(weights, columns, precision=highest, preferred_element_type=jnp.float32)
    product = product.reshape(MATERIALS, MODES, columns.shape[1])
    return jnp.sum(product * onehot.reshape(MATERIALS, 1, columns.shape[1]), axis=0)


def operate(padded, onehot, coupling):
    centre = padded[:, 1:-1, 1:-1, 1:-1]
    stacked = jnp.concatenate(
        [
            centre,
            padded[:, 2:, 1:-1, 1:-1],
            padded[:, :-2, 1:-1, 1:-1],
            padded[:, 1:-1, 2:, 1:-1],
            padded[:, 1:-1, :-2, 1:-1],
            padded[:, 1:-1, 1:-1, 2:],
            padded[:, 1:-1, 1:-1, :-2],
        ],
        axis=0,
    )
    columns = stacked.reshape(7 * MODES, -1)
    return choose_blocks(coupling, columns, onehot.reshape(MATERIALS, -1)).reshape(centre.shape)


def apply_inverse(inverse, field, onehot):
    return choose_blocks(inverse, field.reshape(MODES, -1), onehot.reshape(MATERIALS, -1)).reshape(
        field.shape
    )


def restrict(field, prolong):
    blocked = field.reshape(
        MODES, field.shape[1] // 2, 2, field.shape[2] // 2, 2, field.shape[3] // 2, 2
    )
    return restrict_scale * jnp.einsum(
        "abcji,jxaybzc->ixyz", prolong.reshape(2, 2, 2, MODES, MODES), blocked, precision=highest
    )


def expand(coarse_field, prolong):
    finer = jnp.einsum(
        "abcji,ixyz->jxaybzc",
        prolong.reshape(2, 2, 2, MODES, MODES),
        coarse_field,
        precision=highest,
    )
    return finer.reshape(
        MODES, 2 * coarse_field.shape[1], 2 * coarse_field.shape[2], 2 * coarse_field.shape[3]
    )


def make_onehot(materials):
    return (materials[None] == jnp.arange(MATERIALS, dtype=jnp.int32)[:, None, None, None]).astype(
        jnp.float32
    )


def fine_border(field):
    return padded_2(field, (("gx", 1), ("gy", 2), ("gz", 3)), 1)


def section_border(field):
    padded = padded_2(field, (("gx", 1), ("gy", 2)), 1)
    return jnp.pad(padded, ((0, 0), (0, 0), (0, 0), (1, 1)))


def smooth(iterate, source, onehot, border, inverse, coupling):
    residual = source - operate(border(iterate), onehot, coupling)
    return iterate + relax_weight * apply_inverse(inverse, residual, onehot)


def coarse_solve(source, onehot, border, inverse, coupling):
    iterate = relax_weight * apply_inverse(inverse, source, onehot)
    for repeat in range(COARSE_SWEEPS - 1):
        iterate = smooth(iterate, source, onehot, border, inverse, coupling)
    return iterate


def middle_cycle(source, onehot, border, inverse, coupling, prolong, coarse_solver):
    iterate = relax_weight * apply_inverse(inverse, source, onehot)
    iterate = smooth(iterate, source, onehot, border, inverse, coupling)
    residual = source - operate(border(iterate), onehot, coupling)
    iterate = iterate + expand(coarse_solver(restrict(residual, prolong)), prolong)
    for repeat in range(SWEEPS):
        iterate = smooth(iterate, source, onehot, border, inverse, coupling)
    return iterate


def single_steps(iterate, actions, source, onehot, inverse, coupling):
    residual = None
    for action in actions:
        if action == "sweep":
            iterate = smooth(iterate, source, onehot, fine_border, inverse, coupling)
        else:
            residual = source - operate(fine_border(iterate), onehot, coupling)
    return (iterate, residual)


def per_device(right_side, diag_blocks, face_blocks, prolong, mats_fine, mats_mid, mats_coarse):
    inverse = inverse_blocks(diag_blocks)
    coupling = coupling_matrix(diag_blocks, face_blocks)
    source = right_side[0, 0, 0].reshape(MODES, CX, CY, CZ)
    onehot_fine = make_onehot(mats_fine[0, 0, 0].reshape(CX, CY, CZ))
    onehot_mid = make_onehot(mats_mid[0, 0, 0].reshape(CX // 2, CY // 2, CZ // 2))
    onehot_coarse = make_onehot(mats_coarse[0, 0, 0].reshape(CX // 4, CY // 4, CZ // 4))
    stepper = partial(
        single_steps, source=source, onehot=onehot_fine, inverse=inverse, coupling=coupling
    )
    iterate = relax_weight * apply_inverse(inverse, source, onehot_fine)
    for cycle_index in range(CYCLES):
        if cycle_index == 0:
            actions = ["sweep"] * (SWEEPS - 1) + ["residual"]
        else:
            actions = ["sweep"] * SWEEPS + ["residual"]
        iterate, residual = stepper(iterate, actions)
        gathered_source = lax.all_gather(restrict(residual, prolong), "gz", axis=3, tiled=True)
        gathered_mid = lax.all_gather(onehot_mid, "gz", axis=3, tiled=True)
        gathered_coarse = lax.all_gather(onehot_coarse, "gz", axis=3, tiled=True)
        local_solver = partial(
            coarse_solve,
            onehot=gathered_coarse,
            border=section_border,
            inverse=inverse,
            coupling=coupling,
        )
        section_field = middle_cycle(
            gathered_source, gathered_mid, section_border, inverse, coupling, prolong, local_solver
        )
        iterate = iterate + expand(
            lax.dynamic_slice_in_dim(section_field, lax.axis_index("gz") * (CZ // 2), CZ // 2, 3),
            prolong,
        )
        iterate, unused_residual = stepper(iterate, ["sweep"] * SWEEPS)
    return iterate.reshape(MODES, CX * CY * CZ)[None, None, None]


HALO = 3 * SWEEPS + SWEEPS - 1
PITCH = CY + 2 * HALO
BLOCK = CX * CY * CZ
TILE = 128
LANES = -(-(PITCH * PITCH) // TILE) * TILE
ROWS = MODES + 8
MX, MY, MZ = CX // 2, CY // 2, CZ // 2
f32 = jnp.float32
bf16 = jnp.bfloat16


def split(value):
    high = value.astype(bf16)
    return high, (value - high.astype(f32)).astype(bf16)


def dot(a, b):
    return jnp.dot(a, b, preferred_element_type=f32)


def iota(shape, dim):
    return lax.broadcasted_iota(jnp.int32, shape, dim)


def where_equal(rows, columns):
    return jnp.where(rows == columns, 1.0, 0.0).astype(bf16)


def place(value, selector):
    high, low = split(value)
    return dot(high, selector) + dot(low, selector)


def pick(product, code, first):
    out = jnp.zeros((MODES, product.shape[1]), f32)
    for m in range(MATERIALS):
        out = jnp.where(code == m + first, product[m * MODES:(m + 1) * MODES], out)
    return out


def stack3(value):
    high, low = split(value)
    return jnp.concatenate([high, low, high], axis=0)


def thirds(value):
    high, low = split(value)
    return jnp.concatenate([high, high, low], axis=1)


def inverse_kernel(diag, scaled):
    a = diag[...]
    row_id = iota((1, MODES, 1), 1)
    lane_id = iota((1, 1, MODES), 2)
    for k in range(MODES):
        pivot = 1.0 / a[:, k:k + 1, k:k + 1]
        on_row, on_lane = row_id == k, lane_id == k
        row = jnp.where(on_lane, pivot, a[:, k:k + 1, :] * pivot)
        column = a[:, :, k:k + 1]
        a = jnp.where(on_row, row, jnp.where(on_lane, 0.0, a) - column * row)
    scaled[...] = relax_weight * a


def weights_kernel(scaled, diag, face, prolong, wg, wa, wd, wi, wr, wp):
    beside, gains = [], []
    for m in range(MATERIALS):
        faces = jnp.concatenate([face[d, m] for d in (1, 0, 2, 3, 4, 5)], axis=1)
        beside.append(faces)
        gains.append(jnp.dot(scaled[m], faces, precision=highest, preferred_element_type=f32))
    for target, blocks in ((wa, beside), (wg, gains)):
        high, low = split(jnp.concatenate(blocks, axis=0))
        target[...] = jnp.concatenate([high, low, high], axis=1)
    wd[...] = thirds(jnp.concatenate([diag[m] for m in range(MATERIALS)], axis=0))
    wi[...] = thirds(jnp.concatenate([scaled[m] for m in range(MATERIALS)], axis=0))
    for p in range(2):
        wr[p] = thirds(jnp.concatenate([restrict_scale * prolong[p * 4 + c].T for c in range(4)], axis=0))
    wp[...] = thirds(jnp.concatenate([prolong[c] for c in range(8)], axis=0))


def invert(diag_blocks):
    return call(inverse_kernel, 6, shape_of(*diag_blocks.shape), [], diag_blocks)


def make_weights(scaled, diag_blocks, face_blocks, prolong):
    rows = MATERIALS * MODES
    shapes = [(rows, 18 * MODES)] * 2 + [(rows, 3 * MODES)] * 2
    shapes += [(2, 4 * MODES, 3 * MODES), (8 * MODES, 3 * MODES)]
    shapes = [jax.ShapeDtypeStruct(shape, bf16) for shape in shapes]
    return call(weights_kernel, 1, shapes, [], scaled, diag_blocks, face_blocks, prolong)


SHALLOW = SWEEPS
PAIRS = CX
SLOT = CY * CZ


def layer_rows(depth, halo):
    return CY + 2 * (halo - depth)


SHALLOW_LANES = sum(layer_rows(d, SHALLOW) for d in range(1, SHALLOW + 1))
DEEP_LANES = sum(layer_rows(d, HALO) for d in range(1, HALO + 1))
PER_TILE = TILE // (2 * SHALLOW_LANES)
SHALLOW_TILES = -(-PAIRS // PER_TILE)


def layer_of(index, first, last, halo):
    depth, start, at = jnp.full_like(index, first), jnp.zeros_like(index), 0
    for d in range(first + 1, last + 1):
        at += layer_rows(d - 1, halo)
        inside = index >= at
        depth, start = jnp.where(inside, d, depth), jnp.where(inside, at, start)
    return depth, index - start - (halo - depth)


def lane_of(depth, y, first, last, halo):
    start, at = jnp.zeros_like(depth), 0
    for d in range(first + 1, last + 1):
        at += layer_rows(d - 1, halo)
        start = jnp.where(depth == d, at, start)
    inside = (depth >= first) & (depth <= last) & (y >= depth - halo) & (y < CY + halo - depth)
    return jnp.where(inside, start + y + halo - depth, -(1 << 20))


def prepare_kernel(place_ref, values, other, materials, other_materials, out):
    mine = place_ref[0]
    for half, (block, kinds) in enumerate(((values, materials), (other, other_materials))):
        first = (mine ^ half) * (BLOCK // TILE)
        codes = jnp.broadcast_to((kinds[...] + 1).astype(f32), (ROWS - MODES, BLOCK))
        for tile in range(BLOCK // TILE):
            lanes = slice(tile * TILE, (tile + 1) * TILE)
            out[first + tile, :MODES] = block[:, lanes]
            out[first + tile, MODES:] = codes[:, lanes]


def swap_tile(y, odd):
    place = (y + CY) // CY
    return jnp.where(place == 1, 1, jnp.where(place // 2 == odd, 2, 0))


def pack_kernel(place_ref, own, first, second, thin_first, thin_second, thick_first, thick_second):
    column = iota((1, 4 * TILE), 1)
    lane, kind = column % TILE, column // TILE
    row = iota((3 * TILE, 4 * TILE), 0)
    odd_y, odd_z = place_ref[1] & 1, place_ref[2] & 1
    parts = [jnp.concatenate([r[pair] for r in (first, own, second)], axis=1) for pair in range(PAIRS)]
    parts = split(jnp.concatenate(parts, axis=0))
    shallow = 0.0
    for odd in range(2):
        thin = lane - odd * SHALLOW_LANES
        thin_depth, thin_y = layer_of(thin, 1, SHALLOW, SHALLOW)
        thick_depth, thick_y = layer_of(lane, 1, HALO, HALO)
        depth = jnp.where(kind < 2, thin_depth, thick_depth)
        y = jnp.where(kind < 2, thin_y, thick_y)
        valid = jnp.where(
            kind < 2,
            jnp.where((thin >= 0) & (thin < SHALLOW_LANES), 1, 0),
            jnp.where(lane < DEEP_LANES, 1, 0),
        )
        z = jnp.where(kind % 2 == odd_z, CZ - depth, depth - 1)
        source = swap_tile(y, odd_y) * TILE + ((y + CY) % CY) * CZ + z + odd * SLOT
        selector = where_equal(row, jnp.where(valid == 1, source, -1))
        packed = dot(parts[0], selector) + dot(parts[1], selector)
        shallow = shallow + packed[:, :2 * TILE]
        for pair in range(PAIRS):
            rows = packed[pair * ROWS:(pair + 1) * ROWS]
            thick_first[2 * pair + odd], thick_second[2 * pair + odd] = rows[:, 2 * TILE:3 * TILE], rows[:, 3 * TILE:]
    for tile in range(SHALLOW_TILES):
        for kind, out in enumerate((thin_first, thin_second)):
            strip = 0.0
            for slot in range(PER_TILE):
                pair = tile * PER_TILE + slot
                if pair < PAIRS:
                    piece = shallow[pair * ROWS:(pair + 1) * ROWS, kind * TILE:(kind + 1) * TILE]
                    strip = strip + (pltpu.roll(piece, slot * 2 * SHALLOW_LANES, 1) if slot else piece)
            out[tile] = strip


def shallow_strip(first, second, pair):
    tile, slot = pair // PER_TILE, pair % PER_TILE
    shift = (TILE - slot * 2 * SHALLOW_LANES) % TILE
    lane = iota((1, TILE), 1)
    return jnp.where(
        lane < TILE // 2,
        pltpu.roll(first[tile], shift, 1),
        pltpu.roll(second[tile], (shift + TILE // 2) % TILE, 1),
    )


def in_grid(place_ref, sizes, y, z):
    whole_y, whole_z = y + place_ref[1] * CY, z + place_ref[2] * CZ
    return (whole_y >= 0) & (whole_y < sizes[1] * CY) & (whole_z >= 0) & (whole_z < sizes[2] * CZ)


def unpack(layout, sizes, place_ref, own, along_y, along_z, start, pairs, put, shallow):
    lane = iota((1, layout.lanes), 1)
    y, z = layout.place(lane)
    odd_y, odd_z = place_ref[1] & 1, place_ref[2] & 1
    inner = swap_tile(y, odd_y) * TILE + ((y + CY) % CY) * CZ + z
    depth = jnp.where(z < 0, -z, z - (CZ - 1))
    middle = (z >= 0) & (z < CZ)
    strip = jnp.where(jnp.where(z < 0, 0, 1) == odd_z, 1, 0)
    if shallow:
        outer = lane_of(depth, y, 1, SHALLOW, SHALLOW) + 3 * TILE + strip * (TILE // 2)
        step = SHALLOW_LANES
    else:
        outer = lane_of(depth, y, 1, HALO, HALO) + (3 + strip) * TILE
        step = 0
    row = iota(((4 if shallow else 5) * TILE, layout.lanes), 0)
    valid = (lane < layout.used) & in_grid(place_ref, sizes, y, z)
    parts = []
    for odd in range(2):
        if odd == 0 or not shallow:
            parts = []
            for i in range(pairs):
                pair = start + i
                line = [r[pair] for r in (along_y[0], own, along_y[1])]
                line += [shallow_strip(*along_z, pair)] if shallow else [r[2 * pair + odd] for r in along_z]
                parts.append(jnp.concatenate(line, axis=1))
            parts = split(jnp.concatenate(parts, axis=0))
        source = jnp.where(middle, inner + odd * SLOT, outer + odd * step)
        selector = where_equal(row, jnp.where(valid, source, -1))
        placed = dot(parts[0], selector) + dot(parts[1], selector)
        for i in range(pairs):
            rows = placed[i * ROWS:(i + 1) * ROWS]
            put(2 * (start + i) + odd, rows[:MODES], rows[MODES:MODES + 1])


class Field:
    def __init__(self, full, high, low, shifts, masks=(None,) * 4):
        self.full, self.high, self.low = full, high, low
        self.shifts, self.masks = shifts, masks

    def put(self, x, value):
        self.full[x + 1] = value
        self.high[x + 1], self.low[x + 1] = split(value)

    def put_parts(self, x, high, low):
        self.full[x + 1] = high + low
        self.high[x + 1], self.low[x + 1] = high.astype(bf16), low.astype(bf16)

    def clear_ends(self):
        planes = self.full.shape[0]
        for x in (0, planes - 1):
            self.full[x] = jnp.zeros(self.full.shape[1:], f32)
            self.high[x] = jnp.zeros(self.full.shape[1:], bf16)
            self.low[x] = jnp.zeros(self.full.shape[1:], bf16)

    def get(self, x):
        return self.full[x + 1]


def field_scratch(planes, lanes):
    shape = (planes + 2, MODES, lanes)
    return [pltpu.VMEM(shape, f32), pltpu.VMEM(shape, bf16), pltpu.VMEM(shape, bf16)]


class Layout:
    def __init__(self, halo, lanes):
        self.halo, self.lanes, self.pitch = halo, lanes, CY + 2 * halo
        self.used = self.pitch * self.pitch
        self.factor = -(-(1 << 16) // self.pitch)

    def place(self, lane):
        y = (lane * self.factor) >> 16
        return y - self.halo, lane - y * self.pitch - self.halo

    def parity(self):
        y, z = self.place(iota((1, self.lanes), 1))
        return (y & 1) * 2 + (z & 1)

    def shifts(self):
        return (self.lanes - self.pitch, self.pitch, self.lanes - 1, 1)

    def field(self, refs):
        return Field(*refs, self.shifts())

    def own_lanes(self, lane):
        y, z = self.place(lane)
        return y, z, (lane < self.used) & (y >= 0) & (y < CY) & (z >= 0) & (z < CZ)


def lanes_for(halo):
    return -(-((CY + 2 * halo) ** 2) // TILE) * TILE


NEAR = 2 * SWEEPS
wide_layout = Layout(HALO, lanes_for(HALO))
near_layout = Layout(NEAR, lanes_for(NEAR))


def near_selector():
    y, z = near_layout.place(iota((1, near_layout.lanes), 1))
    source = (y + HALO) * PITCH + z + HALO
    source = jnp.where(iota((1, near_layout.lanes), 1) < near_layout.used, source, -1)
    return where_equal(iota((LANES, near_layout.lanes), 0), source)


def coupled_rows(centre, field, x):
    moved = []
    for shift, mask in zip(field.shifts, field.masks):
        part = pltpu.roll(centre, shift, 1)
        moved.append(part if mask is None else jnp.where(mask, part, 0.0))
    high, low = split(jnp.concatenate(moved, axis=0))
    high = [field.high[x], field.high[x + 2], high]
    low = [field.low[x], field.low[x + 2], low]
    return jnp.concatenate(high + high + low, axis=0)


def grouped(start, count, size, body):
    groups = -(-count // size)
    length = -(-count // groups)
    if groups == 1:
        body(start, count)
        return

    def step(i, carry):
        body(start + jnp.minimum(i * length, count - length), length)
        return carry

    lax.fori_loop(0, groups, step, 0)


def group_size(lanes):
    return 7 if lanes > 2 * TILE else 6


def sweep(source, target, start, count, wg, gain, code, store=None, size=None):
    def body(first, length):
        values = []
        for x in [first + j for j in range(length)]:
            centre = source.get(x)
            product = dot(wg[...], coupled_rows(centre, source, x))
            values.append((1.0 - relax_weight) * centre + gain[x] - pick(product, code[x], 1))
        for j, value in enumerate(values):
            (store or target.put)(first + j, value)

    grouped(start, count, size or group_size(source.full.shape[2]), body)


def residual(field, x, source, wa, wd, code):
    centre = field.get(x)
    applied = dot(wa[...], coupled_rows(centre, field, x)) + dot(wd[...], stack3(centre))
    return source - pick(applied, code, 1)


def restrict_plane(wr, residuals, parity):
    out = 0.0
    for p in range(2):
        out = out + pick(dot(wr[p], stack3(residuals[p])), parity, 0)
    return out


def expand_planes(wp, raised_high, raised_low, parity):
    product = dot(wp[...], jnp.concatenate([raised_high, raised_low, raised_high], axis=0))
    return [pick(product[p * 4 * MODES:(p + 1) * 4 * MODES], parity, 0) for p in range(2)]


def gather_mid(place_ref, here, sibling, sizes, put):
    n_gx, n_gy, n_gz = sizes
    per = MX * MY * MZ
    lines = MY * n_gz * MZ
    column = iota((1, n_gz * 2 * per), 1)
    k, rest = column % MZ, column // MZ
    gz, rest = rest % n_gz, rest // n_gz
    j, rest = rest % MY, rest // MY
    i, h = rest % MX, rest // MX
    source = gz * 2 * per + h * per + (i * MY + j) * MZ + k
    selector = where_equal(iota((n_gz * 2 * per, n_gz * 2 * per), 0), source)
    rows = here.shape[2]
    my_x, my_y, my_z = place_ref[0], place_ref[1], place_ref[2]
    parts = []
    for gx in range(n_gx):
        for gy in range(n_gy):
            slot = ((gx ^ my_x) & 1) + 2 * (((gy ^ my_y) >> 1) & 1)
            line = []
            for gz in range(n_gz):
                turn = my_z ^ gz
                line.append(jnp.where(((gy ^ my_y) & 1) == 0, here[slot, turn], sibling[slot, turn]))
            parts.append(jnp.concatenate(line, axis=1))
    placed = place(jnp.concatenate(parts, axis=0), selector)
    lower = iota((1, TILE), 1) < lines
    for gx in range(n_gx):
        for i in range(MX):
            quarters = []
            for h in range(2):
                tiles = []
                for pair in range(n_gy // 2):
                    block = [placed[(gx * n_gy + 2 * pair + s) * rows:][:rows] for s in range(2)]
                    at = ((h * MX + i) * lines) // TILE * TILE
                    block = [b[:, at:at + TILE] for b in block]
                    if i % 2 == 0:
                        block[1] = pltpu.roll(block[1], lines, 1)
                    else:
                        block[0] = pltpu.roll(block[0], lines, 1)
                    tiles.append(jnp.where(lower, block[0], block[1]))
                quarters.append(jnp.concatenate(tiles, axis=1))
            put(gx * MX + i, quarters)


class Coarse:
    def __init__(self, grid):
        self.x, self.y, self.z = (size // 2 for size in grid)
        self.plane = self.y * self.z
        self.lanes = self.x * self.plane

    def place(self, lane):
        return lane // self.plane, lane // self.z % self.y, lane % self.z

    def solve(self, value, wg, wi, code):
        x, y, z = self.place(iota((1, self.lanes), 1))
        gain = pick(dot(wi[...], stack3(value)), code, 1)
        moves = (
            (self.plane, x > 0), (self.lanes - self.plane, x < self.x - 1),
            (self.lanes - self.z, y < self.y - 1), (self.z, y > 0),
            (self.lanes - 1, z < self.z - 1), (1, z > 0),
        )

        def step(repeat, iterate):
            moved = [jnp.where(mask, pltpu.roll(iterate, shift, 1), 0.0) for shift, mask in moves]
            high, low = split(jnp.concatenate(moved, axis=0))
            product = dot(wg[...], jnp.concatenate([high, high, low], axis=0))
            return (1.0 - relax_weight) * iterate + gain - pick(product, code, 1)

        return lax.fori_loop(0, COARSE_SWEEPS - 1, step, gain)


def solve_mid(source, gain, code, coarse_source, coarse_code, fields, weights, grid):
    wg, wa, wd, wi, wr, wp = weights
    planes, size_y, size_z = grid
    lanes = size_y * size_z
    coarse = Coarse(grid)
    for i in range(2):
        fields(i).clear_ends()

    def begin(first, length):
        values = [pick(dot(wi[...], stack3(source[first + j])), code[first + j], 1) for j in range(length)]
        for j, value in enumerate(values):
            gain[first + j] = value
            fields(0).put(first + j, value)

    grouped(0, planes, 4, begin)
    lane = iota((1, lanes), 1)
    y, z = lane // size_z, lane % size_z
    parity = (y % 2) * 2 + z % 2
    tall, wide = iota((lanes, TILE), 0), iota((lanes, TILE), 1)
    squeeze = (tall // size_z // 2) * coarse.z + tall % size_z // 2
    per_tile = TILE // coarse.plane
    target = (y // 2) * coarse.z + z // 2
    row = iota((coarse.lanes, lanes), 0)

    def correct(field):
        def down(tile, carry):
            total = 0.0
            for part in range(per_tile):
                x = 2 * (tile * per_tile + part)
                rests = [residual(field, x + p, source[x + p], wa, wd, code[x + p]) for p in range(2)]
                selector = where_equal(squeeze + part * coarse.plane, wide)
                total = total + place(restrict_plane(wr, rests, parity), selector)
            coarse_source[:, pl.ds(pl.multiple_of(tile * TILE, TILE), TILE)] = total
            return carry

        lax.fori_loop(0, coarse.lanes // TILE, down, 0)
        result = coarse.solve(coarse_source[...], wg, wi, coarse_code[...])
        parts = jnp.concatenate(split(result), axis=0)

        def up(step, carry):
            for pair in (2 * step, 2 * step + 1):
                raised = dot(parts, where_equal(row, target + pair * coarse.plane)).astype(bf16)
                for p, value in enumerate(expand_planes(wp, raised[:MODES], raised[MODES:], parity)):
                    field.put(2 * pair + p, field.get(2 * pair + p) + value)
            return carry

        lax.fori_loop(0, coarse.x // 2, up, 0)

    def step(i, carry):
        sweep(fields(i % 2), fields(1 - i % 2), 0, planes, wg, gain, code, size=planes)

        @pl.when(i == SWEEPS - 2)
        def _():
            correct(fields(1 - i % 2))

        return carry

    lax.fori_loop(0, 2 * SWEEPS - 1, step, 0)
    return fields((2 * SWEEPS - 1) % 2)


def add_mid(place_ref, layout, result, field, depth, wp, grid, old):
    planes, size_y, size_z = grid
    gx, gy, gz = place_ref[0], place_ref[1], place_ref[2]
    lane = iota((1, layout.lanes), 1)
    y, z = layout.place(lane)
    whole_y, whole_z = y + gy * CY, z + gz * CZ
    inside = (lane < layout.used) & (whole_y >= 0) & (whole_y < 2 * size_y) & (whole_z >= 0) & (whole_z < 2 * size_z)
    target = jnp.where(inside, (whole_y >> 1) * size_z + (whole_z >> 1), -1)
    raise_lanes = where_equal(iota((size_y * size_z, layout.lanes), 0), target)
    parity = layout.parity()

    def body(first, length):
        values = []
        for x in [first + j for j in range(length)]:
            parts = jnp.concatenate([result.high[x + 1], result.low[x + 1]], axis=0)
            raised = dot(parts, raise_lanes).astype(bf16)
            for p, value in enumerate(expand_planes(wp, raised[:MODES], raised[MODES:], parity)):
                values.append(old[2 * x + p] + value)
        for j, value in enumerate(values):
            field.put(2 * first + j, value)

    grouped(gx * ((CX - depth) // 2), (CX + depth) // 2, max(group_size(layout.lanes) // 3, 1), body)


def fine_residual(field, own, source, wr, wa, wd, code):
    layout = near_layout
    tall, wide = iota((layout.lanes, TILE), 0), iota((layout.lanes, TILE), 1)
    y, z, inside = layout.own_lanes(tall)
    target = jnp.where(inside, (y >> 1) * MZ + (z >> 1), -BLOCK)
    per = MX * MY * MZ
    index = wide % per
    parity = layout.parity()
    def add(step, total):
        for i in (2 * step, 2 * step + 1):
            x = own + 2 * i
            rests = [residual(field, x + p, source[2 * i + p], wa, wd, code[x + p]) for p in range(2)]
            total = total + place(restrict_plane(wr, rests, parity), where_equal(target + i * MY * MZ, index))
        return total

    total = lax.fori_loop(0, MX // 2, add, jnp.zeros((MODES, TILE), f32))
    half = MODES // 2
    return jnp.where(iota((1, TILE), 1) < per, total[:half], total[half:])


def near_kernel(sizes, place_ref, own, y0, y1, z0, z1, wg, wa, wd, wi, wr, wp, source, payload, *scratch):
    layout = near_layout
    first, second = layout.field(scratch[0:3]), layout.field(scratch[3:6])
    whole, gain, code = scratch[6:9]
    first.clear_ends()
    second.clear_ends()
    gx = place_ref[0]

    def put(x, value, material):
        whole[x], code[x] = value, material

    start, pairs = gx * ((CX - SHALLOW) // 2), (CX + SHALLOW) // 2
    unpack(layout, sizes, place_ref, own, (y0, y1), (z0, z1), start, pairs, put, True)

    def begin(start, length):
        values = [pick(dot(wi[...], stack3(whole[start + j])), code[start + j], 1) for j in range(length)]
        for j, value in enumerate(values):
            gain[start + j] = value
            first.put(start + j, value)

    grouped(gx * (CX - SHALLOW), CX + SHALLOW, group_size(layout.lanes), begin)
    depth = SHALLOW - 1
    sweep(first, second, gx * (CX - depth), CX + depth, wg, gain, code)
    mine = gx * CX
    source[...] = whole[pl.ds(mine, CX)]
    payload[...] = fine_residual(second, mine, source, wr, wa, wd, code)


def gain_kernel(sizes, place_ref, own, y0, y1, z0, z1, wi, payload, gain, code, near_gain, near_code, passed, whole):
    def put(x, value, material):
        whole[x], code[x] = value, material

    unpack(wide_layout, sizes, place_ref, own, (y0, y1), (z0, z1), 0, PAIRS, put, False)
    to_near = near_selector()

    def begin(start, length):
        values = [pick(dot(wi[...], stack3(whole[start + j])), code[start + j], 1) for j in range(length)]
        for j, value in enumerate(values):
            gain[start + j] = value
            near_gain[start + j] = place(value, to_near)
        for j in range(length):
            near_code[start + j] = dot(jnp.broadcast_to(code[start + j], (8, LANES)).astype(bf16), to_near)[:1]

    grouped(0, 2 * CX, 4, begin)
    passed[...] = payload[...]


def deep_kernel(place_ref, gain, code, wg, column, solved, passed, *scratch):
    passed[...] = column[...]
    first = wide_layout.field(scratch)
    first.clear_ends()
    for x in range(2 * CX):
        first.put(x, gain[x])
    depth = HALO - 1
    gx = place_ref[0]

    def store(x, value):
        solved[x] = value

    sweep(first, None, gx * (CX - depth), CX + depth, wg, gain, code, store)


def mid_scratch(grid):
    planes, size_y, size_z = grid
    lanes = size_y * size_z
    both = [pltpu.VMEM((2,) + ref.shape, ref.dtype) for ref in field_scratch(planes, lanes)]
    return both + [pltpu.VMEM((planes, MODES, lanes), f32)] * 2 + [pltpu.VMEM((MODES, planes * lanes // 8), f32)]


def run_mid(place_ref, here, sibling, sizes, grid, weights, scratch, mid_code, coarse_code, read_codes):
    planes, size_y, size_z = grid
    lanes = size_y * size_z
    lane = iota((1, lanes), 1)
    y, z = lane // size_z, lane % size_z
    shifts = (lanes - size_z, size_z, lanes - 1, 1)
    masks = (y < size_y - 1, y > 0, z < size_z - 1, z > 0)
    source, gain, coarse_source = scratch[3:6]

    def fields(i):
        return Field(*(ref.at[i] for ref in scratch[0:3]), shifts, masks)

    half = MODES // 2
    coarse = Coarse(grid)
    corners = []

    def put(x, quarters):
        source[x, :half] = quarters[0][:half]
        source[x, half:] = quarters[1][:half]
        if read_codes:
            mid_code[x] = quarters[0][half:half + 1]
            if x % 2 == 0:
                corners.append(jnp.broadcast_to(quarters[1][half:half + 1], (8, lanes)).astype(bf16))

    gather_mid(place_ref, here, sibling, sizes, put)
    if read_codes:
        tall, wide = iota((lanes, coarse.lanes), 0), iota((lanes, coarse.lanes), 1)
        x, cy, cz = coarse.place(wide)
        total = 0.0
        for pair in range(coarse.x):
            selector = where_equal(jnp.where(x == pair, 2 * cy * size_z + 2 * cz, -1), tall)
            total = total + dot(corners[pair], selector)
        coarse_code[...] = total[:1]
    return solve_mid(source, gain, mid_code, coarse_source, coarse_code, fields, weights, grid)


def second_kernel(sizes, grid, place_ref, here, sibling, gain, code, solved, near_gain, near_code, source,
                  wg, wa, wd, wi, wr, wp, payload, result, mid_code, coarse_code, *scratch):
    weights = (wg, wa, wd, wi, wr, wp)
    answer = run_mid(place_ref, here, sibling, sizes, grid, weights, scratch[12:], mid_code, coarse_code, True)
    first, second = wide_layout.field(scratch[0:3]), wide_layout.field(scratch[3:6])
    now, other = near_layout.field(scratch[6:9]), near_layout.field(scratch[9:12])
    for field in (first, second, now, other):
        field.clear_ends()
    depth = 3 * SWEEPS
    gx = place_ref[0]
    add_mid(place_ref, wide_layout, answer, first, depth, wp, grid, solved)
    to_near = near_selector()

    def narrow(x, value):
        parts = dot(jnp.concatenate(split(value), axis=0), to_near)
        now.put_parts(x, parts[:MODES], parts[MODES:])

    for repeat in range(2 * SWEEPS):
        depth -= 1
        start, count = gx * (CX - depth), CX + depth
        if depth > NEAR:
            sweep(first, second, start, count, wg, gain, code)
            first, second = second, first
        elif depth == NEAR:
            sweep(first, None, start, count, wg, gain, code, narrow)
        else:
            sweep(now, other, start, count, wg, near_gain, near_code)
            now, other = other, now
    payload[...] = fine_residual(now, gx * CX, source, wr, wa, wd, near_code)
    result[...] = now.full[1:1 + 2 * CX]


def third_kernel(sizes, grid, place_ref, here, sibling, mid_code, coarse_code, near_gain, near_code, solved,
                 wg, wa, wd, wi, wr, wp, result, *scratch):
    weights = (wg, wa, wd, wi, wr, wp)
    answer = run_mid(place_ref, here, sibling, sizes, grid, weights, scratch[6:], mid_code, coarse_code, False)
    layout = near_layout
    now, other = layout.field(scratch[0:3]), layout.field(scratch[3:6])
    now.clear_ends()
    other.clear_ends()
    depth = SWEEPS
    gx = place_ref[0]
    add_mid(place_ref, layout, answer, now, depth, wp, grid, solved)
    for repeat in range(SWEEPS):
        depth -= 1
        sweep(now, other, gx * (CX - depth), CX + depth, wg, near_gain, near_code)
        now, other = other, now
    tall, wide = iota((layout.lanes, TILE), 0), iota((layout.lanes, TILE), 1)
    y, z, inside = layout.own_lanes(tall)
    target = jnp.where(inside, y * CZ + z, -BLOCK)
    selectors = [where_equal(target + odd * CY * CZ, wide) for odd in range(2)]
    for pair in range(CX // 2):
        total = 0.0
        for odd in range(2):
            value = now.get(gx * CX + 2 * pair + odd)
            high, low = split(value)
            lowest = (value - high.astype(f32) - low.astype(f32)).astype(bf16)
            for part in (high, low, lowest):
                total = total + dot(part, selectors[odd])
        result[:, pair * TILE:(pair + 1) * TILE] = total


def call(kernel, cost_us, out_shape, scratch, *args, limit=16):
    vmem, smem = pl.BlockSpec(memory_space=pltpu.VMEM), pl.BlockSpec(memory_space=pltpu.SMEM)
    specs = [smem if a.dtype == jnp.int32 and a.ndim == 1 else vmem for a in args]
    cost = pl.CostEstimate(flops=int(cost_us * 1e9), bytes_accessed=int(cost_us * 3e6), transcendentals=0)
    return pl.pallas_call(
        kernel,
        out_shape=out_shape,
        in_specs=specs,
        out_specs=jax.tree.map(lambda s: vmem, out_shape),
        scratch_shapes=scratch,
        cost_estimate=cost,
        compiler_params=pltpu.CompilerParams(vmem_limit_bytes=limit * 1024 * 1024),
    )(*args)


def shape_of(*dims):
    return jax.ShapeDtypeStruct(dims, f32)


def wide_device(sizes, right_side, diag_blocks, face_blocks, prolong, mats_fine, mats_mid, mats_coarse):
    n_gx, n_gy, n_gz = sizes
    axes = ("gx", "gy", "gz")
    grid = (n_gx * MX, n_gy * MY, n_gz * MZ)
    place_ref = jnp.stack([lax.axis_index(a) for a in axes]).astype(jnp.int32)
    tiles = BLOCK // TILE
    values, kinds = right_side.reshape(MODES, BLOCK), mats_fine.reshape(1, BLOCK)
    swap = [(0, 1), (1, 0)]
    others = lax.ppermute(values, "gx", swap), lax.ppermute(kinds, "gx", swap)
    scaled = invert(diag_blocks)
    own = call(
        prepare_kernel, 0.5, shape_of(2 * tiles, ROWS, TILE), [], place_ref, values, others[0], kinds, others[1]
    )
    swaps = {}
    for axis, n in zip(axes, sizes):
        inner = [pair for i in range(1, n - 1, 2) for pair in ((i, i + 1), (i + 1, i))]
        swaps[axis] = [(i, i ^ 1) for i in range(n)], [(0, 0)] + inner + [(n - 1, n - 1)]
    along_y = [lax.ppermute(own, "gy", swap) for swap in swaps["gy"]]
    weights = make_weights(scaled, diag_blocks, face_blocks, prolong)
    thin, thick = shape_of(SHALLOW_TILES, ROWS, TILE), shape_of(2 * PAIRS, ROWS, TILE)
    send = call(pack_kernel, 1.5, [thin, thin, thick, thick], [], place_ref, own, *along_y)
    shallow = [lax.ppermute(value, "gz", swap) for value, swap in zip(send[:2], swaps["gz"])]
    deep = [lax.ppermute(value, "gz", swap) for value, swap in zip(send[2:], swaps["gz"])]

    wide = field_scratch(2 * CX, LANES)
    near = field_scratch(2 * CX, near_layout.lanes)
    half, per = MODES // 2, MX * MY * MZ
    whole = shape_of(2 * CX, MODES, LANES)
    small = shape_of(2 * CX, MODES, near_layout.lanes)
    small_code = shape_of(2 * CX, 1, near_layout.lanes)
    source, payload = call(
        partial(near_kernel, sizes), 7,
        [shape_of(CX, MODES, near_layout.lanes), shape_of(half, TILE)],
        near * 2 + [pltpu.VMEM(s.shape, f32) for s in (small, small, small_code)],
        place_ref, own, *along_y, *shallow, *weights,
    )
    mid = (mats_mid.reshape(per) + 1).astype(f32)
    coarse = (mats_coarse.reshape(MX // 2, 1, MY // 2, 1, MZ // 2, 1) + 1).astype(f32)
    coarse = jnp.broadcast_to(coarse, (MX // 2, 2, MY // 2, 2, MZ // 2, 2)).reshape(per)
    tail = jnp.broadcast_to(jnp.concatenate([mid, coarse])[None], (8, TILE))

    def along_z(value):
        turns = [[(i, i ^ s) for i in range(n_gz)] for s in range(1, n_gz)]
        return [lax.ppermute(value, "gz", turn) for turn in turns]

    def across(column):
        flips = [
            [(i * n_gy + j, (i ^ dx) * n_gy + (j ^ dy)) for i in range(n_gx) for j in range(n_gy)]
            for dx, dy in ((1, 0), (0, 2), (1, 2))
        ]
        return [lax.ppermute(column, ("gx", "gy"), flip) for flip in flips]

    def with_sibling(here):
        return here, lax.ppermute(here, "gy", [(j, j ^ 1) for j in range(n_gy)])

    payload = jnp.concatenate([payload, tail], axis=0)
    turned = along_z(payload)
    gain, code, near_gain, near_code, payload = call(
        partial(gain_kernel, sizes), 6,
        [whole, shape_of(2 * CX, 1, LANES), small, small_code, shape_of(*payload.shape)],
        [pltpu.VMEM(whole.shape, f32)],
        place_ref, own, *along_y, *deep, weights[3], payload,
    )
    column = jnp.stack([payload] + turned)
    flipped = across(column)
    solved, column = call(
        deep_kernel, 7, [whole, shape_of(*column.shape)], wide, place_ref, gain, code, weights[0], column
    )
    gathered = with_sibling(jnp.stack([column] + flipped))
    planes, lanes = grid[0], grid[1] * grid[2]
    payload, solved, mid_code, coarse_code = call(
        partial(second_kernel, sizes, grid), 37,
        [shape_of(half, TILE), small, shape_of(planes, 1, lanes), shape_of(1, planes * lanes // 8)],
        wide * 2 + near * 2 + mid_scratch(grid),
        place_ref, *gathered, gain, code, solved,
        near_gain, near_code, source, *weights, limit=32,
    )
    column = jnp.stack([payload] + along_z(payload))
    gathered = with_sibling(jnp.stack([column] + across(column)))
    result = call(
        partial(third_kernel, sizes, grid), 18,
        shape_of(MODES, BLOCK),
        near * 2 + mid_scratch(grid),
        place_ref, *gathered, mid_code, coarse_code, near_gain, near_code, solved, *weights,
    )
    return result[None, None, None]


def solution(mesh):
    placed = (
        P("gx", "gy", "gz", None, None),
        P(),
        P(),
        P(),
        P("gx", "gy", "gz", None),
        P("gx", "gy", "gz", None),
        P("gx", "gy", "gz", None),
    )
    sizes = tuple(mesh.shape[a] for a in ("gx", "gy", "gz"))
    wide = sizes[0] == 2 and sizes[1] == 4 and sizes[2] * MY * MZ * 2 == TILE
    return jax.shard_map(
        partial(wide_device, sizes) if wide else per_device,
        mesh=mesh,
        in_specs=placed,
        out_specs=P("gx", "gy", "gz", None, None),
        check_vma=False,
    )
```

```python
from functools import partial

import jax
import jax.numpy as jnp
from jax import lax
from jax.experimental import pallas as pl
from jax.experimental.pallas import tpu as pltpu
from jax.sharding import PartitionSpec as P

MODES = 64
MATERIALS = 4
SWEEPS = 2
COARSE_SWEEPS = 4
CYCLES = 2
CX = 8
CY = 8
CZ = 8


relax_weight = 0.7
restrict_scale = 0.6
highest = lax.Precision.HIGHEST


def padded_2(shard, sides, width):
    for axis, dim in sides:
        size, length = (lax.axis_size(axis), shard.shape[dim])
        up = [(i, (i + 1) % size) for i in range(size - 1)]
        down = [(j, i) for i, j in up]
        last = lax.slice_in_dim(shard, length - width, length, axis=dim)
        first = lax.slice_in_dim(shard, 0, width, axis=dim)
        before = lax.ppermute(last, axis, up)
        after = lax.ppermute(first, axis, down)
        shard = jnp.concatenate([before, shard, after], axis=dim)
    return shard


def inverse_blocks(diag_blocks):
    identity = jnp.eye(MODES, dtype=diag_blocks.dtype)
    result = []
    for material in range(MATERIALS):
        factor = jnp.linalg.cholesky(diag_blocks[material])
        result.append(jax.scipy.linalg.cho_solve((factor, True), identity))
    return jnp.stack(result).reshape(MATERIALS * MODES, MODES)


def coupling_matrix(diag_blocks, face_blocks):
    blocks = jnp.concatenate([diag_blocks[None], face_blocks], axis=0)
    return jnp.transpose(blocks, (1, 2, 0, 3)).reshape(MATERIALS * MODES, 7 * MODES)


def choose_blocks(weights, columns, onehot):
    product = jnp.dot(weights, columns, precision=highest, preferred_element_type=jnp.float32)
    product = product.reshape(MATERIALS, MODES, columns.shape[1])
    return jnp.sum(product * onehot.reshape(MATERIALS, 1, columns.shape[1]), axis=0)


def operate(padded, onehot, coupling):
    centre = padded[:, 1:-1, 1:-1, 1:-1]
    stacked = jnp.concatenate(
        [
            centre,
            padded[:, 2:, 1:-1, 1:-1],
            padded[:, :-2, 1:-1, 1:-1],
            padded[:, 1:-1, 2:, 1:-1],
            padded[:, 1:-1, :-2, 1:-1],
            padded[:, 1:-1, 1:-1, 2:],
            padded[:, 1:-1, 1:-1, :-2],
        ],
        axis=0,
    )
    columns = stacked.reshape(7 * MODES, -1)
    return choose_blocks(coupling, columns, onehot.reshape(MATERIALS, -1)).reshape(centre.shape)


def apply_inverse(inverse, field, onehot):
    return choose_blocks(inverse, field.reshape(MODES, -1), onehot.reshape(MATERIALS, -1)).reshape(
        field.shape
    )


def restrict(field, prolong):
    blocked = field.reshape(
        MODES, field.shape[1] // 2, 2, field.shape[2] // 2, 2, field.shape[3] // 2, 2
    )
    return restrict_scale * jnp.einsum(
        "abcji,jxaybzc->ixyz", prolong.reshape(2, 2, 2, MODES, MODES), blocked, precision=highest
    )


def expand(coarse_field, prolong):
    finer = jnp.einsum(
        "abcji,ixyz->jxaybzc",
        prolong.reshape(2, 2, 2, MODES, MODES),
        coarse_field,
        precision=highest,
    )
    return finer.reshape(
        MODES, 2 * coarse_field.shape[1], 2 * coarse_field.shape[2], 2 * coarse_field.shape[3]
    )


def make_onehot(materials):
    return (materials[None] == jnp.arange(MATERIALS, dtype=jnp.int32)[:, None, None, None]).astype(
        jnp.float32
    )


def fine_border(field):
    return padded_2(field, (("gx", 1), ("gy", 2), ("gz", 3)), 1)


def section_border(field):
    padded = padded_2(field, (("gx", 1), ("gy", 2)), 1)
    return jnp.pad(padded, ((0, 0), (0, 0), (0, 0), (1, 1)))


def smooth(iterate, source, onehot, border, inverse, coupling):
    residual = source - operate(border(iterate), onehot, coupling)
    return iterate + relax_weight * apply_inverse(inverse, residual, onehot)


def coarse_solve(source, onehot, border, inverse, coupling):
    iterate = relax_weight * apply_inverse(inverse, source, onehot)
    for repeat in range(COARSE_SWEEPS - 1):
        iterate = smooth(iterate, source, onehot, border, inverse, coupling)
    return iterate


def middle_cycle(source, onehot, border, inverse, coupling, prolong, coarse_solver):
    iterate = relax_weight * apply_inverse(inverse, source, onehot)
    iterate = smooth(iterate, source, onehot, border, inverse, coupling)
    residual = source - operate(border(iterate), onehot, coupling)
    iterate = iterate + expand(coarse_solver(restrict(residual, prolong)), prolong)
    for repeat in range(SWEEPS):
        iterate = smooth(iterate, source, onehot, border, inverse, coupling)
    return iterate


def single_steps(iterate, actions, source, onehot, inverse, coupling):
    residual = None
    for action in actions:
        if action == "sweep":
            iterate = smooth(iterate, source, onehot, fine_border, inverse, coupling)
        else:
            residual = source - operate(fine_border(iterate), onehot, coupling)
    return (iterate, residual)


def per_device(right_side, diag_blocks, face_blocks, prolong, mats_fine, mats_mid, mats_coarse):
    inverse = inverse_blocks(diag_blocks)
    coupling = coupling_matrix(diag_blocks, face_blocks)
    source = right_side[0, 0, 0].reshape(MODES, CX, CY, CZ)
    onehot_fine = make_onehot(mats_fine[0, 0, 0].reshape(CX, CY, CZ))
    onehot_mid = make_onehot(mats_mid[0, 0, 0].reshape(CX // 2, CY // 2, CZ // 2))
    onehot_coarse = make_onehot(mats_coarse[0, 0, 0].reshape(CX // 4, CY // 4, CZ // 4))
    stepper = partial(
        single_steps, source=source, onehot=onehot_fine, inverse=inverse, coupling=coupling
    )
    iterate = relax_weight * apply_inverse(inverse, source, onehot_fine)
    for cycle_index in range(CYCLES):
        if cycle_index == 0:
            actions = ["sweep"] * (SWEEPS - 1) + ["residual"]
        else:
            actions = ["sweep"] * SWEEPS + ["residual"]
        iterate, residual = stepper(iterate, actions)
        gathered_source = lax.all_gather(restrict(residual, prolong), "gz", axis=3, tiled=True)
        gathered_mid = lax.all_gather(onehot_mid, "gz", axis=3, tiled=True)
        gathered_coarse = lax.all_gather(onehot_coarse, "gz", axis=3, tiled=True)
        local_solver = partial(
            coarse_solve,
            onehot=gathered_coarse,
            border=section_border,
            inverse=inverse,
            coupling=coupling,
        )
        section_field = middle_cycle(
            gathered_source, gathered_mid, section_border, inverse, coupling, prolong, local_solver
        )
        iterate = iterate + expand(
            lax.dynamic_slice_in_dim(section_field, lax.axis_index("gz") * (CZ // 2), CZ // 2, 3),
            prolong,
        )
        iterate, unused_residual = stepper(iterate, ["sweep"] * SWEEPS)
    return iterate.reshape(MODES, CX * CY * CZ)[None, None, None]


HALO = 3 * SWEEPS + SWEEPS - 1
PITCH = CY + 2 * HALO
BLOCK = CX * CY * CZ
TILE = 128
LANES = -(-(PITCH * PITCH) // TILE) * TILE
ROWS = MODES + 8
MX, MY, MZ = CX // 2, CY // 2, CZ // 2
f32 = jnp.float32
bf16 = jnp.bfloat16


def split(value):
    high = value.astype(bf16)
    return high, (value - high.astype(f32)).astype(bf16)


def dot(a, b):
    return jnp.dot(a, b, preferred_element_type=f32)


def iota(shape, dim):
    return lax.broadcasted_iota(jnp.int32, shape, dim)


def where_equal(rows, columns):
    return jnp.where(rows == columns, 1.0, 0.0).astype(bf16)


def place(value, selector):
    high, low = split(value)
    return dot(high, selector) + dot(low, selector)


def pick(product, code, first):
    out = jnp.zeros((MODES, product.shape[1]), f32)
    for m in range(MATERIALS):
        out = jnp.where(code == m + first, product[m * MODES:(m + 1) * MODES], out)
    return out


def stack3(value):
    high, low = split(value)
    return jnp.concatenate([high, low, high], axis=0)


def thirds(value):
    high, low = split(value)
    return jnp.concatenate([high, high, low], axis=1)


def inverse_kernel(pivots, scale, diag, *refs):
    a = diag[...]
    row_id = iota((1, MODES, 1), 1)
    lane_id = iota((1, 1, MODES), 2)
    for k in pivots:
        pivot = 1.0 / a[:, k:k + 1, k:k + 1]
        on_row, on_lane = row_id == k, lane_id == k
        row = jnp.where(on_lane, pivot, a[:, k:k + 1, :] * pivot)
        column = a[:, :, k:k + 1]
        a = jnp.where(on_row, row, jnp.where(on_lane, 0.0, a) - column * row)
    refs[-1][...] = scale * a


def weights_kernel(scaled, diag, face, prolong, wg, wa, wd, wi, wr, wp):
    beside, gains = [], []
    for m in range(MATERIALS):
        faces = jnp.concatenate([face[d, m] for d in (1, 0, 2, 3, 4, 5)], axis=1)
        beside.append(faces)
        gains.append(jnp.dot(scaled[m], faces, precision=highest, preferred_element_type=f32))
    for target, blocks in ((wa, beside), (wg, gains)):
        high, low = split(jnp.concatenate(blocks, axis=0))
        target[...] = jnp.concatenate([high, low, high], axis=1)
    wd[...] = thirds(jnp.concatenate([diag[m] for m in range(MATERIALS)], axis=0))
    wi[...] = thirds(jnp.concatenate([scaled[m] for m in range(MATERIALS)], axis=0))
    for p in range(2):
        wr[p] = thirds(jnp.concatenate([restrict_scale * prolong[p * 4 + c].T for c in range(4)], axis=0))
    wp[...] = thirds(jnp.concatenate([prolong[c] for c in range(8)], axis=0))


def invert_part(pivots, scale, blocks, *after):
    kernel = partial(inverse_kernel, pivots, scale)
    return call(kernel, 3, shape_of(*blocks.shape), [], blocks, *after, unread=len(after))


def make_weights(scaled, diag_blocks, face_blocks, prolong):
    rows = MATERIALS * MODES
    shapes = [(rows, 18 * MODES)] * 2 + [(rows, 3 * MODES)] * 2
    shapes += [(2, 4 * MODES, 3 * MODES), (8 * MODES, 3 * MODES)]
    shapes = [jax.ShapeDtypeStruct(shape, bf16) for shape in shapes]
    return call(weights_kernel, 1, shapes, [], scaled, diag_blocks, face_blocks, prolong)


SHALLOW = SWEEPS
FIRST_PIVOTS = MODES // 2
PAIRS = CX
SLOT = CY * CZ


def layer_rows(depth, halo):
    return CY + 2 * (halo - depth)


SHALLOW_LANES = sum(layer_rows(d, SHALLOW) for d in range(1, SHALLOW + 1))
DEEP_LANES = sum(layer_rows(d, HALO) for d in range(1, HALO + 1))
PER_TILE = TILE // (2 * SHALLOW_LANES)
SHALLOW_TILES = -(-PAIRS // PER_TILE)


def layer_of(index, first, last, halo):
    depth, start, at = jnp.full_like(index, first), jnp.zeros_like(index), 0
    for d in range(first + 1, last + 1):
        at += layer_rows(d - 1, halo)
        inside = index >= at
        depth, start = jnp.where(inside, d, depth), jnp.where(inside, at, start)
    return depth, index - start - (halo - depth)


def lane_of(depth, y, first, last, halo):
    start, at = jnp.zeros_like(depth), 0
    for d in range(first + 1, last + 1):
        at += layer_rows(d - 1, halo)
        start = jnp.where(depth == d, at, start)
    inside = (depth >= first) & (depth <= last) & (y >= depth - halo) & (y < CY + halo - depth)
    return jnp.where(inside, start + y + halo - depth, -(1 << 20))


def prepare_kernel(place_ref, values, other, materials, other_materials, half_way, out):
    mine = place_ref[0]
    for half, (block, kinds) in enumerate(((values, materials), (other, other_materials))):
        first = (mine ^ half) * (BLOCK // TILE)
        codes = jnp.broadcast_to((kinds[...] + 1).astype(f32), (ROWS - MODES, BLOCK))
        for tile in range(BLOCK // TILE):
            lanes = slice(tile * TILE, (tile + 1) * TILE)
            out[first + tile, :MODES] = block[:, lanes]
            out[first + tile, MODES:] = codes[:, lanes]


def swap_tile(y, odd):
    place = (y + CY) // CY
    return jnp.where(place == 1, 1, jnp.where(place // 2 == odd, 2, 0))


def pack_kernel(place_ref, own, first, second, scaled, thin_first, thin_second, thick_first, thick_second):
    column = iota((1, 4 * TILE), 1)
    lane, kind = column % TILE, column // TILE
    row = iota((3 * TILE, 4 * TILE), 0)
    odd_y, odd_z = place_ref[1] & 1, place_ref[2] & 1
    parts = [jnp.concatenate([r[pair] for r in (first, own, second)], axis=1) for pair in range(PAIRS)]
    parts = split(jnp.concatenate(parts, axis=0))
    shallow = 0.0
    for odd in range(2):
        thin = lane - odd * SHALLOW_LANES
        thin_depth, thin_y = layer_of(thin, 1, SHALLOW, SHALLOW)
        thick_depth, thick_y = layer_of(lane, 1, HALO, HALO)
        depth = jnp.where(kind < 2, thin_depth, thick_depth)
        y = jnp.where(kind < 2, thin_y, thick_y)
        valid = jnp.where(
            kind < 2,
            jnp.where((thin >= 0) & (thin < SHALLOW_LANES), 1, 0),
            jnp.where(lane < DEEP_LANES, 1, 0),
        )
        z = jnp.where(kind % 2 == odd_z, CZ - depth, depth - 1)
        source = swap_tile(y, odd_y) * TILE + ((y + CY) % CY) * CZ + z + odd * SLOT
        selector = where_equal(row, jnp.where(valid == 1, source, -1))
        packed = dot(parts[0], selector) + dot(parts[1], selector)
        shallow = shallow + packed[:, :2 * TILE]
        for pair in range(PAIRS):
            rows = packed[pair * ROWS:(pair + 1) * ROWS]
            thick_first[2 * pair + odd], thick_second[2 * pair + odd] = rows[:, 2 * TILE:3 * TILE], rows[:, 3 * TILE:]
    for tile in range(SHALLOW_TILES):
        for kind, out in enumerate((thin_first, thin_second)):
            strip = 0.0
            for slot in range(PER_TILE):
                pair = tile * PER_TILE + slot
                if pair < PAIRS:
                    piece = shallow[pair * ROWS:(pair + 1) * ROWS, kind * TILE:(kind + 1) * TILE]
                    strip = strip + (pltpu.roll(piece, slot * 2 * SHALLOW_LANES, 1) if slot else piece)
            out[tile] = strip


def shallow_strip(first, second, pair):
    tile, slot = pair // PER_TILE, pair % PER_TILE
    shift = (TILE - slot * 2 * SHALLOW_LANES) % TILE
    lane = iota((1, TILE), 1)
    return jnp.where(
        lane < TILE // 2,
        pltpu.roll(first[tile], shift, 1),
        pltpu.roll(second[tile], (shift + TILE // 2) % TILE, 1),
    )


def in_grid(place_ref, sizes, y, z):
    whole_y, whole_z = y + place_ref[1] * CY, z + place_ref[2] * CZ
    return (whole_y >= 0) & (whole_y < sizes[1] * CY) & (whole_z >= 0) & (whole_z < sizes[2] * CZ)


def unpack(layout, sizes, place_ref, own, along_y, along_z, start, pairs, put, shallow):
    lane = iota((1, layout.lanes), 1)
    y, z = layout.place(lane)
    odd_y, odd_z = place_ref[1] & 1, place_ref[2] & 1
    inner = swap_tile(y, odd_y) * TILE + ((y + CY) % CY) * CZ + z
    depth = jnp.where(z < 0, -z, z - (CZ - 1))
    middle = (z >= 0) & (z < CZ)
    strip = jnp.where(jnp.where(z < 0, 0, 1) == odd_z, 1, 0)
    if shallow:
        outer = lane_of(depth, y, 1, SHALLOW, SHALLOW) + 3 * TILE + strip * (TILE // 2)
        step = SHALLOW_LANES
    else:
        outer = lane_of(depth, y, 1, HALO, HALO) + (3 + strip) * TILE
        step = 0
    row = iota(((4 if shallow else 5) * TILE, layout.lanes), 0)
    valid = (lane < layout.used) & in_grid(place_ref, sizes, y, z)
    parts = []
    for odd in range(2):
        if odd == 0 or not shallow:
            parts = []
            for i in range(pairs):
                pair = start + i
                line = [r[pair] for r in (along_y[0], own, along_y[1])]
                line += [shallow_strip(*along_z, pair)] if shallow else [r[2 * pair + odd] for r in along_z]
                parts.append(jnp.concatenate(line, axis=1))
            parts = split(jnp.concatenate(parts, axis=0))
        source = jnp.where(middle, inner + odd * SLOT, outer + odd * step)
        selector = where_equal(row, jnp.where(valid, source, -1))
        placed = dot(parts[0], selector) + dot(parts[1], selector)
        for i in range(pairs):
            rows = placed[i * ROWS:(i + 1) * ROWS]
            put(2 * (start + i) + odd, rows[:MODES], rows[MODES:MODES + 1])


class Field:
    def __init__(self, full, high, low, shifts, masks=(None,) * 4):
        self.full, self.high, self.low = full, high, low
        self.shifts, self.masks = shifts, masks

    def put(self, x, value):
        self.full[x + 1] = value
        self.high[x + 1], self.low[x + 1] = split(value)

    def put_parts(self, x, high, low):
        self.full[x + 1] = high + low
        self.high[x + 1], self.low[x + 1] = high.astype(bf16), low.astype(bf16)

    def clear_ends(self):
        planes = self.full.shape[0]
        for x in (0, planes - 1):
            self.full[x] = jnp.zeros(self.full.shape[1:], f32)
            self.high[x] = jnp.zeros(self.full.shape[1:], bf16)
            self.low[x] = jnp.zeros(self.full.shape[1:], bf16)

    def get(self, x):
        return self.full[x + 1]


def field_scratch(planes, lanes):
    shape = (planes + 2, MODES, lanes)
    return [pltpu.VMEM(shape, f32), pltpu.VMEM(shape, bf16), pltpu.VMEM(shape, bf16)]


class Layout:
    def __init__(self, halo, lanes):
        self.halo, self.lanes, self.pitch = halo, lanes, CY + 2 * halo
        self.used = self.pitch * self.pitch
        self.factor = -(-(1 << 16) // self.pitch)

    def place(self, lane):
        y = (lane * self.factor) >> 16
        return y - self.halo, lane - y * self.pitch - self.halo

    def parity(self):
        y, z = self.place(iota((1, self.lanes), 1))
        return (y & 1) * 2 + (z & 1)

    def shifts(self):
        return (self.lanes - self.pitch, self.pitch, self.lanes - 1, 1)

    def field(self, refs):
        return Field(*refs, self.shifts())

    def own_lanes(self, lane):
        y, z = self.place(lane)
        return y, z, (lane < self.used) & (y >= 0) & (y < CY) & (z >= 0) & (z < CZ)


def lanes_for(halo):
    return -(-((CY + 2 * halo) ** 2) // TILE) * TILE


NEAR = 2 * SWEEPS
wide_layout = Layout(HALO, lanes_for(HALO))
near_layout = Layout(NEAR, lanes_for(NEAR))


def near_selector():
    y, z = near_layout.place(iota((1, near_layout.lanes), 1))
    source = (y + HALO) * PITCH + z + HALO
    source = jnp.where(iota((1, near_layout.lanes), 1) < near_layout.used, source, -1)
    return where_equal(iota((LANES, near_layout.lanes), 0), source)


def coupled_rows(centre, field, x):
    moved = []
    for shift, mask in zip(field.shifts, field.masks):
        part = pltpu.roll(centre, shift, 1)
        moved.append(part if mask is None else jnp.where(mask, part, 0.0))
    high, low = split(jnp.concatenate(moved, axis=0))
    high = [field.high[x], field.high[x + 2], high]
    low = [field.low[x], field.low[x + 2], low]
    return jnp.concatenate(high + high + low, axis=0)


def grouped(start, count, size, body):
    groups = -(-count // size)
    length = -(-count // groups)
    if groups == 1:
        body(start, count)
        return

    def step(i, carry):
        body(start + jnp.minimum(i * length, count - length), length)
        return carry

    lax.fori_loop(0, groups, step, 0)


def group_size(lanes):
    return 7 if lanes > 2 * TILE else 6


def sweep(source, target, start, count, wg, gain, code, store=None, size=None):
    def body(first, length):
        values = []
        for x in [first + j for j in range(length)]:
            centre = source.get(x)
            product = dot(wg[...], coupled_rows(centre, source, x))
            values.append((1.0 - relax_weight) * centre + gain[x] - pick(product, code[x], 1))
        for j, value in enumerate(values):
            (store or target.put)(first + j, value)

    grouped(start, count, size or group_size(source.full.shape[2]), body)


def residual(field, x, source, wa, wd, code):
    centre = field.get(x)
    applied = dot(wa[...], coupled_rows(centre, field, x)) + dot(wd[...], stack3(centre))
    return source - pick(applied, code, 1)


def restrict_plane(wr, residuals, parity):
    out = 0.0
    for p in range(2):
        out = out + pick(dot(wr[p], stack3(residuals[p])), parity, 0)
    return out


def expand_planes(wp, raised_high, raised_low, parity):
    product = dot(wp[...], jnp.concatenate([raised_high, raised_low, raised_high], axis=0))
    return [pick(product[p * 4 * MODES:(p + 1) * 4 * MODES], parity, 0) for p in range(2)]


def gather_mid(place_ref, here, sibling, sizes, put):
    n_gx, n_gy, n_gz = sizes
    per = MX * MY * MZ
    lines = MY * n_gz * MZ
    column = iota((1, n_gz * 2 * per), 1)
    k, rest = column % MZ, column // MZ
    gz, rest = rest % n_gz, rest // n_gz
    j, rest = rest % MY, rest // MY
    i, h = rest % MX, rest // MX
    source = gz * 2 * per + h * per + (i * MY + j) * MZ + k
    selector = where_equal(iota((n_gz * 2 * per, n_gz * 2 * per), 0), source)
    rows = here.shape[2]
    my_x, my_y, my_z = place_ref[0], place_ref[1], place_ref[2]
    parts = []
    for gx in range(n_gx):
        for gy in range(n_gy):
            slot = ((gx ^ my_x) & 1) + 2 * (((gy ^ my_y) >> 1) & 1)
            line = []
            for gz in range(n_gz):
                turn = my_z ^ gz
                line.append(jnp.where(((gy ^ my_y) & 1) == 0, here[slot, turn], sibling[slot, turn]))
            parts.append(jnp.concatenate(line, axis=1))
    placed = place(jnp.concatenate(parts, axis=0), selector)
    lower = iota((1, TILE), 1) < lines
    for gx in range(n_gx):
        for i in range(MX):
            quarters = []
            for h in range(2):
                tiles = []
                for pair in range(n_gy // 2):
                    block = [placed[(gx * n_gy + 2 * pair + s) * rows:][:rows] for s in range(2)]
                    at = ((h * MX + i) * lines) // TILE * TILE
                    block = [b[:, at:at + TILE] for b in block]
                    if i % 2 == 0:
                        block[1] = pltpu.roll(block[1], lines, 1)
                    else:
                        block[0] = pltpu.roll(block[0], lines, 1)
                    tiles.append(jnp.where(lower, block[0], block[1]))
                quarters.append(jnp.concatenate(tiles, axis=1))
            put(gx * MX + i, quarters)


class Coarse:
    def __init__(self, grid):
        self.x, self.y, self.z = (size // 2 for size in grid)
        self.plane = self.y * self.z
        self.lanes = self.x * self.plane

    def place(self, lane):
        return lane // self.plane, lane // self.z % self.y, lane % self.z

    def solve(self, value, wg, wi, code):
        x, y, z = self.place(iota((1, self.lanes), 1))
        gain = pick(dot(wi[...], stack3(value)), code, 1)
        moves = (
            (self.plane, x > 0), (self.lanes - self.plane, x < self.x - 1),
            (self.lanes - self.z, y < self.y - 1), (self.z, y > 0),
            (self.lanes - 1, z < self.z - 1), (1, z > 0),
        )

        def step(repeat, iterate):
            moved = [jnp.where(mask, pltpu.roll(iterate, shift, 1), 0.0) for shift, mask in moves]
            high, low = split(jnp.concatenate(moved, axis=0))
            product = dot(wg[...], jnp.concatenate([high, high, low], axis=0))
            return (1.0 - relax_weight) * iterate + gain - pick(product, code, 1)

        return lax.fori_loop(0, COARSE_SWEEPS - 1, step, gain)


def solve_mid(source, gain, code, coarse_source, coarse_code, fields, weights, grid):
    wg, wa, wd, wi, wr, wp = weights
    planes, size_y, size_z = grid
    lanes = size_y * size_z
    coarse = Coarse(grid)
    for i in range(2):
        fields(i).clear_ends()

    def begin(first, length):
        values = [pick(dot(wi[...], stack3(source[first + j])), code[first + j], 1) for j in range(length)]
        for j, value in enumerate(values):
            gain[first + j] = value
            fields(0).put(first + j, value)

    grouped(0, planes, 4, begin)
    lane = iota((1, lanes), 1)
    y, z = lane // size_z, lane % size_z
    parity = (y % 2) * 2 + z % 2
    tall, wide = iota((lanes, TILE), 0), iota((lanes, TILE), 1)
    squeeze = (tall // size_z // 2) * coarse.z + tall % size_z // 2
    per_tile = TILE // coarse.plane
    target = (y // 2) * coarse.z + z // 2
    row = iota((coarse.lanes, lanes), 0)

    def correct(field):
        def down(tile, carry):
            total = 0.0
            for part in range(per_tile):
                x = 2 * (tile * per_tile + part)
                rests = [residual(field, x + p, source[x + p], wa, wd, code[x + p]) for p in range(2)]
                selector = where_equal(squeeze + part * coarse.plane, wide)
                total = total + place(restrict_plane(wr, rests, parity), selector)
            coarse_source[:, pl.ds(pl.multiple_of(tile * TILE, TILE), TILE)] = total
            return carry

        lax.fori_loop(0, coarse.lanes // TILE, down, 0)
        result = coarse.solve(coarse_source[...], wg, wi, coarse_code[...])
        parts = jnp.concatenate(split(result), axis=0)

        def up(step, carry):
            for pair in (2 * step, 2 * step + 1):
                raised = dot(parts, where_equal(row, target + pair * coarse.plane)).astype(bf16)
                for p, value in enumerate(expand_planes(wp, raised[:MODES], raised[MODES:], parity)):
                    field.put(2 * pair + p, field.get(2 * pair + p) + value)
            return carry

        lax.fori_loop(0, coarse.x // 2, up, 0)

    def step(i, carry):
        sweep(fields(i % 2), fields(1 - i % 2), 0, planes, wg, gain, code, size=planes)

        @pl.when(i == SWEEPS - 2)
        def _():
            correct(fields(1 - i % 2))

        return carry

    lax.fori_loop(0, 2 * SWEEPS - 1, step, 0)
    return fields((2 * SWEEPS - 1) % 2)


def add_mid(place_ref, layout, result, field, depth, wp, grid, old):
    planes, size_y, size_z = grid
    gx, gy, gz = place_ref[0], place_ref[1], place_ref[2]
    lane = iota((1, layout.lanes), 1)
    y, z = layout.place(lane)
    whole_y, whole_z = y + gy * CY, z + gz * CZ
    inside = (lane < layout.used) & (whole_y >= 0) & (whole_y < 2 * size_y) & (whole_z >= 0) & (whole_z < 2 * size_z)
    target = jnp.where(inside, (whole_y >> 1) * size_z + (whole_z >> 1), -1)
    raise_lanes = where_equal(iota((size_y * size_z, layout.lanes), 0), target)
    parity = layout.parity()

    def body(first, length):
        values = []
        for x in [first + j for j in range(length)]:
            parts = jnp.concatenate([result.high[x + 1], result.low[x + 1]], axis=0)
            raised = dot(parts, raise_lanes).astype(bf16)
            for p, value in enumerate(expand_planes(wp, raised[:MODES], raised[MODES:], parity)):
                values.append(old[2 * x + p] + value)
        for j, value in enumerate(values):
            field.put(2 * first + j, value)

    grouped(gx * ((CX - depth) // 2), (CX + depth) // 2, max(group_size(layout.lanes) // 3, 1), body)


def fine_residual(field, own, source, wr, wa, wd, code):
    layout = near_layout
    tall, wide = iota((layout.lanes, TILE), 0), iota((layout.lanes, TILE), 1)
    y, z, inside = layout.own_lanes(tall)
    target = jnp.where(inside, (y >> 1) * MZ + (z >> 1), -BLOCK)
    per = MX * MY * MZ
    index = wide % per
    parity = layout.parity()
    def add(step, total):
        for i in (2 * step, 2 * step + 1):
            x = own + 2 * i
            rests = [residual(field, x + p, source[2 * i + p], wa, wd, code[x + p]) for p in range(2)]
            total = total + place(restrict_plane(wr, rests, parity), where_equal(target + i * MY * MZ, index))
        return total

    total = lax.fori_loop(0, MX // 2, add, jnp.zeros((MODES, TILE), f32))
    half = MODES // 2
    return jnp.where(iota((1, TILE), 1) < per, total[:half], total[half:])


def near_kernel(sizes, place_ref, own, y0, y1, z0, z1, wg, wa, wd, wi, wr, wp, source, payload, *scratch):
    layout = near_layout
    first, second = layout.field(scratch[0:3]), layout.field(scratch[3:6])
    whole, gain, code = scratch[6:9]
    first.clear_ends()
    second.clear_ends()
    gx = place_ref[0]

    def put(x, value, material):
        whole[x], code[x] = value, material

    start, pairs = gx * ((CX - SHALLOW) // 2), (CX + SHALLOW) // 2
    unpack(layout, sizes, place_ref, own, (y0, y1), (z0, z1), start, pairs, put, True)

    def begin(start, length):
        values = [pick(dot(wi[...], stack3(whole[start + j])), code[start + j], 1) for j in range(length)]
        for j, value in enumerate(values):
            gain[start + j] = value
            first.put(start + j, value)

    grouped(gx * (CX - SHALLOW), CX + SHALLOW, group_size(layout.lanes), begin)
    depth = SHALLOW - 1
    sweep(first, second, gx * (CX - depth), CX + depth, wg, gain, code)
    mine = gx * CX
    source[...] = whole[pl.ds(mine, CX)]
    payload[...] = fine_residual(second, mine, source, wr, wa, wd, code)


def gain_kernel(sizes, place_ref, own, y0, y1, z0, z1, wi, payload, gain, code, near_gain, near_code, passed, whole):
    def put(x, value, material):
        whole[x], code[x] = value, material

    unpack(wide_layout, sizes, place_ref, own, (y0, y1), (z0, z1), 0, PAIRS, put, False)
    to_near = near_selector()

    def begin(start, length):
        values = [pick(dot(wi[...], stack3(whole[start + j])), code[start + j], 1) for j in range(length)]
        for j, value in enumerate(values):
            gain[start + j] = value
            near_gain[start + j] = place(value, to_near)
        for j in range(length):
            near_code[start + j] = dot(jnp.broadcast_to(code[start + j], (8, LANES)).astype(bf16), to_near)[:1]

    grouped(0, 2 * CX, 4, begin)
    passed[...] = payload[...]


def deep_kernel(place_ref, gain, code, wg, column, solved, passed, *scratch):
    passed[...] = column[...]
    first = wide_layout.field(scratch)
    first.clear_ends()
    for x in range(2 * CX):
        first.put(x, gain[x])
    depth = HALO - 1
    gx = place_ref[0]

    def store(x, value):
        solved[x] = value

    sweep(first, None, gx * (CX - depth), CX + depth, wg, gain, code, store)


def mid_scratch(grid):
    planes, size_y, size_z = grid
    lanes = size_y * size_z
    both = [pltpu.VMEM((2,) + ref.shape, ref.dtype) for ref in field_scratch(planes, lanes)]
    return both + [pltpu.VMEM((planes, MODES, lanes), f32)] * 2 + [pltpu.VMEM((MODES, planes * lanes // 8), f32)]


def run_mid(place_ref, here, sibling, sizes, grid, weights, scratch, mid_code, coarse_code, read_codes):
    planes, size_y, size_z = grid
    lanes = size_y * size_z
    lane = iota((1, lanes), 1)
    y, z = lane // size_z, lane % size_z
    shifts = (lanes - size_z, size_z, lanes - 1, 1)
    masks = (y < size_y - 1, y > 0, z < size_z - 1, z > 0)
    source, gain, coarse_source = scratch[3:6]

    def fields(i):
        return Field(*(ref.at[i] for ref in scratch[0:3]), shifts, masks)

    half = MODES // 2
    coarse = Coarse(grid)
    corners = []

    def put(x, quarters):
        source[x, :half] = quarters[0][:half]
        source[x, half:] = quarters[1][:half]
        if read_codes:
            mid_code[x] = quarters[0][half:half + 1]
            if x % 2 == 0:
                corners.append(jnp.broadcast_to(quarters[1][half:half + 1], (8, lanes)).astype(bf16))

    gather_mid(place_ref, here, sibling, sizes, put)
    if read_codes:
        tall, wide = iota((lanes, coarse.lanes), 0), iota((lanes, coarse.lanes), 1)
        x, cy, cz = coarse.place(wide)
        total = 0.0
        for pair in range(coarse.x):
            selector = where_equal(jnp.where(x == pair, 2 * cy * size_z + 2 * cz, -1), tall)
            total = total + dot(corners[pair], selector)
        coarse_code[...] = total[:1]
    return solve_mid(source, gain, mid_code, coarse_source, coarse_code, fields, weights, grid)


def second_kernel(sizes, grid, place_ref, here, sibling, gain, code, solved, near_gain, near_code, source,
                  wg, wa, wd, wi, wr, wp, payload, result, mid_code, coarse_code, *scratch):
    weights = (wg, wa, wd, wi, wr, wp)
    answer = run_mid(place_ref, here, sibling, sizes, grid, weights, scratch[12:], mid_code, coarse_code, True)
    first, second = wide_layout.field(scratch[0:3]), wide_layout.field(scratch[3:6])
    now, other = near_layout.field(scratch[6:9]), near_layout.field(scratch[9:12])
    for field in (first, second, now, other):
        field.clear_ends()
    depth = 3 * SWEEPS
    gx = place_ref[0]
    add_mid(place_ref, wide_layout, answer, first, depth, wp, grid, solved)
    to_near = near_selector()

    def narrow(x, value):
        parts = dot(jnp.concatenate(split(value), axis=0), to_near)
        now.put_parts(x, parts[:MODES], parts[MODES:])

    for repeat in range(2 * SWEEPS):
        depth -= 1
        start, count = gx * (CX - depth), CX + depth
        if depth > NEAR:
            sweep(first, second, start, count, wg, gain, code)
            first, second = second, first
        elif depth == NEAR:
            sweep(first, None, start, count, wg, gain, code, narrow)
        else:
            sweep(now, other, start, count, wg, near_gain, near_code)
            now, other = other, now
    payload[...] = fine_residual(now, gx * CX, source, wr, wa, wd, near_code)
    result[...] = now.full[1:1 + 2 * CX]


def third_kernel(sizes, grid, place_ref, here, sibling, mid_code, coarse_code, near_gain, near_code, solved,
                 wg, wa, wd, wi, wr, wp, result, *scratch):
    weights = (wg, wa, wd, wi, wr, wp)
    answer = run_mid(place_ref, here, sibling, sizes, grid, weights, scratch[6:], mid_code, coarse_code, False)
    layout = near_layout
    now, other = layout.field(scratch[0:3]), layout.field(scratch[3:6])
    now.clear_ends()
    other.clear_ends()
    depth = SWEEPS
    gx = place_ref[0]
    add_mid(place_ref, layout, answer, now, depth, wp, grid, solved)
    for repeat in range(SWEEPS):
        depth -= 1
        sweep(now, other, gx * (CX - depth), CX + depth, wg, near_gain, near_code)
        now, other = other, now
    tall, wide = iota((layout.lanes, TILE), 0), iota((layout.lanes, TILE), 1)
    y, z, inside = layout.own_lanes(tall)
    target = jnp.where(inside, y * CZ + z, -BLOCK)
    selectors = [where_equal(target + odd * CY * CZ, wide) for odd in range(2)]
    for pair in range(CX // 2):
        total = 0.0
        for odd in range(2):
            value = now.get(gx * CX + 2 * pair + odd)
            high, low = split(value)
            lowest = (value - high.astype(f32) - low.astype(f32)).astype(bf16)
            for part in (high, low, lowest):
                total = total + dot(part, selectors[odd])
        result[:, pair * TILE:(pair + 1) * TILE] = total


def call(kernel, cost_us, out_shape, scratch, *args, limit=16, unread=0):
    vmem, smem = pl.BlockSpec(memory_space=pltpu.VMEM), pl.BlockSpec(memory_space=pltpu.SMEM)
    specs = [smem if a.dtype == jnp.int32 and a.ndim == 1 else vmem for a in args[:len(args) - unread]]
    specs += [pl.BlockSpec(memory_space=pl.ANY)] * unread
    cost = pl.CostEstimate(flops=int(cost_us * 1e9), bytes_accessed=int(cost_us * 3e6), transcendentals=0)
    return pl.pallas_call(
        kernel,
        out_shape=out_shape,
        in_specs=specs,
        out_specs=jax.tree.map(lambda s: vmem, out_shape),
        scratch_shapes=scratch,
        cost_estimate=cost,
        compiler_params=pltpu.CompilerParams(vmem_limit_bytes=limit * 1024 * 1024),
    )(*args)


def shape_of(*dims):
    return jax.ShapeDtypeStruct(dims, f32)


def wide_device(sizes, right_side, diag_blocks, face_blocks, prolong, mats_fine, mats_mid, mats_coarse):
    n_gx, n_gy, n_gz = sizes
    axes = ("gx", "gy", "gz")
    grid = (n_gx * MX, n_gy * MY, n_gz * MZ)
    place_ref = jnp.stack([lax.axis_index(a) for a in axes]).astype(jnp.int32)
    tiles = BLOCK // TILE
    values, kinds = right_side.reshape(MODES, BLOCK), mats_fine.reshape(1, BLOCK)
    swap = [(0, 1), (1, 0)]
    others = lax.ppermute(values, "gx", swap), lax.ppermute(kinds, "gx", swap)
    half_way = invert_part(range(FIRST_PIVOTS), 1.0, diag_blocks)
    own = call(
        prepare_kernel, 0.5, shape_of(2 * tiles, ROWS, TILE), [],
        place_ref, values, others[0], kinds, others[1], half_way, unread=1,
    )
    swaps = {}
    for axis, n in zip(axes, sizes):
        inner = [pair for i in range(1, n - 1, 2) for pair in ((i, i + 1), (i + 1, i))]
        swaps[axis] = [(i, i ^ 1) for i in range(n)], [(0, 0)] + inner + [(n - 1, n - 1)]
    along_y = [lax.ppermute(own, "gy", swap) for swap in swaps["gy"]]
    scaled = invert_part(range(FIRST_PIVOTS, MODES), relax_weight, half_way, own)
    weights = make_weights(scaled, diag_blocks, face_blocks, prolong)
    thin, thick = shape_of(SHALLOW_TILES, ROWS, TILE), shape_of(2 * PAIRS, ROWS, TILE)
    send = call(pack_kernel, 1.5, [thin, thin, thick, thick], [], place_ref, own, *along_y, scaled, unread=1)
    shallow = [lax.ppermute(value, "gz", swap) for value, swap in zip(send[:2], swaps["gz"])]
    deep = [lax.ppermute(value, "gz", swap) for value, swap in zip(send[2:], swaps["gz"])]

    wide = field_scratch(2 * CX, LANES)
    near = field_scratch(2 * CX, near_layout.lanes)
    half, per = MODES // 2, MX * MY * MZ
    whole = shape_of(2 * CX, MODES, LANES)
    small = shape_of(2 * CX, MODES, near_layout.lanes)
    small_code = shape_of(2 * CX, 1, near_layout.lanes)
    source, payload = call(
        partial(near_kernel, sizes), 7,
        [shape_of(CX, MODES, near_layout.lanes), shape_of(half, TILE)],
        near * 2 + [pltpu.VMEM(s.shape, f32) for s in (small, small, small_code)],
        place_ref, own, *along_y, *shallow, *weights,
    )
    mid = (mats_mid.reshape(per) + 1).astype(f32)
    coarse = (mats_coarse.reshape(MX // 2, 1, MY // 2, 1, MZ // 2, 1) + 1).astype(f32)
    coarse = jnp.broadcast_to(coarse, (MX // 2, 2, MY // 2, 2, MZ // 2, 2)).reshape(per)
    tail = jnp.broadcast_to(jnp.concatenate([mid, coarse])[None], (8, TILE))

    def along_z(value):
        turns = [[(i, i ^ s) for i in range(n_gz)] for s in range(1, n_gz)]
        return [lax.ppermute(value, "gz", turn) for turn in turns]

    def across(column):
        flips = [
            [(i * n_gy + j, (i ^ dx) * n_gy + (j ^ dy)) for i in range(n_gx) for j in range(n_gy)]
            for dx, dy in ((1, 0), (0, 2), (1, 2))
        ]
        return [lax.ppermute(column, ("gx", "gy"), flip) for flip in flips]

    def with_sibling(here):
        return here, lax.ppermute(here, "gy", [(j, j ^ 1) for j in range(n_gy)])

    payload = jnp.concatenate([payload, tail], axis=0)
    turned = along_z(payload)
    gain, code, near_gain, near_code, payload = call(
        partial(gain_kernel, sizes), 6,
        [whole, shape_of(2 * CX, 1, LANES), small, small_code, shape_of(*payload.shape)],
        [pltpu.VMEM(whole.shape, f32)],
        place_ref, own, *along_y, *deep, weights[3], payload,
    )
    column = jnp.stack([payload] + turned)
    flipped = across(column)
    solved, column = call(
        deep_kernel, 7, [whole, shape_of(*column.shape)], wide, place_ref, gain, code, weights[0], column
    )
    gathered = with_sibling(jnp.stack([column] + flipped))
    planes, lanes = grid[0], grid[1] * grid[2]
    payload, solved, mid_code, coarse_code = call(
        partial(second_kernel, sizes, grid), 37,
        [shape_of(half, TILE), small, shape_of(planes, 1, lanes), shape_of(1, planes * lanes // 8)],
        wide * 2 + near * 2 + mid_scratch(grid),
        place_ref, *gathered, gain, code, solved,
        near_gain, near_code, source, *weights, limit=32,
    )
    column = jnp.stack([payload] + along_z(payload))
    gathered = with_sibling(jnp.stack([column] + across(column)))
    result = call(
        partial(third_kernel, sizes, grid), 18,
        shape_of(MODES, BLOCK),
        near * 2 + mid_scratch(grid),
        place_ref, *gathered, mid_code, coarse_code, near_gain, near_code, solved, *weights,
    )
    return result[None, None, None]


def solution(mesh):
    placed = (
        P("gx", "gy", "gz", None, None),
        P(),
        P(),
        P(),
        P("gx", "gy", "gz", None),
        P("gx", "gy", "gz", None),
        P("gx", "gy", "gz", None),
    )
    sizes = tuple(mesh.shape[a] for a in ("gx", "gy", "gz"))
    wide = sizes[0] == 2 and sizes[1] == 4 and sizes[2] * MY * MZ * 2 == TILE
    return jax.shard_map(
        partial(wide_device, sizes) if wide else per_device,
        mesh=mesh,
        in_specs=placed,
        out_specs=P("gx", "gy", "gz", None, None),
        check_vma=False,
    )
```

```python
from functools import partial

import jax
import jax.numpy as jnp
from jax import lax
from jax.experimental import pallas as pl
from jax.experimental.pallas import tpu as pltpu
from jax.sharding import PartitionSpec as P

MODES = 64
MATERIALS = 4
SWEEPS = 2
COARSE_SWEEPS = 4
CYCLES = 2
CX = 8
CY = 8
CZ = 8


relax_weight = 0.7
restrict_scale = 0.6
highest = lax.Precision.HIGHEST


def padded_2(shard, sides, width):
    for axis, dim in sides:
        size, length = (lax.axis_size(axis), shard.shape[dim])
        up = [(i, (i + 1) % size) for i in range(size - 1)]
        down = [(j, i) for i, j in up]
        last = lax.slice_in_dim(shard, length - width, length, axis=dim)
        first = lax.slice_in_dim(shard, 0, width, axis=dim)
        before = lax.ppermute(last, axis, up)
        after = lax.ppermute(first, axis, down)
        shard = jnp.concatenate([before, shard, after], axis=dim)
    return shard


def inverse_blocks(diag_blocks):
    identity = jnp.eye(MODES, dtype=diag_blocks.dtype)
    result = []
    for material in range(MATERIALS):
        factor = jnp.linalg.cholesky(diag_blocks[material])
        result.append(jax.scipy.linalg.cho_solve((factor, True), identity))
    return jnp.stack(result).reshape(MATERIALS * MODES, MODES)


def coupling_matrix(diag_blocks, face_blocks):
    blocks = jnp.concatenate([diag_blocks[None], face_blocks], axis=0)
    return jnp.transpose(blocks, (1, 2, 0, 3)).reshape(MATERIALS * MODES, 7 * MODES)


def choose_blocks(weights, columns, onehot):
    product = jnp.dot(weights, columns, precision=highest, preferred_element_type=jnp.float32)
    product = product.reshape(MATERIALS, MODES, columns.shape[1])
    return jnp.sum(product * onehot.reshape(MATERIALS, 1, columns.shape[1]), axis=0)


def operate(padded, onehot, coupling):
    centre = padded[:, 1:-1, 1:-1, 1:-1]
    stacked = jnp.concatenate(
        [
            centre,
            padded[:, 2:, 1:-1, 1:-1],
            padded[:, :-2, 1:-1, 1:-1],
            padded[:, 1:-1, 2:, 1:-1],
            padded[:, 1:-1, :-2, 1:-1],
            padded[:, 1:-1, 1:-1, 2:],
            padded[:, 1:-1, 1:-1, :-2],
        ],
        axis=0,
    )
    columns = stacked.reshape(7 * MODES, -1)
    return choose_blocks(coupling, columns, onehot.reshape(MATERIALS, -1)).reshape(centre.shape)


def apply_inverse(inverse, field, onehot):
    return choose_blocks(inverse, field.reshape(MODES, -1), onehot.reshape(MATERIALS, -1)).reshape(
        field.shape
    )


def restrict(field, prolong):
    blocked = field.reshape(
        MODES, field.shape[1] // 2, 2, field.shape[2] // 2, 2, field.shape[3] // 2, 2
    )
    return restrict_scale * jnp.einsum(
        "abcji,jxaybzc->ixyz", prolong.reshape(2, 2, 2, MODES, MODES), blocked, precision=highest
    )


def expand(coarse_field, prolong):
    finer = jnp.einsum(
        "abcji,ixyz->jxaybzc",
        prolong.reshape(2, 2, 2, MODES, MODES),
        coarse_field,
        precision=highest,
    )
    return finer.reshape(
        MODES, 2 * coarse_field.shape[1], 2 * coarse_field.shape[2], 2 * coarse_field.shape[3]
    )


def make_onehot(materials):
    return (materials[None] == jnp.arange(MATERIALS, dtype=jnp.int32)[:, None, None, None]).astype(
        jnp.float32
    )


def fine_border(field):
    return padded_2(field, (("gx", 1), ("gy", 2), ("gz", 3)), 1)


def section_border(field):
    padded = padded_2(field, (("gx", 1), ("gy", 2)), 1)
    return jnp.pad(padded, ((0, 0), (0, 0), (0, 0), (1, 1)))


def smooth(iterate, source, onehot, border, inverse, coupling):
    residual = source - operate(border(iterate), onehot, coupling)
    return iterate + relax_weight * apply_inverse(inverse, residual, onehot)


def coarse_solve(source, onehot, border, inverse, coupling):
    iterate = relax_weight * apply_inverse(inverse, source, onehot)
    for repeat in range(COARSE_SWEEPS - 1):
        iterate = smooth(iterate, source, onehot, border, inverse, coupling)
    return iterate


def middle_cycle(source, onehot, border, inverse, coupling, prolong, coarse_solver):
    iterate = relax_weight * apply_inverse(inverse, source, onehot)
    iterate = smooth(iterate, source, onehot, border, inverse, coupling)
    residual = source - operate(border(iterate), onehot, coupling)
    iterate = iterate + expand(coarse_solver(restrict(residual, prolong)), prolong)
    for repeat in range(SWEEPS):
        iterate = smooth(iterate, source, onehot, border, inverse, coupling)
    return iterate


def single_steps(iterate, actions, source, onehot, inverse, coupling):
    residual = None
    for action in actions:
        if action == "sweep":
            iterate = smooth(iterate, source, onehot, fine_border, inverse, coupling)
        else:
            residual = source - operate(fine_border(iterate), onehot, coupling)
    return (iterate, residual)


def per_device(right_side, diag_blocks, face_blocks, prolong, mats_fine, mats_mid, mats_coarse):
    inverse = inverse_blocks(diag_blocks)
    coupling = coupling_matrix(diag_blocks, face_blocks)
    source = right_side[0, 0, 0].reshape(MODES, CX, CY, CZ)
    onehot_fine = make_onehot(mats_fine[0, 0, 0].reshape(CX, CY, CZ))
    onehot_mid = make_onehot(mats_mid[0, 0, 0].reshape(CX // 2, CY // 2, CZ // 2))
    onehot_coarse = make_onehot(mats_coarse[0, 0, 0].reshape(CX // 4, CY // 4, CZ // 4))
    stepper = partial(
        single_steps, source=source, onehot=onehot_fine, inverse=inverse, coupling=coupling
    )
    iterate = relax_weight * apply_inverse(inverse, source, onehot_fine)
    for cycle_index in range(CYCLES):
        if cycle_index == 0:
            actions = ["sweep"] * (SWEEPS - 1) + ["residual"]
        else:
            actions = ["sweep"] * SWEEPS + ["residual"]
        iterate, residual = stepper(iterate, actions)
        gathered_source = lax.all_gather(restrict(residual, prolong), "gz", axis=3, tiled=True)
        gathered_mid = lax.all_gather(onehot_mid, "gz", axis=3, tiled=True)
        gathered_coarse = lax.all_gather(onehot_coarse, "gz", axis=3, tiled=True)
        local_solver = partial(
            coarse_solve,
            onehot=gathered_coarse,
            border=section_border,
            inverse=inverse,
            coupling=coupling,
        )
        section_field = middle_cycle(
            gathered_source, gathered_mid, section_border, inverse, coupling, prolong, local_solver
        )
        iterate = iterate + expand(
            lax.dynamic_slice_in_dim(section_field, lax.axis_index("gz") * (CZ // 2), CZ // 2, 3),
            prolong,
        )
        iterate, unused_residual = stepper(iterate, ["sweep"] * SWEEPS)
    return iterate.reshape(MODES, CX * CY * CZ)[None, None, None]


HALO = 3 * SWEEPS + SWEEPS - 1
PITCH = CY + 2 * HALO
BLOCK = CX * CY * CZ
TILE = 128
LANES = -(-(PITCH * PITCH) // TILE) * TILE
ROWS = MODES + 8
MX, MY, MZ = CX // 2, CY // 2, CZ // 2
f32 = jnp.float32
bf16 = jnp.bfloat16


def split(value):
    high = value.astype(bf16)
    return high, (value - high.astype(f32)).astype(bf16)


def dot(a, b):
    return jnp.dot(a, b, preferred_element_type=f32)


def iota(shape, dim):
    return lax.broadcasted_iota(jnp.int32, shape, dim)


def where_equal(rows, columns):
    return jnp.where(rows == columns, 1.0, 0.0).astype(bf16)


def place(value, selector):
    high, low = split(value)
    return dot(high, selector) + dot(low, selector)


def pick(product, code, first):
    out = jnp.zeros((MODES, product.shape[1]), f32)
    for m in range(MATERIALS):
        out = jnp.where(code == m + first, product[m * MODES:(m + 1) * MODES], out)
    return out


def stack3(value):
    high, low = split(value)
    return jnp.concatenate([high, low, high], axis=0)


def thirds(value):
    high, low = split(value)
    return jnp.concatenate([high, high, low], axis=1)


def inverse_kernel(pivots, scale, diag, *refs):
    a = diag[...]
    row_id = iota((1, MODES, 1), 1)
    lane_id = iota((1, 1, MODES), 2)
    for k in pivots:
        pivot = 1.0 / a[:, k:k + 1, k:k + 1]
        on_row, on_lane = row_id == k, lane_id == k
        row = jnp.where(on_lane, pivot, a[:, k:k + 1, :] * pivot)
        column = a[:, :, k:k + 1]
        a = jnp.where(on_row, row, jnp.where(on_lane, 0.0, a) - column * row)
    refs[-1][...] = scale * a


def weights_kernel(scaled, diag, face, prolong, wg, wa, wd, wi, wr, wp):
    beside, gains = [], []
    for m in range(MATERIALS):
        faces = jnp.concatenate([face[d, m] for d in (1, 0, 2, 3, 4, 5)], axis=1)
        beside.append(faces)
        gains.append(jnp.dot(scaled[m], faces, precision=highest, preferred_element_type=f32))
    for target, blocks in ((wa, beside), (wg, gains)):
        high, low = split(jnp.concatenate(blocks, axis=0))
        target[...] = jnp.concatenate([high, low, high], axis=1)
    wd[...] = thirds(jnp.concatenate([diag[m] for m in range(MATERIALS)], axis=0))
    wi[...] = thirds(jnp.concatenate([scaled[m] for m in range(MATERIALS)], axis=0))
    for p in range(2):
        wr[p] = thirds(jnp.concatenate([restrict_scale * prolong[p * 4 + c].T for c in range(4)], axis=0))
    wp[...] = thirds(jnp.concatenate([prolong[c] for c in range(8)], axis=0))


def invert_part(pivots, scale, blocks, *after):
    kernel = partial(inverse_kernel, pivots, scale)
    return call(kernel, 3, shape_of(*blocks.shape), [], blocks, *after, unread=len(after))


def make_weights(scaled, diag_blocks, face_blocks, prolong):
    rows = MATERIALS * MODES
    shapes = [(rows, 18 * MODES)] * 2 + [(rows, 3 * MODES)] * 2
    shapes += [(2, 4 * MODES, 3 * MODES), (8 * MODES, 3 * MODES)]
    shapes = [jax.ShapeDtypeStruct(shape, bf16) for shape in shapes]
    return call(weights_kernel, 1, shapes, [], scaled, diag_blocks, face_blocks, prolong)


SHALLOW = SWEEPS
FIRST_PIVOTS = MODES // 2
PAIRS = CX
THICK = CX + HALO - 1
SLOT = CY * CZ


def layer_rows(depth, halo):
    return CY + 2 * (halo - depth)


SHALLOW_LANES = sum(layer_rows(d, SHALLOW) for d in range(1, SHALLOW + 1))
DEEP_LANES = sum(layer_rows(d, HALO) for d in range(1, HALO + 1))
PER_TILE = TILE // (2 * SHALLOW_LANES)
SHALLOW_TILES = -(-(THICK // 2) // PER_TILE)


def layer_of(index, first, last, halo):
    depth, start, at = jnp.full_like(index, first), jnp.zeros_like(index), 0
    for d in range(first + 1, last + 1):
        at += layer_rows(d - 1, halo)
        inside = index >= at
        depth, start = jnp.where(inside, d, depth), jnp.where(inside, at, start)
    return depth, index - start - (halo - depth)


def lane_of(depth, y, first, last, halo):
    start, at = jnp.zeros_like(depth), 0
    for d in range(first + 1, last + 1):
        at += layer_rows(d - 1, halo)
        start = jnp.where(depth == d, at, start)
    inside = (depth >= first) & (depth <= last) & (y >= depth - halo) & (y < CY + halo - depth)
    return jnp.where(inside, start + y + halo - depth, -(1 << 20))


def prepare_kernel(place_ref, values, other, materials, other_materials, half_way, out):
    mine = place_ref[0]
    for half, (block, kinds) in enumerate(((values, materials), (other, other_materials))):
        first = (mine ^ half) * (BLOCK // TILE)
        codes = jnp.broadcast_to((kinds[...] + 1).astype(f32), (ROWS - MODES, BLOCK))
        for tile in range(BLOCK // TILE):
            lanes = slice(tile * TILE, (tile + 1) * TILE)
            out[first + tile, :MODES] = block[:, lanes]
            out[first + tile, MODES:] = codes[:, lanes]


def swap_tile(y, odd):
    place = (y + CY) // CY
    return jnp.where(place == 1, 1, jnp.where(place // 2 == odd, 2, 0))


def pairs_skipped(place_ref):
    return place_ref[0] * ((2 * CX - THICK) // 2)


def pack_kernel(place_ref, own, first, second, scaled, thin_first, thin_second, thick_first, thick_second):
    column = iota((1, 4 * TILE), 1)
    lane, kind = column % TILE, column // TILE
    row = iota((3 * TILE, 4 * TILE), 0)
    odd_y, odd_z = place_ref[1] & 1, place_ref[2] & 1
    skipped = pairs_skipped(place_ref)
    parts = [
        jnp.concatenate([r[skipped + pair] for r in (first, own, second)], axis=1) for pair in range(THICK // 2)
    ]
    parts = split(jnp.concatenate(parts, axis=0))
    shallow = 0.0
    for odd in range(2):
        thin = lane - odd * SHALLOW_LANES
        thin_depth, thin_y = layer_of(thin, 1, SHALLOW, SHALLOW)
        thick_depth, thick_y = layer_of(lane, 1, HALO, HALO)
        depth = jnp.where(kind < 2, thin_depth, thick_depth)
        y = jnp.where(kind < 2, thin_y, thick_y)
        valid = jnp.where(
            kind < 2,
            jnp.where((thin >= 0) & (thin < SHALLOW_LANES), 1, 0),
            jnp.where(lane < DEEP_LANES, 1, 0),
        )
        z = jnp.where(kind % 2 == odd_z, CZ - depth, depth - 1)
        source = swap_tile(y, odd_y) * TILE + ((y + CY) % CY) * CZ + z + odd * SLOT
        selector = where_equal(row, jnp.where(valid == 1, source, -1))
        packed = dot(parts[0], selector) + dot(parts[1], selector)
        shallow = shallow + packed[:, :2 * TILE]
        for pair in range(THICK // 2):
            rows = packed[pair * ROWS:(pair + 1) * ROWS]
            thick_first[2 * pair + odd], thick_second[2 * pair + odd] = rows[:, 2 * TILE:3 * TILE], rows[:, 3 * TILE:]
    for tile in range(SHALLOW_TILES):
        for kind, out in enumerate((thin_first, thin_second)):
            strip = 0.0
            for slot in range(PER_TILE):
                pair = tile * PER_TILE + slot
                if pair < THICK // 2:
                    piece = shallow[pair * ROWS:(pair + 1) * ROWS, kind * TILE:(kind + 1) * TILE]
                    strip = strip + (pltpu.roll(piece, slot * 2 * SHALLOW_LANES, 1) if slot else piece)
            out[tile] = strip


def shallow_strip(first, second, pair):
    tile, slot = pair // PER_TILE, pair % PER_TILE
    shift = (TILE - slot * 2 * SHALLOW_LANES) % TILE
    lane = iota((1, TILE), 1)
    return jnp.where(
        lane < TILE // 2,
        pltpu.roll(first[tile], shift, 1),
        pltpu.roll(second[tile], (shift + TILE // 2) % TILE, 1),
    )


def in_grid(place_ref, sizes, y, z):
    whole_y, whole_z = y + place_ref[1] * CY, z + place_ref[2] * CZ
    return (whole_y >= 0) & (whole_y < sizes[1] * CY) & (whole_z >= 0) & (whole_z < sizes[2] * CZ)


def unpack(layout, sizes, place_ref, own, along_y, along_z, start, pairs, put, shallow):
    lane = iota((1, layout.lanes), 1)
    y, z = layout.place(lane)
    odd_y, odd_z = place_ref[1] & 1, place_ref[2] & 1
    inner = swap_tile(y, odd_y) * TILE + ((y + CY) % CY) * CZ + z
    depth = jnp.where(z < 0, -z, z - (CZ - 1))
    middle = (z >= 0) & (z < CZ)
    strip = jnp.where(jnp.where(z < 0, 0, 1) == odd_z, 1, 0)
    skipped = pairs_skipped(place_ref)
    if shallow:
        outer = lane_of(depth, y, 1, SHALLOW, SHALLOW) + 3 * TILE + strip * (TILE // 2)
        step = SHALLOW_LANES
    else:
        outer = lane_of(depth, y, 1, HALO, HALO) + (3 + strip) * TILE
        step = 0
    row = iota(((4 if shallow else 5) * TILE, layout.lanes), 0)
    valid = (lane < layout.used) & in_grid(place_ref, sizes, y, z)
    parts = []
    for odd in range(2):
        if odd == 0 or not shallow:
            parts = []
            for i in range(pairs):
                pair = start + i
                line = [r[pair] for r in (along_y[0], own, along_y[1])]
                if shallow:
                    line += [shallow_strip(*along_z, pair - skipped)]
                else:
                    line += [r[jnp.clip(2 * (pair - skipped) + odd, 0, THICK - 1)] for r in along_z]
                parts.append(jnp.concatenate(line, axis=1))
            parts = split(jnp.concatenate(parts, axis=0))
        source = jnp.where(middle, inner + odd * SLOT, outer + odd * step)
        selector = where_equal(row, jnp.where(valid, source, -1))
        placed = dot(parts[0], selector) + dot(parts[1], selector)
        for i in range(pairs):
            rows = placed[i * ROWS:(i + 1) * ROWS]
            put(2 * (start + i) + odd, rows[:MODES], rows[MODES:MODES + 1])


class Field:
    def __init__(self, full, high, low, shifts, masks=(None,) * 4):
        self.full, self.high, self.low = full, high, low
        self.shifts, self.masks = shifts, masks

    def put(self, x, value):
        self.full[x + 1] = value
        self.high[x + 1], self.low[x + 1] = split(value)

    def put_parts(self, x, high, low):
        self.full[x + 1] = high + low
        self.high[x + 1], self.low[x + 1] = high.astype(bf16), low.astype(bf16)

    def clear_ends(self):
        planes = self.full.shape[0]
        for x in (0, planes - 1):
            self.full[x] = jnp.zeros(self.full.shape[1:], f32)
            self.high[x] = jnp.zeros(self.full.shape[1:], bf16)
            self.low[x] = jnp.zeros(self.full.shape[1:], bf16)

    def get(self, x):
        return self.full[x + 1]


def field_scratch(planes, lanes):
    shape = (planes + 2, MODES, lanes)
    return [pltpu.VMEM(shape, f32), pltpu.VMEM(shape, bf16), pltpu.VMEM(shape, bf16)]


class Layout:
    def __init__(self, halo, lanes):
        self.halo, self.lanes, self.pitch = halo, lanes, CY + 2 * halo
        self.used = self.pitch * self.pitch
        self.factor = -(-(1 << 16) // self.pitch)

    def place(self, lane):
        y = (lane * self.factor) >> 16
        return y - self.halo, lane - y * self.pitch - self.halo

    def parity(self):
        y, z = self.place(iota((1, self.lanes), 1))
        return (y & 1) * 2 + (z & 1)

    def shifts(self):
        return (self.lanes - self.pitch, self.pitch, self.lanes - 1, 1)

    def field(self, refs):
        return Field(*refs, self.shifts())

    def own_lanes(self, lane):
        y, z = self.place(lane)
        return y, z, (lane < self.used) & (y >= 0) & (y < CY) & (z >= 0) & (z < CZ)


def lanes_for(halo):
    return -(-((CY + 2 * halo) ** 2) // TILE) * TILE


NEAR = 2 * SWEEPS
wide_layout = Layout(HALO, lanes_for(HALO))
near_layout = Layout(NEAR, lanes_for(NEAR))


def near_selector():
    y, z = near_layout.place(iota((1, near_layout.lanes), 1))
    source = (y + HALO) * PITCH + z + HALO
    source = jnp.where(iota((1, near_layout.lanes), 1) < near_layout.used, source, -1)
    return where_equal(iota((LANES, near_layout.lanes), 0), source)


def coupled_rows(centre, field, x):
    moved = []
    for shift, mask in zip(field.shifts, field.masks):
        part = pltpu.roll(centre, shift, 1)
        moved.append(part if mask is None else jnp.where(mask, part, 0.0))
    high, low = split(jnp.concatenate(moved, axis=0))
    high = [field.high[x], field.high[x + 2], high]
    low = [field.low[x], field.low[x + 2], low]
    return jnp.concatenate(high + high + low, axis=0)


def grouped(start, count, size, body):
    groups = -(-count // size)
    length = -(-count // groups)
    if groups == 1:
        body(start, count)
        return

    def step(i, carry):
        body(start + jnp.minimum(i * length, count - length), length)
        return carry

    lax.fori_loop(0, groups, step, 0)


def group_size(lanes):
    return 7 if lanes > 2 * TILE else 6


def sweep(source, target, start, count, wg, gain, code, store=None, size=None):
    def body(first, length):
        values = []
        for x in [first + j for j in range(length)]:
            centre = source.get(x)
            product = dot(wg[...], coupled_rows(centre, source, x))
            values.append((1.0 - relax_weight) * centre + gain[x] - pick(product, code[x], 1))
        for j, value in enumerate(values):
            (store or target.put)(first + j, value)

    grouped(start, count, size or group_size(source.full.shape[2]), body)


def residual(field, x, source, wa, wd, code):
    centre = field.get(x)
    applied = dot(wa[...], coupled_rows(centre, field, x)) + dot(wd[...], stack3(centre))
    return source - pick(applied, code, 1)


def restrict_plane(wr, residuals, parity):
    out = 0.0
    for p in range(2):
        out = out + pick(dot(wr[p], stack3(residuals[p])), parity, 0)
    return out


def expand_planes(wp, raised_high, raised_low, parity):
    product = dot(wp[...], jnp.concatenate([raised_high, raised_low, raised_high], axis=0))
    return [pick(product[p * 4 * MODES:(p + 1) * 4 * MODES], parity, 0) for p in range(2)]


def gather_mid(place_ref, here, sibling, sizes, put):
    n_gx, n_gy, n_gz = sizes
    per = MX * MY * MZ
    lines = MY * n_gz * MZ
    column = iota((1, n_gz * 2 * per), 1)
    k, rest = column % MZ, column // MZ
    gz, rest = rest % n_gz, rest // n_gz
    j, rest = rest % MY, rest // MY
    i, h = rest % MX, rest // MX
    source = gz * 2 * per + h * per + (i * MY + j) * MZ + k
    selector = where_equal(iota((n_gz * 2 * per, n_gz * 2 * per), 0), source)
    rows = here.shape[2]
    my_x, my_y, my_z = place_ref[0], place_ref[1], place_ref[2]
    parts = []
    for gx in range(n_gx):
        for gy in range(n_gy):
            slot = ((gx ^ my_x) & 1) + 2 * (((gy ^ my_y) >> 1) & 1)
            line = []
            for gz in range(n_gz):
                turn = my_z ^ gz
                line.append(jnp.where(((gy ^ my_y) & 1) == 0, here[slot, turn], sibling[slot, turn]))
            parts.append(jnp.concatenate(line, axis=1))
    placed = place(jnp.concatenate(parts, axis=0), selector)
    lower = iota((1, TILE), 1) < lines
    for gx in range(n_gx):
        for i in range(MX):
            quarters = []
            for h in range(2):
                tiles = []
                for pair in range(n_gy // 2):
                    block = [placed[(gx * n_gy + 2 * pair + s) * rows:][:rows] for s in range(2)]
                    at = ((h * MX + i) * lines) // TILE * TILE
                    block = [b[:, at:at + TILE] for b in block]
                    if i % 2 == 0:
                        block[1] = pltpu.roll(block[1], lines, 1)
                    else:
                        block[0] = pltpu.roll(block[0], lines, 1)
                    tiles.append(jnp.where(lower, block[0], block[1]))
                quarters.append(jnp.concatenate(tiles, axis=1))
            put(gx * MX + i, quarters)


class Coarse:
    def __init__(self, grid):
        self.x, self.y, self.z = (size // 2 for size in grid)
        self.plane = self.y * self.z
        self.lanes = self.x * self.plane

    def place(self, lane):
        return lane // self.plane, lane // self.z % self.y, lane % self.z

    def solve(self, value, wg, wi, code):
        x, y, z = self.place(iota((1, self.lanes), 1))
        gain = pick(dot(wi[...], stack3(value)), code, 1)
        moves = (
            (self.plane, x > 0), (self.lanes - self.plane, x < self.x - 1),
            (self.lanes - self.z, y < self.y - 1), (self.z, y > 0),
            (self.lanes - 1, z < self.z - 1), (1, z > 0),
        )

        def step(repeat, iterate):
            moved = [jnp.where(mask, pltpu.roll(iterate, shift, 1), 0.0) for shift, mask in moves]
            high, low = split(jnp.concatenate(moved, axis=0))
            product = dot(wg[...], jnp.concatenate([high, high, low], axis=0))
            return (1.0 - relax_weight) * iterate + gain - pick(product, code, 1)

        return lax.fori_loop(0, COARSE_SWEEPS - 1, step, gain)


def solve_mid(source, gain, code, coarse_source, coarse_code, fields, weights, grid):
    wg, wa, wd, wi, wr, wp = weights
    planes, size_y, size_z = grid
    lanes = size_y * size_z
    coarse = Coarse(grid)
    for i in range(2):
        fields(i).clear_ends()

    def begin(first, length):
        values = [pick(dot(wi[...], stack3(source[first + j])), code[first + j], 1) for j in range(length)]
        for j, value in enumerate(values):
            gain[first + j] = value
            fields(0).put(first + j, value)

    grouped(0, planes, 4, begin)
    lane = iota((1, lanes), 1)
    y, z = lane // size_z, lane % size_z
    parity = (y % 2) * 2 + z % 2
    tall, wide = iota((lanes, TILE), 0), iota((lanes, TILE), 1)
    squeeze = (tall // size_z // 2) * coarse.z + tall % size_z // 2
    per_tile = TILE // coarse.plane
    target = (y // 2) * coarse.z + z // 2
    row = iota((coarse.lanes, lanes), 0)

    def correct(field):
        def down(tile, carry):
            total = 0.0
            for part in range(per_tile):
                x = 2 * (tile * per_tile + part)
                rests = [residual(field, x + p, source[x + p], wa, wd, code[x + p]) for p in range(2)]
                selector = where_equal(squeeze + part * coarse.plane, wide)
                total = total + place(restrict_plane(wr, rests, parity), selector)
            coarse_source[:, pl.ds(pl.multiple_of(tile * TILE, TILE), TILE)] = total
            return carry

        lax.fori_loop(0, coarse.lanes // TILE, down, 0)
        result = coarse.solve(coarse_source[...], wg, wi, coarse_code[...])
        parts = jnp.concatenate(split(result), axis=0)

        def up(step, carry):
            for pair in (2 * step, 2 * step + 1):
                raised = dot(parts, where_equal(row, target + pair * coarse.plane)).astype(bf16)
                for p, value in enumerate(expand_planes(wp, raised[:MODES], raised[MODES:], parity)):
                    field.put(2 * pair + p, field.get(2 * pair + p) + value)
            return carry

        lax.fori_loop(0, coarse.x // 2, up, 0)

    def step(i, carry):
        sweep(fields(i % 2), fields(1 - i % 2), 0, planes, wg, gain, code, size=planes)

        @pl.when(i == SWEEPS - 2)
        def _():
            correct(fields(1 - i % 2))

        return carry

    lax.fori_loop(0, 2 * SWEEPS - 1, step, 0)
    return fields((2 * SWEEPS - 1) % 2)


def add_mid(place_ref, layout, result, field, depth, wp, grid, old):
    planes, size_y, size_z = grid
    gx, gy, gz = place_ref[0], place_ref[1], place_ref[2]
    lane = iota((1, layout.lanes), 1)
    y, z = layout.place(lane)
    whole_y, whole_z = y + gy * CY, z + gz * CZ
    inside = (lane < layout.used) & (whole_y >= 0) & (whole_y < 2 * size_y) & (whole_z >= 0) & (whole_z < 2 * size_z)
    target = jnp.where(inside, (whole_y >> 1) * size_z + (whole_z >> 1), -1)
    raise_lanes = where_equal(iota((size_y * size_z, layout.lanes), 0), target)
    parity = layout.parity()

    def body(first, length):
        values = []
        for x in [first + j for j in range(length)]:
            parts = jnp.concatenate([result.high[x + 1], result.low[x + 1]], axis=0)
            raised = dot(parts, raise_lanes).astype(bf16)
            for p, value in enumerate(expand_planes(wp, raised[:MODES], raised[MODES:], parity)):
                values.append(old[2 * x + p] + value)
        for j, value in enumerate(values):
            field.put(2 * first + j, value)

    pairs = (CX + depth) // 2
    grouped(gx * ((CX - depth) // 2), pairs, -(-pairs // 2), body)


def fine_residual(field, own, source, wr, wa, wd, code):
    layout = near_layout
    tall, wide = iota((layout.lanes, TILE), 0), iota((layout.lanes, TILE), 1)
    y, z, inside = layout.own_lanes(tall)
    target = jnp.where(inside, (y >> 1) * MZ + (z >> 1), -BLOCK)
    per = MX * MY * MZ
    index = wide % per
    parity = layout.parity()
    def add(step, total):
        for i in (2 * step, 2 * step + 1):
            x = own + 2 * i
            rests = [residual(field, x + p, source[2 * i + p], wa, wd, code[x + p]) for p in range(2)]
            total = total + place(restrict_plane(wr, rests, parity), where_equal(target + i * MY * MZ, index))
        return total

    total = lax.fori_loop(0, MX // 2, add, jnp.zeros((MODES, TILE), f32))
    half = MODES // 2
    return jnp.where(iota((1, TILE), 1) < per, total[:half], total[half:])


def near_kernel(sizes, place_ref, own, y0, y1, z0, z1, wg, wa, wd, wi, wr, wp, source, payload, *scratch):
    layout = near_layout
    first, second = layout.field(scratch[0:3]), layout.field(scratch[3:6])
    whole, gain, code = scratch[6:9]
    first.clear_ends()
    second.clear_ends()
    gx = place_ref[0]

    def put(x, value, material):
        whole[x], code[x] = value, material

    start, pairs = gx * ((CX - SHALLOW) // 2), (CX + SHALLOW) // 2
    unpack(layout, sizes, place_ref, own, (y0, y1), (z0, z1), start, pairs, put, True)

    def begin(start, length):
        values = [pick(dot(wi[...], stack3(whole[start + j])), code[start + j], 1) for j in range(length)]
        for j, value in enumerate(values):
            gain[start + j] = value
            first.put(start + j, value)

    grouped(gx * (CX - SHALLOW), CX + SHALLOW, group_size(layout.lanes), begin)
    depth = SHALLOW - 1
    sweep(first, second, gx * (CX - depth), CX + depth, wg, gain, code)
    mine = gx * CX
    source[...] = whole[pl.ds(mine, CX)]
    payload[...] = fine_residual(second, mine, source, wr, wa, wd, code)


def gain_kernel(sizes, place_ref, own, y0, y1, z0, z1, wi, payload, gain, code, near_gain, near_code, passed, whole):
    def put(x, value, material):
        whole[x], code[x] = value, material

    unpack(wide_layout, sizes, place_ref, own, (y0, y1), (z0, z1), 0, PAIRS, put, False)
    to_near = near_selector()

    def begin(start, length):
        values = [pick(dot(wi[...], stack3(whole[start + j])), code[start + j], 1) for j in range(length)]
        for j, value in enumerate(values):
            gain[start + j] = value
            near_gain[start + j] = place(value, to_near)
        for j in range(length):
            near_code[start + j] = dot(jnp.broadcast_to(code[start + j], (8, LANES)).astype(bf16), to_near)[:1]

    grouped(0, 2 * CX, 4, begin)
    passed[...] = payload[...]


def deep_kernel(place_ref, gain, code, wg, column, solved, passed, *scratch):
    passed[...] = column[...]
    first = wide_layout.field(scratch)
    first.clear_ends()
    for x in range(2 * CX):
        first.put(x, gain[x])
    depth = HALO - 1
    gx = place_ref[0]

    def store(x, value):
        solved[x] = value

    sweep(first, None, gx * (CX - depth), CX + depth, wg, gain, code, store)


def mid_scratch(grid):
    planes, size_y, size_z = grid
    lanes = size_y * size_z
    both = [pltpu.VMEM((2,) + ref.shape, ref.dtype) for ref in field_scratch(planes, lanes)]
    return both + [pltpu.VMEM((planes, MODES, lanes), f32)] * 2 + [pltpu.VMEM((MODES, planes * lanes // 8), f32)]


def run_mid(place_ref, here, sibling, sizes, grid, weights, scratch, mid_code, coarse_code, read_codes):
    planes, size_y, size_z = grid
    lanes = size_y * size_z
    lane = iota((1, lanes), 1)
    y, z = lane // size_z, lane % size_z
    shifts = (lanes - size_z, size_z, lanes - 1, 1)
    masks = (y < size_y - 1, y > 0, z < size_z - 1, z > 0)
    source, gain, coarse_source = scratch[3:6]

    def fields(i):
        return Field(*(ref.at[i] for ref in scratch[0:3]), shifts, masks)

    half = MODES // 2
    coarse = Coarse(grid)
    corners = []

    def put(x, quarters):
        source[x, :half] = quarters[0][:half]
        source[x, half:] = quarters[1][:half]
        if read_codes:
            mid_code[x] = quarters[0][half:half + 1]
            if x % 2 == 0:
                corners.append(jnp.broadcast_to(quarters[1][half:half + 1], (8, lanes)).astype(bf16))

    gather_mid(place_ref, here, sibling, sizes, put)
    if read_codes:
        tall, wide = iota((lanes, coarse.lanes), 0), iota((lanes, coarse.lanes), 1)
        x, cy, cz = coarse.place(wide)
        total = 0.0
        for pair in range(coarse.x):
            selector = where_equal(jnp.where(x == pair, 2 * cy * size_z + 2 * cz, -1), tall)
            total = total + dot(corners[pair], selector)
        coarse_code[...] = total[:1]
    return solve_mid(source, gain, mid_code, coarse_source, coarse_code, fields, weights, grid)


def second_kernel(sizes, grid, place_ref, here, sibling, gain, code, solved, near_gain, near_code, source,
                  wg, wa, wd, wi, wr, wp, payload, result, mid_code, coarse_code, *scratch):
    weights = (wg, wa, wd, wi, wr, wp)
    answer = run_mid(place_ref, here, sibling, sizes, grid, weights, scratch[12:], mid_code, coarse_code, True)
    first, second = wide_layout.field(scratch[0:3]), wide_layout.field(scratch[3:6])
    now, other = near_layout.field(scratch[6:9]), near_layout.field(scratch[9:12])
    for field in (first, second, now, other):
        field.clear_ends()
    depth = 3 * SWEEPS
    gx = place_ref[0]
    add_mid(place_ref, wide_layout, answer, first, depth, wp, grid, solved)
    to_near = near_selector()

    def narrow(x, value):
        parts = dot(jnp.concatenate(split(value), axis=0), to_near)
        now.put_parts(x, parts[:MODES], parts[MODES:])

    for repeat in range(2 * SWEEPS):
        depth -= 1
        start, count = gx * (CX - depth), CX + depth
        if depth > NEAR:
            sweep(first, second, start, count, wg, gain, code)
            first, second = second, first
        elif depth == NEAR:
            sweep(first, None, start, count, wg, gain, code, narrow)
        else:
            def store(x, value, target=other):
                target.put(x, value)
                if depth == SWEEPS:
                    result[x] = value

            sweep(now, other, start, count, wg, near_gain, near_code, store)
            now, other = other, now
    payload[...] = fine_residual(now, gx * CX, source, wr, wa, wd, near_code)


def third_kernel(sizes, grid, place_ref, here, sibling, mid_code, coarse_code, near_gain, near_code, solved,
                 wg, wa, wd, wi, wr, wp, result, *scratch):
    weights = (wg, wa, wd, wi, wr, wp)
    answer = run_mid(place_ref, here, sibling, sizes, grid, weights, scratch[6:], mid_code, coarse_code, False)
    layout = near_layout
    now, other = layout.field(scratch[0:3]), layout.field(scratch[3:6])
    now.clear_ends()
    other.clear_ends()
    depth = SWEEPS
    gx = place_ref[0]
    add_mid(place_ref, layout, answer, now, depth, wp, grid, solved)
    for repeat in range(SWEEPS):
        depth -= 1
        sweep(now, other, gx * (CX - depth), CX + depth, wg, near_gain, near_code)
        now, other = other, now
    tall, wide = iota((layout.lanes, TILE), 0), iota((layout.lanes, TILE), 1)
    y, z, inside = layout.own_lanes(tall)
    target = jnp.where(inside, y * CZ + z, -BLOCK)
    selectors = [where_equal(target + odd * CY * CZ, wide) for odd in range(2)]
    for pair in range(CX // 2):
        total = 0.0
        for odd in range(2):
            value = now.get(gx * CX + 2 * pair + odd)
            high, low = split(value)
            lowest = (value - high.astype(f32) - low.astype(f32)).astype(bf16)
            for part in (high, low, lowest):
                total = total + dot(part, selectors[odd])
        result[:, pair * TILE:(pair + 1) * TILE] = total


def call(kernel, cost_us, out_shape, scratch, *args, limit=16, unread=0):
    vmem, smem = pl.BlockSpec(memory_space=pltpu.VMEM), pl.BlockSpec(memory_space=pltpu.SMEM)
    specs = [smem if a.dtype == jnp.int32 and a.ndim == 1 else vmem for a in args[:len(args) - unread]]
    specs += [pl.BlockSpec(memory_space=pl.ANY)] * unread
    cost = pl.CostEstimate(flops=int(cost_us * 1e9), bytes_accessed=int(cost_us * 3e6), transcendentals=0)
    return pl.pallas_call(
        kernel,
        out_shape=out_shape,
        in_specs=specs,
        out_specs=jax.tree.map(lambda s: vmem, out_shape),
        scratch_shapes=scratch,
        cost_estimate=cost,
        compiler_params=pltpu.CompilerParams(vmem_limit_bytes=limit * 1024 * 1024),
    )(*args)


def shape_of(*dims):
    return jax.ShapeDtypeStruct(dims, f32)


def wide_device(sizes, right_side, diag_blocks, face_blocks, prolong, mats_fine, mats_mid, mats_coarse):
    n_gx, n_gy, n_gz = sizes
    axes = ("gx", "gy", "gz")
    grid = (n_gx * MX, n_gy * MY, n_gz * MZ)
    place_ref = jnp.stack([lax.axis_index(a) for a in axes]).astype(jnp.int32)
    tiles = BLOCK // TILE
    values, kinds = right_side.reshape(MODES, BLOCK), mats_fine.reshape(1, BLOCK)
    swap = [(0, 1), (1, 0)]
    others = lax.ppermute(values, "gx", swap), lax.ppermute(kinds, "gx", swap)
    half_way = invert_part(range(FIRST_PIVOTS), 1.0, diag_blocks)
    own = call(
        prepare_kernel, 0.5, shape_of(2 * tiles, ROWS, TILE), [],
        place_ref, values, others[0], kinds, others[1], half_way, unread=1,
    )
    swaps = {}
    for axis, n in zip(axes, sizes):
        inner = [pair for i in range(1, n - 1, 2) for pair in ((i, i + 1), (i + 1, i))]
        swaps[axis] = [(i, i ^ 1) for i in range(n)], [(0, 0)] + inner + [(n - 1, n - 1)]
    along_y = [lax.ppermute(own, "gy", swap) for swap in swaps["gy"]]
    scaled = invert_part(range(FIRST_PIVOTS, MODES), relax_weight, half_way, own)
    weights = make_weights(scaled, diag_blocks, face_blocks, prolong)
    thin, thick = shape_of(SHALLOW_TILES, ROWS, TILE), shape_of(THICK, ROWS, TILE)
    send = call(pack_kernel, 1.5, [thin, thin, thick, thick], [], place_ref, own, *along_y, scaled, unread=1)
    shallow = [lax.ppermute(value, "gz", swap) for value, swap in zip(send[:2], swaps["gz"])]
    deep = [lax.ppermute(value, "gz", swap) for value, swap in zip(send[2:], swaps["gz"])]

    wide = field_scratch(2 * CX, LANES)
    near = field_scratch(2 * CX, near_layout.lanes)
    half, per = MODES // 2, MX * MY * MZ
    whole = shape_of(2 * CX, MODES, LANES)
    small = shape_of(2 * CX, MODES, near_layout.lanes)
    small_code = shape_of(2 * CX, 1, near_layout.lanes)
    source, payload = call(
        partial(near_kernel, sizes), 7,
        [shape_of(CX, MODES, near_layout.lanes), shape_of(half, TILE)],
        near * 2 + [pltpu.VMEM(s.shape, f32) for s in (small, small, small_code)],
        place_ref, own, *along_y, *shallow, *weights,
    )
    mid = (mats_mid.reshape(per) + 1).astype(f32)
    coarse = (mats_coarse.reshape(MX // 2, 1, MY // 2, 1, MZ // 2, 1) + 1).astype(f32)
    coarse = jnp.broadcast_to(coarse, (MX // 2, 2, MY // 2, 2, MZ // 2, 2)).reshape(per)
    tail = jnp.broadcast_to(jnp.concatenate([mid, coarse])[None], (8, TILE))

    def along_z(value):
        turns = [[(i, i ^ s) for i in range(n_gz)] for s in range(1, n_gz)]
        return [lax.ppermute(value, "gz", turn) for turn in turns]

    def across(column):
        flips = [
            [(i * n_gy + j, (i ^ dx) * n_gy + (j ^ dy)) for i in range(n_gx) for j in range(n_gy)]
            for dx, dy in ((1, 0), (0, 2), (1, 2))
        ]
        return [lax.ppermute(column, ("gx", "gy"), flip) for flip in flips]

    def with_sibling(here):
        return here, lax.ppermute(here, "gy", [(j, j ^ 1) for j in range(n_gy)])

    payload = jnp.concatenate([payload, tail], axis=0)
    turned = along_z(payload)
    gain, code, near_gain, near_code, payload = call(
        partial(gain_kernel, sizes), 6,
        [whole, shape_of(2 * CX, 1, LANES), small, small_code, shape_of(*payload.shape)],
        [pltpu.VMEM(whole.shape, f32)],
        place_ref, own, *along_y, *deep, weights[3], payload,
    )
    column = jnp.stack([payload] + turned)
    flipped = across(column)
    solved, column = call(
        deep_kernel, 7, [whole, shape_of(*column.shape)], wide, place_ref, gain, code, weights[0], column
    )
    gathered = with_sibling(jnp.stack([column] + flipped))
    planes, lanes = grid[0], grid[1] * grid[2]
    payload, solved, mid_code, coarse_code = call(
        partial(second_kernel, sizes, grid), 37,
        [shape_of(half, TILE), small, shape_of(planes, 1, lanes), shape_of(1, planes * lanes // 8)],
        wide * 2 + near * 2 + mid_scratch(grid),
        place_ref, *gathered, gain, code, solved,
        near_gain, near_code, source, *weights, limit=32,
    )
    column = jnp.stack([payload] + along_z(payload))
    gathered = with_sibling(jnp.stack([column] + across(column)))
    result = call(
        partial(third_kernel, sizes, grid), 18,
        shape_of(MODES, BLOCK),
        near * 2 + mid_scratch(grid),
        place_ref, *gathered, mid_code, coarse_code, near_gain, near_code, solved, *weights,
    )
    return result[None, None, None]


def solution(mesh):
    placed = (
        P("gx", "gy", "gz", None, None),
        P(),
        P(),
        P(),
        P("gx", "gy", "gz", None),
        P("gx", "gy", "gz", None),
        P("gx", "gy", "gz", None),
    )
    sizes = tuple(mesh.shape[a] for a in ("gx", "gy", "gz"))
    wide = sizes[0] == 2 and sizes[1] == 4 and sizes[2] * MY * MZ * 2 == TILE
    return jax.shard_map(
        partial(wide_device, sizes) if wide else per_device,
        mesh=mesh,
        in_specs=placed,
        out_specs=P("gx", "gy", "gz", None, None),
        check_vma=False,
    )
```

```python
from functools import partial

import jax
import jax.numpy as jnp
from jax import lax
from jax.experimental import pallas as pl
from jax.experimental.pallas import tpu as pltpu
from jax.sharding import PartitionSpec as P

MODES = 64
MATERIALS = 4
SWEEPS = 2
COARSE_SWEEPS = 4
CYCLES = 2
CX = 8
CY = 8
CZ = 8


relax_weight = 0.7
restrict_scale = 0.6
highest = lax.Precision.HIGHEST


def padded_2(shard, sides, width):
    for axis, dim in sides:
        size, length = (lax.axis_size(axis), shard.shape[dim])
        up = [(i, (i + 1) % size) for i in range(size - 1)]
        down = [(j, i) for i, j in up]
        last = lax.slice_in_dim(shard, length - width, length, axis=dim)
        first = lax.slice_in_dim(shard, 0, width, axis=dim)
        before = lax.ppermute(last, axis, up)
        after = lax.ppermute(first, axis, down)
        shard = jnp.concatenate([before, shard, after], axis=dim)
    return shard


def inverse_blocks(diag_blocks):
    identity = jnp.eye(MODES, dtype=diag_blocks.dtype)
    result = []
    for material in range(MATERIALS):
        factor = jnp.linalg.cholesky(diag_blocks[material])
        result.append(jax.scipy.linalg.cho_solve((factor, True), identity))
    return jnp.stack(result).reshape(MATERIALS * MODES, MODES)


def coupling_matrix(diag_blocks, face_blocks):
    blocks = jnp.concatenate([diag_blocks[None], face_blocks], axis=0)
    return jnp.transpose(blocks, (1, 2, 0, 3)).reshape(MATERIALS * MODES, 7 * MODES)


def choose_blocks(weights, columns, onehot):
    product = jnp.dot(weights, columns, precision=highest, preferred_element_type=jnp.float32)
    product = product.reshape(MATERIALS, MODES, columns.shape[1])
    return jnp.sum(product * onehot.reshape(MATERIALS, 1, columns.shape[1]), axis=0)


def operate(padded, onehot, coupling):
    centre = padded[:, 1:-1, 1:-1, 1:-1]
    stacked = jnp.concatenate(
        [
            centre,
            padded[:, 2:, 1:-1, 1:-1],
            padded[:, :-2, 1:-1, 1:-1],
            padded[:, 1:-1, 2:, 1:-1],
            padded[:, 1:-1, :-2, 1:-1],
            padded[:, 1:-1, 1:-1, 2:],
            padded[:, 1:-1, 1:-1, :-2],
        ],
        axis=0,
    )
    columns = stacked.reshape(7 * MODES, -1)
    return choose_blocks(coupling, columns, onehot.reshape(MATERIALS, -1)).reshape(centre.shape)


def apply_inverse(inverse, field, onehot):
    return choose_blocks(inverse, field.reshape(MODES, -1), onehot.reshape(MATERIALS, -1)).reshape(
        field.shape
    )


def restrict(field, prolong):
    blocked = field.reshape(
        MODES, field.shape[1] // 2, 2, field.shape[2] // 2, 2, field.shape[3] // 2, 2
    )
    return restrict_scale * jnp.einsum(
        "abcji,jxaybzc->ixyz", prolong.reshape(2, 2, 2, MODES, MODES), blocked, precision=highest
    )


def expand(coarse_field, prolong):
    finer = jnp.einsum(
        "abcji,ixyz->jxaybzc",
        prolong.reshape(2, 2, 2, MODES, MODES),
        coarse_field,
        precision=highest,
    )
    return finer.reshape(
        MODES, 2 * coarse_field.shape[1], 2 * coarse_field.shape[2], 2 * coarse_field.shape[3]
    )


def make_onehot(materials):
    return (materials[None] == jnp.arange(MATERIALS, dtype=jnp.int32)[:, None, None, None]).astype(
        jnp.float32
    )


def fine_border(field):
    return padded_2(field, (("gx", 1), ("gy", 2), ("gz", 3)), 1)


def section_border(field):
    padded = padded_2(field, (("gx", 1), ("gy", 2)), 1)
    return jnp.pad(padded, ((0, 0), (0, 0), (0, 0), (1, 1)))


def smooth(iterate, source, onehot, border, inverse, coupling):
    residual = source - operate(border(iterate), onehot, coupling)
    return iterate + relax_weight * apply_inverse(inverse, residual, onehot)


def coarse_solve(source, onehot, border, inverse, coupling):
    iterate = relax_weight * apply_inverse(inverse, source, onehot)
    for repeat in range(COARSE_SWEEPS - 1):
        iterate = smooth(iterate, source, onehot, border, inverse, coupling)
    return iterate


def middle_cycle(source, onehot, border, inverse, coupling, prolong, coarse_solver):
    iterate = relax_weight * apply_inverse(inverse, source, onehot)
    iterate = smooth(iterate, source, onehot, border, inverse, coupling)
    residual = source - operate(border(iterate), onehot, coupling)
    iterate = iterate + expand(coarse_solver(restrict(residual, prolong)), prolong)
    for repeat in range(SWEEPS):
        iterate = smooth(iterate, source, onehot, border, inverse, coupling)
    return iterate


def single_steps(iterate, actions, source, onehot, inverse, coupling):
    residual = None
    for action in actions:
        if action == "sweep":
            iterate = smooth(iterate, source, onehot, fine_border, inverse, coupling)
        else:
            residual = source - operate(fine_border(iterate), onehot, coupling)
    return (iterate, residual)


def per_device(right_side, diag_blocks, face_blocks, prolong, mats_fine, mats_mid, mats_coarse):
    inverse = inverse_blocks(diag_blocks)
    coupling = coupling_matrix(diag_blocks, face_blocks)
    source = right_side[0, 0, 0].reshape(MODES, CX, CY, CZ)
    onehot_fine = make_onehot(mats_fine[0, 0, 0].reshape(CX, CY, CZ))
    onehot_mid = make_onehot(mats_mid[0, 0, 0].reshape(CX // 2, CY // 2, CZ // 2))
    onehot_coarse = make_onehot(mats_coarse[0, 0, 0].reshape(CX // 4, CY // 4, CZ // 4))
    stepper = partial(
        single_steps, source=source, onehot=onehot_fine, inverse=inverse, coupling=coupling
    )
    iterate = relax_weight * apply_inverse(inverse, source, onehot_fine)
    for cycle_index in range(CYCLES):
        if cycle_index == 0:
            actions = ["sweep"] * (SWEEPS - 1) + ["residual"]
        else:
            actions = ["sweep"] * SWEEPS + ["residual"]
        iterate, residual = stepper(iterate, actions)
        gathered_source = lax.all_gather(restrict(residual, prolong), "gz", axis=3, tiled=True)
        gathered_mid = lax.all_gather(onehot_mid, "gz", axis=3, tiled=True)
        gathered_coarse = lax.all_gather(onehot_coarse, "gz", axis=3, tiled=True)
        local_solver = partial(
            coarse_solve,
            onehot=gathered_coarse,
            border=section_border,
            inverse=inverse,
            coupling=coupling,
        )
        section_field = middle_cycle(
            gathered_source, gathered_mid, section_border, inverse, coupling, prolong, local_solver
        )
        iterate = iterate + expand(
            lax.dynamic_slice_in_dim(section_field, lax.axis_index("gz") * (CZ // 2), CZ // 2, 3),
            prolong,
        )
        iterate, unused_residual = stepper(iterate, ["sweep"] * SWEEPS)
    return iterate.reshape(MODES, CX * CY * CZ)[None, None, None]


HALO = 3 * SWEEPS + SWEEPS - 1
PITCH = CY + 2 * HALO
BLOCK = CX * CY * CZ
TILE = 128
LANES = -(-(PITCH * PITCH) // TILE) * TILE
ROWS = MODES + 8
MX, MY, MZ = CX // 2, CY // 2, CZ // 2
f32 = jnp.float32
bf16 = jnp.bfloat16


def split(value):
    high = value.astype(bf16)
    return high, (value - high.astype(f32)).astype(bf16)


def dot(a, b):
    return jnp.dot(a, b, preferred_element_type=f32)


def iota(shape, dim):
    return lax.broadcasted_iota(jnp.int32, shape, dim)


def where_equal(rows, columns):
    return jnp.where(rows == columns, 1.0, 0.0).astype(bf16)


def place(value, selector):
    high, low = split(value)
    return dot(high, selector) + dot(low, selector)


def pick(product, code, first):
    out = jnp.zeros((MODES, product.shape[1]), f32)
    for m in range(MATERIALS):
        out = jnp.where(code == m + first, product[m * MODES:(m + 1) * MODES], out)
    return out


def stack3(value):
    high, low = split(value)
    return jnp.concatenate([high, low, high], axis=0)


def thirds(value):
    high, low = split(value)
    return jnp.concatenate([high, high, low], axis=1)


def inverse_kernel(pivots, scale, diag, *refs):
    a = diag[...]
    row_id = iota((1, MODES, 1), 1)
    lane_id = iota((1, 1, MODES), 2)
    for k in pivots:
        pivot = 1.0 / a[:, k:k + 1, k:k + 1]
        on_row, on_lane = row_id == k, lane_id == k
        row = jnp.where(on_lane, pivot, a[:, k:k + 1, :] * pivot)
        column = a[:, :, k:k + 1]
        a = jnp.where(on_row, row, jnp.where(on_lane, 0.0, a) - column * row)
    refs[-1][...] = scale * a


def weights_kernel(scaled, diag, face, prolong, wg, wa, wd, wi, wr, wp):
    beside, gains = [], []
    for m in range(MATERIALS):
        faces = jnp.concatenate([face[d, m] for d in (1, 0, 2, 3, 4, 5)], axis=1)
        beside.append(faces)
        gains.append(jnp.dot(scaled[m], faces, precision=highest, preferred_element_type=f32))
    for target, blocks in ((wa, beside), (wg, gains)):
        high, low = split(jnp.concatenate(blocks, axis=0))
        target[...] = jnp.concatenate([high, low, high], axis=1)
    wd[...] = thirds(jnp.concatenate([diag[m] for m in range(MATERIALS)], axis=0))
    wi[...] = thirds(jnp.concatenate([scaled[m] for m in range(MATERIALS)], axis=0))
    for p in range(2):
        wr[p] = thirds(jnp.concatenate([restrict_scale * prolong[p * 4 + c].T for c in range(4)], axis=0))
    wp[...] = thirds(jnp.concatenate([prolong[c] for c in range(8)], axis=0))


def invert_part(pivots, scale, blocks, *after):
    kernel = partial(inverse_kernel, pivots, scale)
    return call(kernel, 3, shape_of(*blocks.shape), [], blocks, *after, unread=len(after))


def make_weights(scaled, diag_blocks, face_blocks, prolong):
    rows = MATERIALS * MODES
    shapes = [(rows, 18 * MODES)] * 2 + [(rows, 3 * MODES)] * 2
    shapes += [(2, 4 * MODES, 3 * MODES), (8 * MODES, 3 * MODES)]
    shapes = [jax.ShapeDtypeStruct(shape, bf16) for shape in shapes]
    return call(weights_kernel, 1, shapes, [], scaled, diag_blocks, face_blocks, prolong)


SHALLOW = SWEEPS
FIRST_PIVOTS = MODES // 2
PAIRS = CX
THICK = CX + HALO - 1
SLOT = CY * CZ


def layer_rows(depth, halo):
    return CY + 2 * (halo - depth)


SHALLOW_LANES = sum(layer_rows(d, SHALLOW) for d in range(1, SHALLOW + 1))
DEEP_LANES = sum(layer_rows(d, HALO) for d in range(1, HALO + 1))
PER_TILE = TILE // (2 * SHALLOW_LANES)
SHALLOW_TILES = -(-(THICK // 2) // PER_TILE)


def layer_of(index, first, last, halo):
    depth, start, at = jnp.full_like(index, first), jnp.zeros_like(index), 0
    for d in range(first + 1, last + 1):
        at += layer_rows(d - 1, halo)
        inside = index >= at
        depth, start = jnp.where(inside, d, depth), jnp.where(inside, at, start)
    return depth, index - start - (halo - depth)


def lane_of(depth, y, first, last, halo):
    start, at = jnp.zeros_like(depth), 0
    for d in range(first + 1, last + 1):
        at += layer_rows(d - 1, halo)
        start = jnp.where(depth == d, at, start)
    inside = (depth >= first) & (depth <= last) & (y >= depth - halo) & (y < CY + halo - depth)
    return jnp.where(inside, start + y + halo - depth, -(1 << 20))


def prepare_kernel(place_ref, values, other, materials, other_materials, half_way, out):
    mine = place_ref[0]
    for half, (block, kinds) in enumerate(((values, materials), (other, other_materials))):
        first = (mine ^ half) * (BLOCK // TILE)
        codes = jnp.broadcast_to((kinds[...] + 1).astype(f32), (ROWS - MODES, BLOCK))
        for tile in range(BLOCK // TILE):
            lanes = slice(tile * TILE, (tile + 1) * TILE)
            out[first + tile, :MODES] = block[:, lanes]
            out[first + tile, MODES:] = codes[:, lanes]


def swap_tile(y, odd):
    place = (y + CY) // CY
    return jnp.where(place == 1, 1, jnp.where(place // 2 == odd, 2, 0))


def pairs_skipped(place_ref):
    return place_ref[0] * ((2 * CX - THICK) // 2)


def pack_kernel(place_ref, own, first, second, scaled, thin_first, thin_second, thick_first, thick_second):
    column = iota((1, 4 * TILE), 1)
    lane, kind = column % TILE, column // TILE
    row = iota((3 * TILE, 4 * TILE), 0)
    odd_y, odd_z = place_ref[1] & 1, place_ref[2] & 1
    skipped = pairs_skipped(place_ref)
    parts = [
        jnp.concatenate([r[skipped + pair] for r in (first, own, second)], axis=1) for pair in range(THICK // 2)
    ]
    parts = split(jnp.concatenate(parts, axis=0))
    shallow = 0.0
    for odd in range(2):
        thin = lane - odd * SHALLOW_LANES
        thin_depth, thin_y = layer_of(thin, 1, SHALLOW, SHALLOW)
        thick_depth, thick_y = layer_of(lane, 1, HALO, HALO)
        depth = jnp.where(kind < 2, thin_depth, thick_depth)
        y = jnp.where(kind < 2, thin_y, thick_y)
        valid = jnp.where(
            kind < 2,
            jnp.where((thin >= 0) & (thin < SHALLOW_LANES), 1, 0),
            jnp.where(lane < DEEP_LANES, 1, 0),
        )
        z = jnp.where(kind % 2 == odd_z, CZ - depth, depth - 1)
        source = swap_tile(y, odd_y) * TILE + ((y + CY) % CY) * CZ + z + odd * SLOT
        selector = where_equal(row, jnp.where(valid == 1, source, -1))
        packed = dot(parts[0], selector) + dot(parts[1], selector)
        shallow = shallow + packed[:, :2 * TILE]
        for pair in range(THICK // 2):
            rows = packed[pair * ROWS:(pair + 1) * ROWS]
            thick_first[2 * pair + odd], thick_second[2 * pair + odd] = rows[:, 2 * TILE:3 * TILE], rows[:, 3 * TILE:]
    for tile in range(SHALLOW_TILES):
        for kind, out in enumerate((thin_first, thin_second)):
            strip = 0.0
            for slot in range(PER_TILE):
                pair = tile * PER_TILE + slot
                if pair < THICK // 2:
                    piece = shallow[pair * ROWS:(pair + 1) * ROWS, kind * TILE:(kind + 1) * TILE]
                    strip = strip + (pltpu.roll(piece, slot * 2 * SHALLOW_LANES, 1) if slot else piece)
            out[tile] = strip


def shallow_strip(first, second, pair):
    tile, slot = pair // PER_TILE, pair % PER_TILE
    shift = (TILE - slot * 2 * SHALLOW_LANES) % TILE
    lane = iota((1, TILE), 1)
    return jnp.where(
        lane < TILE // 2,
        pltpu.roll(first[tile], shift, 1),
        pltpu.roll(second[tile], (shift + TILE // 2) % TILE, 1),
    )


def in_grid(place_ref, sizes, y, z):
    whole_y, whole_z = y + place_ref[1] * CY, z + place_ref[2] * CZ
    return (whole_y >= 0) & (whole_y < sizes[1] * CY) & (whole_z >= 0) & (whole_z < sizes[2] * CZ)


def unpack(layout, sizes, place_ref, own, along_y, along_z, start, pairs, put, shallow):
    lane = iota((1, layout.lanes), 1)
    y, z = layout.place(lane)
    odd_y, odd_z = place_ref[1] & 1, place_ref[2] & 1
    inner = swap_tile(y, odd_y) * TILE + ((y + CY) % CY) * CZ + z
    depth = jnp.where(z < 0, -z, z - (CZ - 1))
    middle = (z >= 0) & (z < CZ)
    strip = jnp.where(jnp.where(z < 0, 0, 1) == odd_z, 1, 0)
    skipped = pairs_skipped(place_ref)
    if shallow:
        outer = lane_of(depth, y, 1, SHALLOW, SHALLOW) + 3 * TILE + strip * (TILE // 2)
        step = SHALLOW_LANES
    else:
        outer = lane_of(depth, y, 1, HALO, HALO) + (3 + strip) * TILE
        step = 0
    row = iota(((4 if shallow else 5) * TILE, layout.lanes), 0)
    valid = (lane < layout.used) & in_grid(place_ref, sizes, y, z)
    parts = []
    for odd in range(2):
        if odd == 0 or not shallow:
            parts = []
            for i in range(pairs):
                pair = start + i
                line = [r[pair] for r in (along_y[0], own, along_y[1])]
                if shallow:
                    line += [shallow_strip(*along_z, pair - skipped)]
                else:
                    line += [r[jnp.clip(2 * (pair - skipped) + odd, 0, THICK - 1)] for r in along_z]
                parts.append(jnp.concatenate(line, axis=1))
            parts = split(jnp.concatenate(parts, axis=0))
        source = jnp.where(middle, inner + odd * SLOT, outer + odd * step)
        selector = where_equal(row, jnp.where(valid, source, -1))
        placed = dot(parts[0], selector) + dot(parts[1], selector)
        for i in range(pairs):
            rows = placed[i * ROWS:(i + 1) * ROWS]
            put(2 * (start + i) + odd, rows[:MODES], rows[MODES:MODES + 1])


class Field:
    def __init__(self, full, high, low, shifts, masks=(None,) * 4):
        self.full, self.high, self.low = full, high, low
        self.shifts, self.masks = shifts, masks

    def put(self, x, value):
        self.full[x + 1] = value
        self.high[x + 1], self.low[x + 1] = split(value)

    def put_parts(self, x, high, low):
        self.full[x + 1] = high + low
        self.high[x + 1], self.low[x + 1] = high.astype(bf16), low.astype(bf16)

    def clear_ends(self):
        planes = self.full.shape[0]
        for x in (0, planes - 1):
            self.full[x] = jnp.zeros(self.full.shape[1:], f32)
            self.high[x] = jnp.zeros(self.full.shape[1:], bf16)
            self.low[x] = jnp.zeros(self.full.shape[1:], bf16)

    def get(self, x):
        return self.full[x + 1]


def field_scratch(planes, lanes):
    shape = (planes + 2, MODES, lanes)
    return [pltpu.VMEM(shape, f32), pltpu.VMEM(shape, bf16), pltpu.VMEM(shape, bf16)]


class Layout:
    def __init__(self, halo, lanes):
        self.halo, self.lanes, self.pitch = halo, lanes, CY + 2 * halo
        self.used = self.pitch * self.pitch
        self.factor = -(-(1 << 16) // self.pitch)

    def place(self, lane):
        y = (lane * self.factor) >> 16
        return y - self.halo, lane - y * self.pitch - self.halo

    def parity(self):
        y, z = self.place(iota((1, self.lanes), 1))
        return (y & 1) * 2 + (z & 1)

    def shifts(self):
        return (self.lanes - self.pitch, self.pitch, self.lanes - 1, 1)

    def field(self, refs):
        return Field(*refs, self.shifts())

    def own_lanes(self, lane):
        y, z = self.place(lane)
        return y, z, (lane < self.used) & (y >= 0) & (y < CY) & (z >= 0) & (z < CZ)


def lanes_for(halo):
    return -(-((CY + 2 * halo) ** 2) // TILE) * TILE


NEAR = 2 * SWEEPS
wide_layout = Layout(HALO, lanes_for(HALO))
near_layout = Layout(NEAR, lanes_for(NEAR))


def near_selector():
    y, z = near_layout.place(iota((1, near_layout.lanes), 1))
    source = (y + HALO) * PITCH + z + HALO
    source = jnp.where(iota((1, near_layout.lanes), 1) < near_layout.used, source, -1)
    return where_equal(iota((LANES, near_layout.lanes), 0), source)


def coupled_rows(centre, field, x):
    moved = []
    for shift, mask in zip(field.shifts, field.masks):
        part = pltpu.roll(centre, shift, 1)
        moved.append(part if mask is None else jnp.where(mask, part, 0.0))
    high, low = split(jnp.concatenate(moved, axis=0))
    high = [field.high[x], field.high[x + 2], high]
    low = [field.low[x], field.low[x + 2], low]
    return jnp.concatenate(high + high + low, axis=0)


def grouped(start, count, size, body):
    groups = -(-count // size)
    length = -(-count // groups)
    if groups == 1:
        body(start, count)
        return

    def step(i, carry):
        body(start + jnp.minimum(i * length, count - length), length)
        return carry

    lax.fori_loop(0, groups, step, 0)


def group_size(lanes):
    return 7 if lanes > 2 * TILE else 6


def sweep(source, target, start, count, wg, gain, code, store=None, size=None):
    def body(first, length):
        values = []
        for x in [first + j for j in range(length)]:
            centre = source.get(x)
            product = dot(wg[...], coupled_rows(centre, source, x))
            values.append((1.0 - relax_weight) * centre + gain[x] - pick(product, code[x], 1))
        for j, value in enumerate(values):
            (store or target.put)(first + j, value)

    grouped(start, count, size or group_size(source.full.shape[2]), body)


def residual(field, x, source, wa, wd, code):
    centre = field.get(x)
    applied = dot(wa[...], coupled_rows(centre, field, x)) + dot(wd[...], stack3(centre))
    return source - pick(applied, code, 1)


def restrict_plane(wr, residuals, parity):
    out = 0.0
    for p in range(2):
        out = out + pick(dot(wr[p], stack3(residuals[p])), parity, 0)
    return out


def expand_planes(wp, raised_high, raised_low, parity):
    product = dot(wp[...], jnp.concatenate([raised_high, raised_low, raised_high], axis=0))
    return [pick(product[p * 4 * MODES:(p + 1) * 4 * MODES], parity, 0) for p in range(2)]


def gather_mid(place_ref, here, sibling, sizes, put):
    n_gx, n_gy, n_gz = sizes
    per = MX * MY * MZ
    lines = MY * n_gz * MZ
    column = iota((1, n_gz * 2 * per), 1)
    k, rest = column % MZ, column // MZ
    gz, rest = rest % n_gz, rest // n_gz
    j, rest = rest % MY, rest // MY
    i, h = rest % MX, rest // MX
    source = gz * 2 * per + h * per + (i * MY + j) * MZ + k
    selector = where_equal(iota((n_gz * 2 * per, n_gz * 2 * per), 0), source)
    rows = here.shape[2]
    my_x, my_y, my_z = place_ref[0], place_ref[1], place_ref[2]
    parts = []
    for gx in range(n_gx):
        for gy in range(n_gy):
            slot = ((gx ^ my_x) & 1) + 2 * (((gy ^ my_y) >> 1) & 1)
            line = []
            for gz in range(n_gz):
                turn = my_z ^ gz
                line.append(jnp.where(((gy ^ my_y) & 1) == 0, here[slot, turn], sibling[slot, turn]))
            parts.append(jnp.concatenate(line, axis=1))
    placed = place(jnp.concatenate(parts, axis=0), selector)
    lower = iota((1, TILE), 1) < lines
    for gx in range(n_gx):
        for i in range(MX):
            quarters = []
            for h in range(2):
                tiles = []
                for pair in range(n_gy // 2):
                    block = [placed[(gx * n_gy + 2 * pair + s) * rows:][:rows] for s in range(2)]
                    at = ((h * MX + i) * lines) // TILE * TILE
                    block = [b[:, at:at + TILE] for b in block]
                    if i % 2 == 0:
                        block[1] = pltpu.roll(block[1], lines, 1)
                    else:
                        block[0] = pltpu.roll(block[0], lines, 1)
                    tiles.append(jnp.where(lower, block[0], block[1]))
                quarters.append(jnp.concatenate(tiles, axis=1))
            put(gx * MX + i, quarters)


class Coarse:
    def __init__(self, grid):
        self.x, self.y, self.z = (size // 2 for size in grid)
        self.plane = self.y * self.z
        self.lanes = self.x * self.plane

    def place(self, lane):
        return lane // self.plane, lane // self.z % self.y, lane % self.z

    def solve(self, value, wg, wi, code):
        x, y, z = self.place(iota((1, self.lanes), 1))
        gain = pick(dot(wi[...], stack3(value)), code, 1)
        moves = (
            (self.plane, x > 0), (self.lanes - self.plane, x < self.x - 1),
            (self.lanes - self.z, y < self.y - 1), (self.z, y > 0),
            (self.lanes - 1, z < self.z - 1), (1, z > 0),
        )

        def step(repeat, iterate):
            moved = [jnp.where(mask, pltpu.roll(iterate, shift, 1), 0.0) for shift, mask in moves]
            high, low = split(jnp.concatenate(moved, axis=0))
            product = dot(wg[...], jnp.concatenate([high, high, low], axis=0))
            return (1.0 - relax_weight) * iterate + gain - pick(product, code, 1)

        return lax.fori_loop(0, COARSE_SWEEPS - 1, step, gain)


def solve_mid(source, gain, code, coarse_source, coarse_code, fields, weights, grid):
    wg, wa, wd, wi, wr, wp = weights
    planes, size_y, size_z = grid
    lanes = size_y * size_z
    coarse = Coarse(grid)
    for i in range(2):
        fields(i).clear_ends()

    def begin(first, length):
        values = [pick(dot(wi[...], stack3(source[first + j])), code[first + j], 1) for j in range(length)]
        for j, value in enumerate(values):
            gain[first + j] = value
            fields(0).put(first + j, value)

    grouped(0, planes, 4, begin)
    lane = iota((1, lanes), 1)
    y, z = lane // size_z, lane % size_z
    parity = (y % 2) * 2 + z % 2
    tall, wide = iota((lanes, TILE), 0), iota((lanes, TILE), 1)
    squeeze = (tall // size_z // 2) * coarse.z + tall % size_z // 2
    per_tile = TILE // coarse.plane
    target = (y // 2) * coarse.z + z // 2
    row = iota((coarse.lanes, lanes), 0)

    def correct(field):
        def down(tile, carry):
            total = 0.0
            for part in range(per_tile):
                x = 2 * (tile * per_tile + part)
                rests = [residual(field, x + p, source[x + p], wa, wd, code[x + p]) for p in range(2)]
                selector = where_equal(squeeze + part * coarse.plane, wide)
                total = total + place(restrict_plane(wr, rests, parity), selector)
            coarse_source[:, pl.ds(pl.multiple_of(tile * TILE, TILE), TILE)] = total
            return carry

        lax.fori_loop(0, coarse.lanes // TILE, down, 0)
        result = coarse.solve(coarse_source[...], wg, wi, coarse_code[...])
        parts = jnp.concatenate(split(result), axis=0)

        def up(step, carry):
            for pair in (2 * step, 2 * step + 1):
                raised = dot(parts, where_equal(row, target + pair * coarse.plane)).astype(bf16)
                for p, value in enumerate(expand_planes(wp, raised[:MODES], raised[MODES:], parity)):
                    field.put(2 * pair + p, field.get(2 * pair + p) + value)
            return carry

        lax.fori_loop(0, coarse.x // 2, up, 0)

    def step(i, carry):
        sweep(fields(i % 2), fields(1 - i % 2), 0, planes, wg, gain, code, size=planes)

        @pl.when(i == SWEEPS - 2)
        def _():
            correct(fields(1 - i % 2))

        return carry

    lax.fori_loop(0, 2 * SWEEPS - 1, step, 0)
    return fields((2 * SWEEPS - 1) % 2)


def add_mid(place_ref, layout, result, field, depth, wp, grid, old):
    planes, size_y, size_z = grid
    gx, gy, gz = place_ref[0], place_ref[1], place_ref[2]
    lane = iota((1, layout.lanes), 1)
    y, z = layout.place(lane)
    whole_y, whole_z = y + gy * CY, z + gz * CZ
    inside = (lane < layout.used) & (whole_y >= 0) & (whole_y < 2 * size_y) & (whole_z >= 0) & (whole_z < 2 * size_z)
    target = jnp.where(inside, (whole_y >> 1) * size_z + (whole_z >> 1), -1)
    raise_lanes = where_equal(iota((size_y * size_z, layout.lanes), 0), target)
    parity = layout.parity()

    def body(first, length):
        values = []
        for x in [first + j for j in range(length)]:
            parts = jnp.concatenate([result.high[x + 1], result.low[x + 1]], axis=0)
            raised = dot(parts, raise_lanes).astype(bf16)
            for p, value in enumerate(expand_planes(wp, raised[:MODES], raised[MODES:], parity)):
                values.append(old[2 * x + p] + value)
        for j, value in enumerate(values):
            field.put(2 * first + j, value)

    pairs = (CX + depth) // 2
    grouped(gx * ((CX - depth) // 2), pairs, -(-pairs // 2), body)


def fine_residual(field, own, source, wr, wa, wd, code):
    layout = near_layout
    tall, wide = iota((layout.lanes, TILE), 0), iota((layout.lanes, TILE), 1)
    y, z, inside = layout.own_lanes(tall)
    target = jnp.where(inside, (y >> 1) * MZ + (z >> 1), -BLOCK)
    per = MX * MY * MZ
    index = wide % per
    parity = layout.parity()
    def add(step, total):
        for i in (2 * step, 2 * step + 1):
            x = own + 2 * i
            rests = [residual(field, x + p, source[2 * i + p], wa, wd, code[x + p]) for p in range(2)]
            total = total + place(restrict_plane(wr, rests, parity), where_equal(target + i * MY * MZ, index))
        return total

    total = lax.fori_loop(0, MX // 2, add, jnp.zeros((MODES, TILE), f32))
    half = MODES // 2
    return jnp.where(iota((1, TILE), 1) < per, total[:half], total[half:])


def near_kernel(sizes, place_ref, own, y0, y1, z0, z1, wg, wa, wd, wi, wr, wp, source, payload, *scratch):
    layout = near_layout
    first, second = layout.field(scratch[0:3]), layout.field(scratch[3:6])
    whole, gain, code = scratch[6:9]
    first.clear_ends()
    second.clear_ends()
    gx = place_ref[0]

    def put(x, value, material):
        whole[x], code[x] = value, material

    start, pairs = gx * ((CX - SHALLOW) // 2), (CX + SHALLOW) // 2
    unpack(layout, sizes, place_ref, own, (y0, y1), (z0, z1), start, pairs, put, True)

    def begin(start, length):
        values = [pick(dot(wi[...], stack3(whole[start + j])), code[start + j], 1) for j in range(length)]
        for j, value in enumerate(values):
            gain[start + j] = value
            first.put(start + j, value)

    grouped(gx * (CX - SHALLOW), CX + SHALLOW, group_size(layout.lanes), begin)
    depth = SHALLOW - 1
    sweep(first, second, gx * (CX - depth), CX + depth, wg, gain, code)
    mine = gx * CX
    source[...] = whole[pl.ds(mine, CX)]
    payload[...] = fine_residual(second, mine, source, wr, wa, wd, code)


def gain_kernel(sizes, place_ref, own, y0, y1, z0, z1, wi, payload, gain, code, passed, whole):
    def put(x, value, material):
        whole[x], code[x] = value, material

    unpack(wide_layout, sizes, place_ref, own, (y0, y1), (z0, z1), 0, PAIRS, put, False)

    def begin(start, length):
        values = [pick(dot(wi[...], stack3(whole[start + j])), code[start + j], 1) for j in range(length)]
        for j, value in enumerate(values):
            gain[start + j] = value

    grouped(0, 2 * CX, 4, begin)
    passed[...] = payload[...]


def narrow_kernel(place_ref, gain, code, solved, near_gain, near_code):
    to_near = near_selector()

    def body(start, length):
        for j in range(length):
            near_gain[start + j] = place(gain[start + j], to_near)
            near_code[start + j] = dot(jnp.broadcast_to(code[start + j], (8, LANES)).astype(bf16), to_near)[:1]

    grouped(place_ref[0] * (CX - NEAR), CX + NEAR, 4, body)


def deep_kernel(place_ref, gain, code, wg, column, solved, passed, *scratch):
    passed[...] = column[...]
    first = wide_layout.field(scratch)
    first.clear_ends()
    for x in range(2 * CX):
        first.put(x, gain[x])
    depth = HALO - 1
    gx = place_ref[0]

    def store(x, value):
        solved[x] = value

    sweep(first, None, gx * (CX - depth), CX + depth, wg, gain, code, store)


def mid_scratch(grid):
    planes, size_y, size_z = grid
    lanes = size_y * size_z
    both = [pltpu.VMEM((2,) + ref.shape, ref.dtype) for ref in field_scratch(planes, lanes)]
    return both + [pltpu.VMEM((planes, MODES, lanes), f32)] * 2 + [pltpu.VMEM((MODES, planes * lanes // 8), f32)]


def run_mid(place_ref, here, sibling, sizes, grid, weights, scratch, mid_code, coarse_code, read_codes):
    planes, size_y, size_z = grid
    lanes = size_y * size_z
    lane = iota((1, lanes), 1)
    y, z = lane // size_z, lane % size_z
    shifts = (lanes - size_z, size_z, lanes - 1, 1)
    masks = (y < size_y - 1, y > 0, z < size_z - 1, z > 0)
    source, gain, coarse_source = scratch[3:6]

    def fields(i):
        return Field(*(ref.at[i] for ref in scratch[0:3]), shifts, masks)

    half = MODES // 2
    coarse = Coarse(grid)
    corners = []

    def put(x, quarters):
        source[x, :half] = quarters[0][:half]
        source[x, half:] = quarters[1][:half]
        if read_codes:
            mid_code[x] = quarters[0][half:half + 1]
            if x % 2 == 0:
                corners.append(jnp.broadcast_to(quarters[1][half:half + 1], (8, lanes)).astype(bf16))

    gather_mid(place_ref, here, sibling, sizes, put)
    if read_codes:
        tall, wide = iota((lanes, coarse.lanes), 0), iota((lanes, coarse.lanes), 1)
        x, cy, cz = coarse.place(wide)
        total = 0.0
        for pair in range(coarse.x):
            selector = where_equal(jnp.where(x == pair, 2 * cy * size_z + 2 * cz, -1), tall)
            total = total + dot(corners[pair], selector)
        coarse_code[...] = total[:1]
    return solve_mid(source, gain, mid_code, coarse_source, coarse_code, fields, weights, grid)


def second_kernel(sizes, grid, place_ref, here, sibling, gain, code, solved, near_gain, near_code, source,
                  wg, wa, wd, wi, wr, wp, payload, result, mid_code, coarse_code, *scratch):
    weights = (wg, wa, wd, wi, wr, wp)
    answer = run_mid(place_ref, here, sibling, sizes, grid, weights, scratch[12:], mid_code, coarse_code, True)
    first, second = wide_layout.field(scratch[0:3]), wide_layout.field(scratch[3:6])
    now, other = near_layout.field(scratch[6:9]), near_layout.field(scratch[9:12])
    for field in (first, second, now, other):
        field.clear_ends()
    depth = 3 * SWEEPS
    gx = place_ref[0]
    add_mid(place_ref, wide_layout, answer, first, depth, wp, grid, solved)
    to_near = near_selector()

    def narrow(x, value):
        parts = dot(jnp.concatenate(split(value), axis=0), to_near)
        now.put_parts(x, parts[:MODES], parts[MODES:])

    for repeat in range(2 * SWEEPS):
        depth -= 1
        start, count = gx * (CX - depth), CX + depth
        if depth > NEAR:
            sweep(first, second, start, count, wg, gain, code)
            first, second = second, first
        elif depth == NEAR:
            sweep(first, None, start, count, wg, gain, code, narrow)
        else:
            def store(x, value, target=other):
                target.put(x, value)
                if depth == SWEEPS:
                    result[x] = value

            sweep(now, other, start, count, wg, near_gain, near_code, store)
            now, other = other, now
    payload[...] = fine_residual(now, gx * CX, source, wr, wa, wd, near_code)


def third_kernel(sizes, grid, place_ref, here, sibling, mid_code, coarse_code, near_gain, near_code, solved,
                 wg, wa, wd, wi, wr, wp, result, *scratch):
    weights = (wg, wa, wd, wi, wr, wp)
    answer = run_mid(place_ref, here, sibling, sizes, grid, weights, scratch[6:], mid_code, coarse_code, False)
    layout = near_layout
    now, other = layout.field(scratch[0:3]), layout.field(scratch[3:6])
    now.clear_ends()
    other.clear_ends()
    depth = SWEEPS
    gx = place_ref[0]
    add_mid(place_ref, layout, answer, now, depth, wp, grid, solved)
    for repeat in range(SWEEPS):
        depth -= 1
        sweep(now, other, gx * (CX - depth), CX + depth, wg, near_gain, near_code)
        now, other = other, now
    tall, wide = iota((layout.lanes, TILE), 0), iota((layout.lanes, TILE), 1)
    y, z, inside = layout.own_lanes(tall)
    target = jnp.where(inside, y * CZ + z, -BLOCK)
    selectors = [where_equal(target + odd * CY * CZ, wide) for odd in range(2)]
    for pair in range(CX // 2):
        total = 0.0
        for odd in range(2):
            value = now.get(gx * CX + 2 * pair + odd)
            high, low = split(value)
            lowest = (value - high.astype(f32) - low.astype(f32)).astype(bf16)
            for part in (high, low, lowest):
                total = total + dot(part, selectors[odd])
        result[:, pair * TILE:(pair + 1) * TILE] = total


def call(kernel, cost_us, out_shape, scratch, *args, limit=16, unread=0):
    vmem, smem = pl.BlockSpec(memory_space=pltpu.VMEM), pl.BlockSpec(memory_space=pltpu.SMEM)
    specs = [smem if a.dtype == jnp.int32 and a.ndim == 1 else vmem for a in args[:len(args) - unread]]
    specs += [pl.BlockSpec(memory_space=pl.ANY)] * unread
    cost = pl.CostEstimate(flops=int(cost_us * 1e9), bytes_accessed=int(cost_us * 3e6), transcendentals=0)
    return pl.pallas_call(
        kernel,
        out_shape=out_shape,
        in_specs=specs,
        out_specs=jax.tree.map(lambda s: vmem, out_shape),
        scratch_shapes=scratch,
        cost_estimate=cost,
        compiler_params=pltpu.CompilerParams(vmem_limit_bytes=limit * 1024 * 1024),
    )(*args)


def shape_of(*dims):
    return jax.ShapeDtypeStruct(dims, f32)


def wide_device(sizes, right_side, diag_blocks, face_blocks, prolong, mats_fine, mats_mid, mats_coarse):
    n_gx, n_gy, n_gz = sizes
    axes = ("gx", "gy", "gz")
    grid = (n_gx * MX, n_gy * MY, n_gz * MZ)
    place_ref = jnp.stack([lax.axis_index(a) for a in axes]).astype(jnp.int32)
    tiles = BLOCK // TILE
    values, kinds = right_side.reshape(MODES, BLOCK), mats_fine.reshape(1, BLOCK)
    swap = [(0, 1), (1, 0)]
    others = lax.ppermute(values, "gx", swap), lax.ppermute(kinds, "gx", swap)
    half_way = invert_part(range(FIRST_PIVOTS), 1.0, diag_blocks)
    own = call(
        prepare_kernel, 0.5, shape_of(2 * tiles, ROWS, TILE), [],
        place_ref, values, others[0], kinds, others[1], half_way, unread=1,
    )
    swaps = {}
    for axis, n in zip(axes, sizes):
        inner = [pair for i in range(1, n - 1, 2) for pair in ((i, i + 1), (i + 1, i))]
        swaps[axis] = [(i, i ^ 1) for i in range(n)], [(0, 0)] + inner + [(n - 1, n - 1)]
    along_y = [lax.ppermute(own, "gy", swap) for swap in swaps["gy"]]
    scaled = invert_part(range(FIRST_PIVOTS, MODES), relax_weight, half_way, own)
    weights = make_weights(scaled, diag_blocks, face_blocks, prolong)
    thin, thick = shape_of(SHALLOW_TILES, ROWS, TILE), shape_of(THICK, ROWS, TILE)
    send = call(pack_kernel, 1.5, [thin, thin, thick, thick], [], place_ref, own, *along_y, scaled, unread=1)
    shallow = [lax.ppermute(value, "gz", swap) for value, swap in zip(send[:2], swaps["gz"])]
    deep = [lax.ppermute(value, "gz", swap) for value, swap in zip(send[2:], swaps["gz"])]

    wide = field_scratch(2 * CX, LANES)
    near = field_scratch(2 * CX, near_layout.lanes)
    half, per = MODES // 2, MX * MY * MZ
    whole = shape_of(2 * CX, MODES, LANES)
    small = shape_of(2 * CX, MODES, near_layout.lanes)
    small_code = shape_of(2 * CX, 1, near_layout.lanes)
    source, payload = call(
        partial(near_kernel, sizes), 7,
        [shape_of(CX, MODES, near_layout.lanes), shape_of(half, TILE)],
        near * 2 + [pltpu.VMEM(s.shape, f32) for s in (small, small, small_code)],
        place_ref, own, *along_y, *shallow, *weights,
    )
    mid = (mats_mid.reshape(per) + 1).astype(f32)
    coarse = (mats_coarse.reshape(MX // 2, 1, MY // 2, 1, MZ // 2, 1) + 1).astype(f32)
    coarse = jnp.broadcast_to(coarse, (MX // 2, 2, MY // 2, 2, MZ // 2, 2)).reshape(per)
    tail = jnp.broadcast_to(jnp.concatenate([mid, coarse])[None], (8, TILE))

    def along_z(value):
        turns = [[(i, i ^ s) for i in range(n_gz)] for s in range(1, n_gz)]
        return [lax.ppermute(value, "gz", turn) for turn in turns]

    def across(column):
        flips = [
            [(i * n_gy + j, (i ^ dx) * n_gy + (j ^ dy)) for i in range(n_gx) for j in range(n_gy)]
            for dx, dy in ((1, 0), (0, 2), (1, 2))
        ]
        return [lax.ppermute(column, ("gx", "gy"), flip) for flip in flips]

    def with_sibling(here):
        return here, lax.ppermute(here, "gy", [(j, j ^ 1) for j in range(n_gy)])

    payload = jnp.concatenate([payload, tail], axis=0)
    turned = along_z(payload)
    gain, code, payload = call(
        partial(gain_kernel, sizes), 6,
        [whole, shape_of(2 * CX, 1, LANES), shape_of(*payload.shape)],
        [pltpu.VMEM(whole.shape, f32)],
        place_ref, own, *along_y, *deep, weights[3], payload,
    )
    column = jnp.stack([payload] + turned)
    flipped = across(column)
    solved, column = call(
        deep_kernel, 7, [whole, shape_of(*column.shape)], wide, place_ref, gain, code, weights[0], column
    )
    gathered = with_sibling(jnp.stack([column] + flipped))
    near_gain, near_code = call(narrow_kernel, 1, [small, small_code], [], place_ref, gain, code, solved, unread=1)
    planes, lanes = grid[0], grid[1] * grid[2]
    payload, solved, mid_code, coarse_code = call(
        partial(second_kernel, sizes, grid), 37,
        [shape_of(half, TILE), small, shape_of(planes, 1, lanes), shape_of(1, planes * lanes // 8)],
        wide * 2 + near * 2 + mid_scratch(grid),
        place_ref, *gathered, gain, code, solved,
        near_gain, near_code, source, *weights, limit=32,
    )
    column = jnp.stack([payload] + along_z(payload))
    gathered = with_sibling(jnp.stack([column] + across(column)))
    result = call(
        partial(third_kernel, sizes, grid), 18,
        shape_of(MODES, BLOCK),
        near * 2 + mid_scratch(grid),
        place_ref, *gathered, mid_code, coarse_code, near_gain, near_code, solved, *weights,
    )
    return result[None, None, None]


def solution(mesh):
    placed = (
        P("gx", "gy", "gz", None, None),
        P(),
        P(),
        P(),
        P("gx", "gy", "gz", None),
        P("gx", "gy", "gz", None),
        P("gx", "gy", "gz", None),
    )
    sizes = tuple(mesh.shape[a] for a in ("gx", "gy", "gz"))
    wide = sizes[0] == 2 and sizes[1] == 4 and sizes[2] * MY * MZ * 2 == TILE
    return jax.shard_map(
        partial(wide_device, sizes) if wide else per_device,
        mesh=mesh,
        in_specs=placed,
        out_specs=P("gx", "gy", "gz", None, None),
        check_vma=False,
    )
```
